512 devices in a mesh: dp: 32 (over x, y), tensor: 8 (over z), section: 2 (over core).
Axes of the slice: x: 4, y: 8, z: 8, core: 2. Of those that a mesh axis runs over, the one named last changes fastest.
Arguments:
- hidden_in: bfloat16 [192, 8192], P(None, 'dp'), may hold values from -12 to 12
- norm_gain: float32 [2, 8192], P('section', 'dp'), may hold values from 0.25 to 1.75
- w_query: bfloat16 [2, 8192, 8192], P('section', 'dp', 'tensor'), may hold values from -0.0625 to 0.0625
- w_key: bfloat16 [2, 8192, 1024], P('section', 'dp', 'tensor'), may hold values from -0.0625 to 0.0625
- w_value: bfloat16 [2, 8192, 1024], P('section', 'dp', 'tensor'), may hold values from -0.0625 to 0.0625
- w_out: bfloat16 [2, 8192, 8192], P('section', 'tensor', 'dp'), may hold values from -0.0625 to 0.0625
- key_cache: bfloat16 [2, 192, 64, 1024], P('section', 'dp', None, 'tensor'), may hold values from -320 to 320
- value_cache: bfloat16 [2, 192, 64, 1024], P('section', 'dp', None, 'tensor'), may hold values from -6 to 6
- context_len: int32 [192], replicated, may hold values from 1 to 63, as said below
- dest_replica: int32 [192], replicated, may hold values from 0 to 31, as said below
- dest_slot: int32 [192], replicated, may hold values from 0 to 5
Outputs:
- layer_out: bfloat16 [2, 192, 8192], P('section', None, 'dp')
- key_out: bfloat16 [2, 192, 64, 1024], P('section', 'dp', None, 'tensor')
- value_out: bfloat16 [2, 192, 64, 1024], P('section', 'dp', None, 'tensor')
The draws below stay inside these ranges and needn't reach their ends.
Inputs may be any that keep to these rules, and one draw needn't show every extreme that they name: `context_len`: the longest row has exactly 63 live positions. dest_replica[g] * 6 + dest_slot[g] is a permutation of 0..191; every replica hands exactly 4 of its rows to other replicas, never two to the same one, and receives 4.
All inputs are finite; a program needn't handle non-finite values.
Results may differ from the reference program's by a relative error of at most 0.015.
Values may be sent and summed in bfloat16 or wider, within the bound.
No kernel may reach another device: no remote copies, remote signals or barrier semaphores. Data moves between devices by JAX's collectives and lax.ppermute only.
A program may use at most 64 MiB of HBM per device.

```python
import jax
import jax.numpy as jnp
from jax import lax

D = 8192
HEADS = 64
KV_HEADS = 8
HEAD = 128
ROWS_DEV = 6
CACHE_POSITIONS = 64
DEPTH_TOTAL = 2
SEQUENCE_TOTAL = 192
MOVES = 4
N_DP = 32


def plan_tables(key):
    key_relabel, key_offsets, key_orders = jax.random.split(key, 3)
    relabel = jax.random.permutation(key_relabel, N_DP).astype(jnp.int32)
    offsets = (jax.random.permutation(key_offsets, N_DP - 1)[:MOVES] + 1).astype(jnp.int32)
    classes = jnp.concatenate([offsets, jnp.zeros((ROWS_DEV - MOVES,), jnp.int32)])
    orders = jax.vmap(lambda subkey: jax.random.permutation(subkey, ROWS_DEV))(jax.random.split(key_orders, N_DP)).astype(jnp.int32)
    placing = jnp.argsort(relabel).astype(jnp.int32)
    target_place = (placing[:, None] + classes[None, :]) % N_DP
    target = jnp.take(relabel, target_place)
    target_slot = orders[target, jnp.arange(ROWS_DEV, dtype=jnp.int32)[None, :]]
    row_index = (jnp.arange(N_DP, dtype=jnp.int32)[:, None] * ROWS_DEV + orders).reshape(-1)
    replica_table = jnp.zeros((SEQUENCE_TOTAL,), jnp.int32).at[row_index].set(target.reshape(-1).astype(jnp.int32))
    slot_table = jnp.zeros((SEQUENCE_TOTAL,), jnp.int32).at[row_index].set(target_slot.reshape(-1).astype(jnp.int32))
    return (replica_table, slot_table)


def draw_dest_replica(key, part):
    return plan_tables(key)[0]


def draw_dest_slot(key, part):
    return plan_tables(key)[1]


def draw_context_len(key, part):
    key = jax.random.fold_in(key, 7)
    key_heavy, key_base, key_peak = jax.random.split(key, 3)
    heavy = jax.random.randint(key_heavy, (N_DP,), 0, 4) == 0
    reach = jnp.where(heavy, CACHE_POSITIONS - 1, max(CACHE_POSITIONS // 4, 1)).astype(jnp.int32)
    base_ints = jax.random.randint(key_base, (N_DP, ROWS_DEV), 0, 1 << 20)
    lengths = (1 + base_ints % reach[:, None]).reshape(-1).astype(jnp.int32)
    peak_row = jax.random.randint(key_peak, (), 0, SEQUENCE_TOTAL)
    return lengths.at[peak_row].set(CACHE_POSITIONS - 1).astype(jnp.int32)


def draw_hidden_in(key, part):
    key = jax.random.fold_in(key, 11)
    master_seed, key_rough = jax.random.split(key, 2)
    column = jnp.arange(D, dtype=jnp.float32) / D
    rising = 0.5 * 3.0 ** column
    rough = jax.random.uniform(key_rough, (D,), jnp.float32, 0.6, 1.6)
    payload_vectors = jax.random.normal(master_seed, (SEQUENCE_TOTAL, D), jnp.float32) * rising[None, :] * rough[None, :]
    return jnp.clip(payload_vectors, -12.0, 12.0).astype(jnp.bfloat16)


def draw_key_cache(key, part):
    key = jax.random.fold_in(key, 13)
    master_seed = jax.random.fold_in(key, 0)
    full_dimensions = (DEPTH_TOTAL, SEQUENCE_TOTAL, CACHE_POSITIONS, KV_HEADS * HEAD)
    payload_vectors = jax.random.normal(master_seed, full_dimensions, jnp.float32)
    return jnp.clip(payload_vectors, -6.0, 6.0).astype(jnp.bfloat16)


def shard_levels(key, extent, cuts, smallest, high):
    gain = 1.0
    for position, blocks in cuts:
        steps = jax.random.uniform(jax.random.fold_in(jax.random.fold_in(key, 6), position), (blocks,), jnp.float32, smallest / len(cuts), high / len(cuts))
        gain = gain * jnp.repeat(jnp.exp(steps), extent[position] // blocks).reshape((-1,) + (1,) * (len(extent) - 1 - position))
    return gain


def gaussian(key, dims, scale, limit, cuts=(), kind=jnp.bfloat16):
    drawn = scale * jax.random.normal(key, dims, jnp.float32)
    if cuts:
        drawn = drawn * shard_levels(key, dims, cuts, -0.22, 0.18)
    return jnp.clip(drawn, -limit, limit).astype(kind)


def setup_inputs(seed: int = 0) -> dict:
    arg_keys = jax.random.split(jax.random.key(seed), 12)
    return {
        "hidden_in": draw_hidden_in(jax.random.fold_in(arg_keys[11], 71), 0),
        "norm_gain": jnp.clip(1.0 + 0.15 * jax.random.normal(arg_keys[1], (DEPTH_TOTAL, D), jnp.float32), 0.25, 1.75),
        "w_query": gaussian(arg_keys[2], (DEPTH_TOTAL, D, HEADS * HEAD), D ** -0.5, 0.0625, ((0, 2), (1, 32), (2, 8))),
        "w_key": gaussian(arg_keys[3], (DEPTH_TOTAL, D, KV_HEADS * HEAD), D ** -0.5, 0.0625, ((0, 2), (1, 32), (2, 8))),
        "w_value": gaussian(arg_keys[4], (DEPTH_TOTAL, D, KV_HEADS * HEAD), D ** -0.5, 0.0625, ((0, 2), (1, 32), (2, 8))),
        "w_out": gaussian(arg_keys[5], (DEPTH_TOTAL, HEADS * HEAD, D), (HEADS * HEAD) ** -0.5, 0.0625, ((0, 2), (1, 8), (2, 32))),
        "key_cache": draw_key_cache(jax.random.fold_in(arg_keys[11], 71), 0),
        "value_cache": gaussian(arg_keys[7], (DEPTH_TOTAL, SEQUENCE_TOTAL, CACHE_POSITIONS, KV_HEADS * HEAD), 1.0, 6.0, ((0, 2), (1, 32), (3, 8))),
        "context_len": draw_context_len(jax.random.fold_in(arg_keys[11], 71), 0),
        "dest_replica": draw_dest_replica(jax.random.fold_in(arg_keys[11], 71), 0),
        "dest_slot": draw_dest_slot(jax.random.fold_in(arg_keys[11], 71), 0),
    }


epsilon = 1e-06
rope_base = 1000000.0

def rotate(vectors, positions):
    half_width = vectors.shape[-1] // 2
    exponent = jnp.arange(half_width, dtype=jnp.float32) * (2.0 / vectors.shape[-1])
    inverse_freq = rope_base ** (-exponent)
    angles = positions.astype(jnp.float32)[:, None] * inverse_freq[None, :]
    cosine = jnp.cos(angles)[:, None, :]
    sine = jnp.sin(angles)[:, None, :]
    first_half = vectors[..., :half_width]
    second_half = vectors[..., half_width:]
    return jnp.concatenate([first_half * cosine - second_half * sine, second_half * cosine + first_half * sine], -1)

def attend(queries, cached_keys, cached_values, own_key, own_value, lengths):
    score_scale = queries.shape[-1] ** (-0.5)
    scores = jnp.einsum('nkgd,nckd->nkgc', queries.astype(jnp.float32), cached_keys.astype(jnp.float32)) * score_scale
    own_score = jnp.einsum('nkgd,nkd->nkg', queries.astype(jnp.float32), own_key.astype(jnp.float32)) * score_scale
    live_mask = (jnp.arange(cached_keys.shape[1], dtype=jnp.int32)[None, :] < lengths[:, None])[:, None, None, :]
    scores = jnp.where(live_mask, scores, -1e+30)
    highest = jnp.maximum(lax.optimization_barrier(jnp.max(scores, -1)), own_score)
    cache_terms = jnp.exp(scores - highest[..., None])
    own_term = jnp.exp(own_score - highest)
    denominator = lax.optimization_barrier(jnp.sum(cache_terms, -1)) + own_term
    cache_weights = (cache_terms / denominator[..., None]).astype(jnp.bfloat16)
    own_weight = (own_term / denominator).astype(jnp.bfloat16)
    attended = jnp.einsum('nkgc,nckd->nkgd', cache_weights.astype(jnp.float32), cached_values.astype(jnp.float32))
    attended = attended + own_weight.astype(jnp.float32)[..., None] * own_value.astype(jnp.float32)[:, :, None, :]
    return attended.astype(jnp.bfloat16)

def layer(hidden, gain_row, query_weight, key_weight, value_weight, out_weight, cached_keys, cached_values, lengths):
    row_count = hidden.shape[0]
    context = cached_keys.shape[1]
    widened = hidden.astype(jnp.float32)
    mean_square = lax.optimization_barrier(jnp.mean(widened * widened, axis=1, keepdims=True))
    normed = (widened * lax.rsqrt(mean_square + epsilon) * gain_row[None, :]).astype(jnp.bfloat16)
    query_part = jnp.dot(normed, query_weight, preferred_element_type=jnp.float32)
    key_part = jnp.dot(normed, key_weight, preferred_element_type=jnp.float32)
    value_part = jnp.dot(normed, value_weight, preferred_element_type=jnp.float32)
    queries = rotate(query_part.reshape(row_count, HEADS, HEAD), lengths).astype(jnp.bfloat16)
    queries = queries.reshape(row_count, KV_HEADS, HEADS // KV_HEADS, HEAD)
    own_key = rotate(key_part.reshape(row_count, KV_HEADS, HEAD), lengths).astype(jnp.bfloat16)
    own_value = value_part.reshape(row_count, KV_HEADS, HEAD).astype(jnp.bfloat16)
    attended = attend(queries, cached_keys.reshape(row_count, context, KV_HEADS, HEAD), cached_values.reshape(row_count, context, KV_HEADS, HEAD), own_key, own_value, lengths)
    projected = jnp.dot(attended.reshape(row_count, HEADS * HEAD), out_weight, preferred_element_type=jnp.float32)
    result = (widened + projected).astype(jnp.bfloat16)
    written = (jnp.arange(context, dtype=jnp.int32)[None, :] == lengths[:, None])[:, :, None]
    keys_out = jnp.where(written, own_key.reshape(row_count, 1, KV_HEADS * HEAD), cached_keys)
    values_out = jnp.where(written, own_value.reshape(row_count, 1, KV_HEADS * HEAD), cached_values)
    return (result, keys_out, values_out)

def reference(hidden_in, norm_gain, w_query, w_key, w_value, w_out, key_cache, value_cache, context_len, dest_replica, dest_slot):
    all_rows = dest_replica.shape[0]
    new_index = (dest_replica * ROWS_DEV + dest_slot).astype(jnp.int32)
    source_of = jnp.zeros((all_rows,), jnp.int32).at[new_index].set(jnp.arange(all_rows, dtype=jnp.int32))
    lengths = jnp.take(context_len, source_of)
    current = hidden_in
    outputs = []
    key_list = []
    value_list = []
    for layer_id in range(DEPTH_TOTAL):
        moved_keys = jnp.take(key_cache[layer_id], source_of, axis=0)
        moved_values = jnp.take(value_cache[layer_id], source_of, axis=0)
        current, new_keys, new_values = layer(current, norm_gain[layer_id], w_query[layer_id], w_key[layer_id], w_value[layer_id], w_out[layer_id], moved_keys, moved_values, lengths)
        outputs.append(current)
        key_list.append(new_keys)
        value_list.append(new_values)
    return (jnp.stack(outputs), jnp.stack(key_list), jnp.stack(value_list))
```

```python
import jax
import jax.numpy as jnp
from jax import lax
from jax.experimental import pallas as pl
from jax.experimental.pallas import tpu as pltpu
from jax.sharding import PartitionSpec as P

N_DP = 32
ROWS_DEV = 6
ROWS = 192
SLOTS = 8
PADDED = N_DP * SLOTS
CONTEXT = 64
HEAD = 128
GROUP = 8
PARTS = GROUP + 2
BLOCK = 64
WIDTH = 256
MODEL = 8192
N_TS = 16
TS_ROWS = PADDED // N_TS
EPSILON = 1e-06
ROPE_BASE = 1000000.0
F32 = jnp.float32
BF16 = jnp.bfloat16

SECTION, REPLICA, TS_BLOCK, DEST, HELD_LEN, SOURCE, NEW_LEN = 0, 1, 2, 4, 10, 16, 22

SMEM_SPEC = pl.BlockSpec(memory_space=pltpu.SMEM)
VMEM_SPEC = pl.BlockSpec(memory_space=pltpu.VMEM)


def iota(shape, dim):
    return lax.broadcasted_iota(jnp.int32, shape, dim)


def pick(condition):
    return jnp.where(condition, 1.0, 0.0).astype(BF16)


def over_six(index):
    return (index * 171) >> 10


def dot(left, right, contract=((1,), (0,))):
    return lax.dot_general(left, right, (contract, ((), ())), preferred_element_type=F32)


def old_order(new_index, hidden):
    to_new = pick(iota((ROWS, ROWS), 0) == new_index)
    return dot(to_new, hidden, ((0,), (0,))).astype(BF16)


def project_kernel(layer, scalars, *refs):
    if layer == 0:
        replica, slot, hidden, gain, w_query, w_key, w_value, keys, payload, spread = refs
    else:
        hidden, gain, w_query, w_key, w_value, keys, payload, spread = refs

    @pl.when(scalars[SECTION] == layer)
    def _():
        if layer == 0:
            new_index = replica[...] * ROWS_DEV + slot[...]
            rows = old_order(new_index, hidden[...])
            row, column = iota((ROWS, ROWS), 0), iota((ROWS, ROWS), 1)
            order = pick(column == (row & (N_DP - 1)) * ROWS_DEV + (row >> 5))
        else:
            rows = hidden[...].reshape(PADDED, WIDTH)
            row, column = iota((ROWS, PADDED), 0), iota((ROWS, PADDED), 1)
            order = pick(column == (row & (N_DP - 1)) * SLOTS + (row >> 5))
        by_slot = dot(order, rows)
        square = jnp.sum(by_slot * by_slot, axis=1, keepdims=True)
        scaled = (by_slot * gain[...]).astype(BF16)

        def place(part, product):
            for s in range(ROWS_DEV):
                spread[pl.ds((s * PARTS + part) * N_DP, N_DP), :] = product[s * N_DP : (s + 1) * N_DP]

        for part in range(0, GROUP, 2):
            product = dot(scaled, w_query[:, part * HEAD : (part + 2) * HEAD])
            place(part, product[:, :HEAD])
            place(part + 1, product[:, HEAD:])
        place(GROUP, dot(scaled, w_key[...]))
        place(GROUP + 1, dot(scaled, w_value[...]))
        lane = iota((N_DP, HEAD), 1)
        squares = jnp.zeros((N_DP, HEAD), F32)
        for s in range(ROWS_DEV):
            squares = jnp.where(lane == s, square[s * N_DP : (s + 1) * N_DP], squares)
        high = squares.astype(BF16).astype(F32)
        tail = ROWS_DEV * PARTS
        spread[pl.ds(tail * N_DP, N_DP), :] = high
        spread[pl.ds((tail + 1) * N_DP, N_DP), :] = squares - high
        spread[pl.ds((tail + 2) * N_DP, 2 * N_DP), :] = jnp.zeros((2 * N_DP, HEAD), F32)
        for p in range(N_DP):
            payload[p] = spread[pl.ds(p, BLOCK, stride=N_DP), :].astype(BF16)

    @pl.when(scalars[SECTION] != layer)
    def _():
        for s in range(ROWS_DEV):
            payload[scalars[DEST + s]] = keys[s]


def attend_kernel(layer, scalars, cosine, sine, received, keys, values, payload, own):
    @pl.when(scalars[SECTION] == layer)
    def _():
        total = received[0].astype(F32)
        for p in range(1, N_DP):
            total = total + received[p].astype(F32)
        row = iota((BLOCK, HEAD), 0)
        lane = iota((BLOCK, HEAD), 1)
        slot = (row * 205) >> 11
        part = row - slot * PARTS
        tail = ROWS_DEV * PARTS
        squares = total[tail : tail + 1] + total[tail + 1 : tail + 2]
        square = jnp.sum(jnp.where(lane == slot, squares, 0.0), axis=1, keepdims=True)
        projected = total * lax.rsqrt(square / MODEL + EPSILON)
        cos_rows = jnp.ones((BLOCK, HEAD), F32)
        sin_rows = jnp.zeros((BLOCK, HEAD), F32)
        for s in range(ROWS_DEV):
            turned = (slot == s) & (part <= GROUP)
            cos_rows = jnp.where(turned, cosine[s : s + 1, :], cos_rows)
            sin_rows = jnp.where(turned, sine[s : s + 1, :], sin_rows)
        vectors = (
            projected * cos_rows + pltpu.roll(projected, HEAD // 2, 1) * sin_rows
        ).astype(BF16)

        all_keys = keys[...].reshape(ROWS_DEV * CONTEXT, HEAD)
        all_values = values[...].reshape(ROWS_DEV * CONTEXT, HEAD)
        scale = HEAD ** (-0.5)
        scores = dot(vectors, all_keys, ((1,), (1,))) * scale
        among = dot(vectors, vectors, ((1,), (1,))) * scale
        wide = (BLOCK, ROWS_DEV * CONTEXT)
        wide_slot = (iota(wide, 0) * 205) >> 11
        column = iota(wide, 1)
        live = column < 0
        for s in range(ROWS_DEV):
            live = live | (
                (wide_slot == s)
                & (column >= s * CONTEXT)
                & (column < s * CONTEXT + scalars[HELD_LEN + s])
            )
        scores = jnp.where(live, scores, -1e30)
        narrow_slot = slot[:, :BLOCK]
        narrow_column = lane[:, :BLOCK]
        own_score = jnp.sum(
            jnp.where(narrow_column == narrow_slot * PARTS + GROUP, among, 0.0), axis=1, keepdims=True
        )
        highest = jnp.maximum(jnp.max(scores, axis=1, keepdims=True), own_score)
        terms = jnp.exp(scores - highest)
        own_term = jnp.exp(own_score - highest)
        denominator = jnp.sum(terms, axis=1, keepdims=True) + own_term
        weights = (terms / denominator).astype(BF16)
        own_weight = own_term / denominator
        own_weights = jnp.where(
            narrow_column == narrow_slot * PARTS + GROUP + 1, own_weight, 0.0
        ).astype(BF16)
        attended = (dot(weights, all_values) + dot(own_weights, vectors)).astype(BF16)

        out_row, in_row = iota((BLOCK, BLOCK), 0), iota((BLOCK, BLOCK), 1)
        out_slot = out_row & (SLOTS - 1)
        order = pick((in_row == out_slot * PARTS + (out_row >> 3)) & (out_slot < ROWS_DEV))
        block = dot(order, attended)
        own_row, own_in = iota((16, BLOCK), 0), iota((16, BLOCK), 1)
        own_slot = own_row & (SLOTS - 1)
        own_pick = pick(
            (own_in == own_slot * PARTS + GROUP + (own_row >> 3)) & (own_slot < ROWS_DEV)
        )
        own_pair = dot(own_pick, vectors)
        own[...] = own_pair.astype(BF16)
        block_out = block.astype(BF16)
        for p in range(N_DP):
            payload[p] = block_out
        for s in range(ROWS_DEV):
            with_own = jnp.where(row == ROWS_DEV, own_pair[s : s + 1], block)
            with_own = jnp.where(row == ROWS_DEV + 1, own_pair[SLOTS + s : SLOTS + s + 1], with_own)
            payload[scalars[DEST + s]] = with_own.astype(BF16)

    @pl.when(scalars[SECTION] != layer)
    def _():
        for s in range(ROWS_DEV):
            payload[scalars[DEST + s]] = values[s]


def output_kernel(layer, scalars, received, w_out, payload):
    @pl.when(scalars[SECTION] == layer)
    def _():
        total = jnp.zeros((PADDED, WIDTH), F32)
        for h in range(0, GROUP, 2):
            pair = received[:, h * SLOTS : (h + 2) * SLOTS, :].astype(F32)
            left = pair[:, :SLOTS].reshape(PADDED, HEAD).astype(BF16)
            right = pair[:, SLOTS:].reshape(PADDED, HEAD).astype(BF16)
            total = total + dot(
                jnp.concatenate([left, right], 1), w_out[h * HEAD : (h + 2) * HEAD, :]
            )
        real = (iota((PADDED, WIDTH), 0) & (SLOTS - 1)) < ROWS_DEV
        payload[...] = jnp.where(real, total, 0.0).astype(BF16).reshape(N_TS, TS_ROWS, WIDTH)


def sum_kernel(layer, scalars, *refs):
    if layer == 0:
        replica, slot, hidden, received, payload, result = refs
        new_index = replica[...] * ROWS_DEV + slot[...]
        rows = old_order(new_index, hidden[...])
        row, column = iota((TS_ROWS, ROWS), 0), iota((TS_ROWS, ROWS), 1)
        in_slot = row & (SLOTS - 1)
        place = (scalars[TS_BLOCK] * 2 + (row >> 3)) * ROWS_DEV + in_slot
        residual = dot(pick((column == place) & (in_slot < ROWS_DEV)), rows)
    else:
        before, received, payload, result = refs
        residual = before[...].astype(F32)
    total = received[layer].astype(F32)
    for t in range(1, N_TS // 2):
        total = total + received[2 * t + layer].astype(F32)
    total = (residual + total).astype(BF16)
    result[...] = total
    for i in range(N_TS):
        payload[i] = total


def order_kernel(scalars, replica, slot, first, second, out):
    new_index = replica[...] * ROWS_DEV + slot[...]
    to_new = pick(iota((ROWS, ROWS), 0) == new_index)
    row, column = iota((ROWS, PADDED), 0), iota((ROWS, PADDED), 1)
    group = over_six(row)
    compact = pick(column == group * SLOTS + row - group * ROWS_DEV)

    def write(source):
        rows = dot(compact, source[...].reshape(PADDED, WIDTH)).astype(BF16)
        out[...] = dot(to_new, rows).astype(BF16)

    pl.when(scalars[SECTION] == 0)(lambda: write(first))
    pl.when(scalars[SECTION] == 1)(lambda: write(second))


def cache_kernel(
    scalars, keys, values, own_0, own_1, scatter_0, gather_0, scatter_1, gather_1, key_out, value_out
):
    me = scalars[REPLICA]
    position = iota((CONTEXT, HEAD), 0)

    def write(moved_keys, moved_values, gathered, own):
        own_rows = own[...].astype(F32)
        for r in range(ROWS_DEV):
            source = scalars[SOURCE + r]
            anchor = over_six(source)
            held = source - anchor * ROWS_DEV
            written = position == scalars[NEW_LEN + r]

            @pl.when(anchor == me)
            def _():
                own_row = iota((16, HEAD), 0)
                new_key = jnp.sum(jnp.where(own_row == held, own_rows, 0.0), axis=0, keepdims=True)
                new_value = jnp.sum(
                    jnp.where(own_row == held + SLOTS, own_rows, 0.0), axis=0, keepdims=True
                )
                key_out[r] = jnp.where(written, new_key, keys[held].astype(F32)).astype(BF16)
                value_out[r] = jnp.where(written, new_value, values[held].astype(F32)).astype(BF16)

            @pl.when(anchor != me)
            def _():
                pair = gathered[anchor, 0:16, :].astype(F32)
                new_key = pair[ROWS_DEV : ROWS_DEV + 1]
                new_value = pair[ROWS_DEV + 1 : ROWS_DEV + 2]
                key_out[r] = jnp.where(written, new_key, moved_keys[anchor].astype(F32)).astype(BF16)
                value_out[r] = jnp.where(
                    written, new_value, moved_values[anchor].astype(F32)
                ).astype(BF16)

    pl.when(scalars[SECTION] == 0)(lambda: write(scatter_1, gather_1, gather_0, own_0))
    pl.when(scalars[SECTION] == 1)(lambda: write(scatter_0, gather_0, gather_1, own_1))


def call(kernel, out_shapes, operands, scratch=(), name=None):
    return pl.pallas_call(
        kernel,
        out_shape=out_shapes,
        in_specs=[SMEM_SPEC] + [VMEM_SPEC] * (len(operands) - 1),
        out_specs=jax.tree.map(lambda _: VMEM_SPEC, out_shapes),
        scratch_shapes=list(scratch),
        compiler_params=pltpu.CompilerParams(vmem_limit_bytes=24 * 1024 * 1024),
        name=name,
    )(*operands)


def exchange(value, axes):
    return lax.all_to_all(value, axes, split_axis=0, concat_axis=0, tiled=True)


def on_device(
    hidden_in,
    norm_gain,
    w_query,
    w_key,
    w_value,
    w_out,
    key_cache,
    value_cache,
    context_len,
    dest_replica,
    dest_slot,
):
    me = lax.axis_index("dp")
    section = lax.axis_index("section")
    ts_block = lax.axis_index("tensor") * 2 + section
    keys, values = key_cache[0], value_cache[0]
    first_row = me * ROWS_DEV
    new_index = dest_replica * ROWS_DEV + dest_slot
    dest = lax.dynamic_slice_in_dim(dest_replica, first_row, ROWS_DEV)
    held_len = lax.dynamic_slice_in_dim(context_len, first_row, ROWS_DEV)
    mine = new_index[None, :] == (first_row + jnp.arange(ROWS_DEV, dtype=jnp.int32))[:, None]
    source = jnp.sum(jnp.where(mine, jnp.arange(ROWS, dtype=jnp.int32)[None, :], 0), 1)
    new_len = jnp.sum(jnp.where(mine, context_len[None, :], 0), 1)
    scalars = jnp.concatenate(
        [jnp.stack([section, me, ts_block, section]).astype(jnp.int32), dest, held_len, source, new_len]
    )
    half = HEAD // 2
    inverse_freq = ROPE_BASE ** (-(jnp.arange(half, dtype=F32) * (2.0 / HEAD)))
    padded_len = jnp.concatenate([held_len, jnp.zeros((SLOTS - ROWS_DEV,), jnp.int32)])
    angles = padded_len.astype(F32)[:, None] * jnp.concatenate([inverse_freq, inverse_freq])[None, :]
    cosine = jnp.cos(angles)
    sine = jnp.sin(angles) * jnp.where(jnp.arange(HEAD) < half, -1.0, 1.0)[None, :]
    replica_row, slot_row = dest_replica[None, :], dest_slot[None, :]

    block_shape = jax.ShapeDtypeStruct((N_DP, BLOCK, HEAD), BF16)
    ts_shape = jax.ShapeDtypeStruct((N_TS, TS_ROWS, WIDTH), BF16)
    result_shape = jax.ShapeDtypeStruct((TS_ROWS, WIDTH), BF16)
    own_shape = jax.ShapeDtypeStruct((16, HEAD), BF16)
    tables = (replica_row, slot_row)
    weights = (norm_gain, w_query[0], w_key[0], w_value[0])

    hidden, before = hidden_in, None
    scattered, gathered, owns, outputs = [], [], [], []
    for layer in range(2):
        project = lambda *refs, layer=layer: project_kernel(layer, *refs)
        attend = lambda *refs, layer=layer: attend_kernel(layer, *refs)
        output = lambda *refs, layer=layer: output_kernel(layer, *refs)
        summed = lambda *refs, layer=layer: sum_kernel(layer, *refs)
        payload = call(
            project,
            block_shape,
            (scalars,) + (tables if layer == 0 else ()) + (hidden,) + weights + (keys,),
            [pltpu.VMEM((BLOCK * N_DP, HEAD), F32)],
            name="project",
        )
        partials = exchange(payload, "dp")
        payload, own = call(
            attend,
            (block_shape, own_shape),
            (scalars, cosine, sine, partials, keys, values),
            name="attend",
        )
        rows = exchange(payload, "dp")
        payload = call(output, ts_shape, (scalars, rows, w_out[0]), name="output")
        received = exchange(payload, ("tensor", "section"))
        payload, before = call(
            summed,
            (ts_shape, result_shape),
            (scalars,) + (tables + (hidden_in,) if layer == 0 else (before,)) + (received,),
            name="sum",
        )
        hidden = exchange(payload, ("tensor", "section"))
        scattered.append(partials)
        gathered.append(rows)
        owns.append(own)
        outputs.append(hidden)

    cache_shape = jax.ShapeDtypeStruct((ROWS_DEV, CONTEXT, HEAD), BF16)
    key_out, value_out = call(
        cache_kernel,
        (cache_shape, cache_shape),
        (scalars, keys, values, *owns, scattered[0], gathered[0], scattered[1], gathered[1]),
        name="caches",
    )
    layer_out = call(
        order_kernel,
        jax.ShapeDtypeStruct((ROWS, WIDTH), BF16),
        (scalars,) + tables + tuple(outputs),
        name="order",
    )
    return layer_out[None], key_out[None], value_out[None]


def solution(mesh):
    return jax.shard_map(
        on_device,
        mesh=mesh,
        in_specs=(
            P(None, "dp"),
            P("section", "dp"),
            P("section", "dp", "tensor"),
            P("section", "dp", "tensor"),
            P("section", "dp", "tensor"),
            P("section", "tensor", "dp"),
            P("section", "dp", None, "tensor"),
            P("section", "dp", None, "tensor"),
            P(),
            P(),
            P(),
        ),
        out_specs=(
            P("section", None, "dp"),
            P("section", "dp", None, "tensor"),
            P("section", "dp", None, "tensor"),
        ),
        check_vma=False,
    )
```

```python
import jax
import jax.numpy as jnp
from jax import lax
from jax.experimental import pallas as pl
from jax.experimental.pallas import tpu as pltpu
from jax.sharding import PartitionSpec as P

N_DP = 32
N_TENSOR = 8
ROWS_DEV = 6
ROWS = 192
TRIO = 3
HALF_ROWS = N_DP * TRIO
CONTEXT = 64
MOVES = 4
PIECES = 4
HEAD = 128
GROUP = 8
PARTS = GROUP + 2
USED = 32
BLOCK = USED + MOVES * PIECES
WIDTH = 256
MODEL = 8192
CACHE_ROWS = TRIO * CONTEXT
GAIN_ROW = CACHE_ROWS + WIDTH
EPSILON = 1e-06
ROPE_BASE = 1000000.0
F32 = jnp.float32
BF16 = jnp.bfloat16

SECTION, REPLICA = 0, 1
DEST, HELD_LEN, NEW_LEN, SOURCE = 0, 6, 12, 18

SMEM_SPEC = pl.BlockSpec(memory_space=pltpu.SMEM)
VMEM_SPEC = pl.BlockSpec(memory_space=pltpu.VMEM)
HBM_SPEC = pl.BlockSpec(memory_space=pltpu.HBM)


def iota(shape, dim):
    return lax.broadcasted_iota(jnp.int32, shape, dim)


def pick(condition):
    return jnp.where(condition, 1.0, 0.0).astype(BF16)


def over_six(index):
    return (index * 171) >> 10


def over_ten(index):
    return (index * 205) >> 11


def dot(left, right, contract=((1,), (0,))):
    return lax.dot_general(left, right, (contract, ((), ())), preferred_element_type=F32)


def to_new_order(new_index):
    return pick(iota((ROWS, ROWS), 0) == new_index)


def spread_part(spread, slots, part, product, first=0):
    for s in range(slots):
        row = (s // TRIO) * USED + (s % TRIO) * PARTS + part
        spread[pl.ds(row * N_DP, N_DP), :] = product[s * N_DP : (s + 1) * N_DP]


def spread_squares(spread, slots, square):
    lane = iota((N_DP, HEAD), 1)
    for half in range(slots // TRIO):
        squares = jnp.zeros((N_DP, HEAD), F32)
        for s in range(TRIO):
            first = (half * TRIO + s) * N_DP
            squares = jnp.where(lane == s, square[first : first + N_DP], squares)
        high = squares.astype(BF16).astype(F32)
        row = half * USED + TRIO * PARTS
        spread[pl.ds(row * N_DP, N_DP), :] = high
        spread[pl.ds((row + 1) * N_DP, N_DP), :] = squares - high


def spread_products(spread, slots, scaled, w_query, w_key, w_value):
    for part in range(0, GROUP, 2):
        product = dot(scaled, w_query[:, part * HEAD : (part + 2) * HEAD])
        spread_part(spread, slots, part, product[:, :HEAD])
        spread_part(spread, slots, part + 1, product[:, HEAD:])
    spread_part(spread, slots, GROUP, dot(scaled, w_key))
    spread_part(spread, slots, GROUP + 1, dot(scaled, w_value))


def gathered_block(spread, half, replica):
    return spread[pl.ds(half * USED * N_DP + replica, USED, stride=N_DP), :].astype(BF16)


def first_kernel(
    ids, new_index, hidden_in, gain_in, query_in, key_in, value_in,
    kept, shipped, residual, to_slots_out,
    spread, hidden, gain, w_query, w_key, w_value, arrived,
):
    pairs = (
        (hidden_in, hidden),
        (gain_in, gain),
        (query_in.at[0], w_query),
        (key_in.at[0], w_key),
        (value_in.at[0], w_value),
    )
    copies = [pltpu.make_async_copy(src, dst, arrived.at[i]) for i, (src, dst) in enumerate(pairs)]
    for copy in copies:
        copy.start()
    row, column = iota((ROWS, ROWS), 0), iota((ROWS, ROWS), 1)
    by_slot_order = pick(column == (row & (N_DP - 1)) * ROWS_DEV + (row >> 5))
    to_slots = dot(by_slot_order, to_new_order(new_index[...]), ((1,), (1,))).astype(BF16)
    to_slots_out[...] = to_slots
    copies[0].wait()
    by_slot = dot(to_slots, hidden[...])

    @pl.when(ids[SECTION] == 0)
    def _():
        residual[...] = by_slot[:HALF_ROWS].astype(BF16)

    @pl.when(ids[SECTION] == 1)
    def _():
        residual[...] = by_slot[HALF_ROWS:].astype(BF16)

    for copy in copies[1:]:
        copy.wait()

    @pl.when(ids[SECTION] == 0)
    def _():
        square = jnp.sum(by_slot * by_slot, axis=1, keepdims=True)
        scaled = (by_slot * gain[...]).astype(BF16)
        spread_products(spread, ROWS_DEV, scaled, w_query, w_key[...], w_value[...])
        spread_squares(spread, ROWS_DEV, square)
        for p in range(N_DP):
            kept[p] = gathered_block(spread, 0, p)
            shipped[p] = gathered_block(spread, 1, p)


def join_kernel(ids, table, kept, received, keys, values, payload, spread):
    count = jnp.int32(0)
    for s in range(ROWS_DEV):
        leaves = table[DEST + s] != ids[REPLICA]

        @pl.when(leaves)
        def _():
            base = pl.multiple_of(count * (PIECES * N_DP), N_DP)
            spread[pl.ds(base, CONTEXT), :] = keys[s].astype(F32)
            spread[pl.ds(base + CONTEXT, CONTEXT), :] = values[s].astype(F32)

        count = count + jnp.where(leaves, 1, 0)
    for p in range(N_DP):
        payload[p, USED:, :] = spread[pl.ds(p, MOVES * PIECES, stride=N_DP), :].astype(BF16)

    @pl.when(ids[SECTION] == 0)
    def _():
        payload[:, :USED, :] = kept[...]

    @pl.when(ids[SECTION] == 1)
    def _():
        payload[:, :USED, :] = received[...]


def pack_kernel(ids, keys, values, w_key, w_value, gain, packed):
    other = (1 - ids[SECTION]) * TRIO
    for s in range(TRIO):
        packed[s * CONTEXT : (s + 1) * CONTEXT, :HEAD] = keys[other + s]
        packed[s * CONTEXT : (s + 1) * CONTEXT, HEAD:] = values[other + s]
    packed[CACHE_ROWS:GAIN_ROW, :HEAD] = w_key[...]
    packed[CACHE_ROWS:GAIN_ROW, HEAD:] = w_value[...]
    high = gain[...].astype(BF16).astype(F32)
    middle = (gain[...] - high).astype(BF16).astype(F32)
    low = gain[...] - high - middle
    row = iota((16, WIDTH), 0)
    terms = jnp.where(row == 0, high, jnp.where(row == 1, middle, jnp.where(row == 2, low, 0.0)))
    packed[GAIN_ROW:, :] = terms.astype(BF16)


def choose_kernel(layer, ids, local, other, chosen):
    @pl.when(ids[SECTION] == layer)
    def _():
        chosen[...] = local[...]

    @pl.when(ids[SECTION] != layer)
    def _():
        chosen[...] = other[...]


def forward(route, received, payload, pieces, sorted_pieces):
    count = N_DP * MOVES
    for p in range(N_DP):
        pieces[pl.ds(p * MOVES * PIECES, MOVES * PIECES), :] = received[p, USED:, :].astype(F32)
    to_replica = pick(iota((count, count), 0) == route[...])
    for i in range(PIECES):
        part = pieces[pl.ds(i, count, stride=PIECES), :].astype(BF16)
        sorted_pieces[pl.ds(i, count, stride=PIECES), :] = dot(to_replica, part, ((0,), (0,)))
    for p in range(N_DP):
        payload[p, USED:, :] = sorted_pieces[
            pl.ds(p * MOVES * PIECES, MOVES * PIECES), :
        ].astype(BF16)


def attend_kernel(
    layer, ids, table, cosine, sine, received, keys, values, packed, *refs
):
    if layer == 0:
        route, payload, own, pieces, sorted_pieces = refs
        forward(route, received, payload, pieces, sorted_pieces)
    else:
        payload, own = refs
    section = ids[SECTION]

    def attend(all_keys, all_values):
        total = received[0, :USED, :].astype(F32)
        for p in range(1, N_DP):
            total = total + received[p, :USED, :].astype(F32)
        row = iota((USED, HEAD), 0)
        lane = iota((USED, HEAD), 1)
        slot = over_ten(row)
        part = row - slot * PARTS
        tail = TRIO * PARTS
        squares = total[tail : tail + 1] + total[tail + 1 : tail + 2]
        square = jnp.sum(jnp.where(lane == slot, squares, 0.0), axis=1, keepdims=True)
        projected = total * lax.rsqrt(square / MODEL + EPSILON)
        cos_rows = jnp.ones((USED, HEAD), F32)
        sin_rows = jnp.zeros((USED, HEAD), F32)
        for s in range(TRIO):
            turned = (slot == s) & (part <= GROUP)
            cos_rows = jnp.where(turned, cosine[pl.ds(section * TRIO + s, 1), :], cos_rows)
            sin_rows = jnp.where(turned, sine[pl.ds(section * TRIO + s, 1), :], sin_rows)
        vectors = (
            projected * cos_rows + pltpu.roll(projected, HEAD // 2, 1) * sin_rows
        ).astype(BF16)

        scale = HEAD ** (-0.5)
        scores = dot(vectors, all_keys, ((1,), (1,))) * scale
        among = dot(vectors, vectors, ((1,), (1,))) * scale
        wide = (USED, CACHE_ROWS)
        wide_slot = over_ten(iota(wide, 0))
        column = iota(wide, 1)
        live = column < 0
        for s in range(TRIO):
            live = live | (
                (wide_slot == s)
                & (column >= s * CONTEXT)
                & (column < s * CONTEXT + table[HELD_LEN + section * TRIO + s])
            )
        scores = jnp.where(live, scores, -1e30)
        small_slot = over_ten(iota((USED, USED), 0))
        small_column = iota((USED, USED), 1)
        own_score = jnp.sum(
            jnp.where(small_column == small_slot * PARTS + GROUP, among, 0.0), axis=1, keepdims=True
        )
        highest = jnp.maximum(jnp.max(scores, axis=1, keepdims=True), own_score)
        terms = jnp.exp(scores - highest)
        own_term = jnp.exp(own_score - highest)
        denominator = jnp.sum(terms, axis=1, keepdims=True) + own_term
        weights = (terms / denominator).astype(BF16)
        own_weights = jnp.where(
            small_column == small_slot * PARTS + GROUP + 1, own_term / denominator, 0.0
        ).astype(BF16)
        attended = (dot(weights, all_values) + dot(own_weights, vectors)).astype(BF16)

        out_row, in_row = iota((USED, USED), 0), iota((USED, USED), 1)
        out_slot = out_row >> 3
        order = pick((in_row == out_slot * PARTS + (out_row & 7)) & (out_slot < TRIO))
        block = dot(order, attended)
        own_row, own_in = iota((16, USED), 0), iota((16, USED), 1)
        own_slot = own_row & 7
        own_pick = pick(
            (own_in == own_slot * PARTS + GROUP + (own_row >> 3)) & (own_slot < TRIO)
        )
        own_pair = dot(own_pick, vectors)
        own[...] = own_pair.astype(BF16)
        block_out = block.astype(BF16)
        for p in range(N_DP):
            payload[p, :USED, :] = block_out
        for s in range(TRIO):
            with_own = jnp.where(row == TRIO * 8, own_pair[s : s + 1], block)
            with_own = jnp.where(row == TRIO * 8 + 1, own_pair[8 + s : 9 + s], with_own)
            payload[table[DEST + section * TRIO + s], :USED, :] = with_own.astype(BF16)

    @pl.when(section == layer)
    def _():
        first = layer * TRIO
        attend(
            keys[first : first + TRIO].reshape(CACHE_ROWS, HEAD),
            values[first : first + TRIO].reshape(CACHE_ROWS, HEAD),
        )

    @pl.when(section != layer)
    def _():
        attend(packed[:CACHE_ROWS, :HEAD], packed[:CACHE_ROWS, HEAD:])


def output_kernel(received, weight, payload, wide, rows):
    for p in range(N_DP):
        wide[pl.ds(p * USED, USED), :] = received[p, :USED, :].astype(F32)
    for s in range(TRIO):
        for h in range(GROUP):
            rows[s * N_DP : (s + 1) * N_DP, h * HEAD : (h + 1) * HEAD] = wide[
                pl.ds(s * 8 + h, N_DP, stride=USED), :
            ].astype(BF16)

    product = dot(rows[...], weight[...]).astype(BF16)
    for t in range(N_TENSOR):
        payload[t] = product


def summed(received, residual):
    total = received[0].astype(F32)
    for t in range(1, N_TENSOR):
        total = total + received[t].astype(F32)
    return (residual[...].astype(F32) + total).astype(BF16)


def second_kernel(
    ids, received, residual, gain, query, w_key, w_value, packed, payload, result, spread
):
    rows = summed(received, residual)
    result[...] = rows
    by_slot = rows.astype(F32)
    spread_squares(spread, TRIO, jnp.sum(by_slot * by_slot, axis=1, keepdims=True))

    @pl.when(ids[SECTION] == 1)
    def _():
        scaled = (by_slot * gain[...]).astype(BF16)
        spread_products(spread, TRIO, scaled, query, w_key[...], w_value[...])

    @pl.when(ids[SECTION] == 0)
    def _():
        terms = packed[GAIN_ROW:, :].astype(F32)
        other_gain = terms[0:1] + terms[1:2] + terms[2:3]
        scaled = (by_slot * other_gain).astype(BF16)
        spread_products(
            spread,
            TRIO,
            scaled,
            query,
            packed[CACHE_ROWS:GAIN_ROW, :HEAD],
            packed[CACHE_ROWS:GAIN_ROW, HEAD:],
        )

    for p in range(N_DP):
        payload[p] = gathered_block(spread, 0, p)


def last_kernel(ids, received, before, done, result, swapped):
    rows = summed(received, before)
    result[...] = rows

    @pl.when(ids[SECTION] == 0)
    def _():
        swapped[...] = rows

    @pl.when(ids[SECTION] == 1)
    def _():
        swapped[...] = before[...]


def order_kernel(ids, to_slots, first, second, received, out):
    def write(low, high):
        out[...] = (
            dot(to_slots[:HALF_ROWS, :], low[...], ((0,), (0,)))
            + dot(to_slots[HALF_ROWS:, :], high[...], ((0,), (0,)))
        ).astype(BF16)

    pl.when(ids[SECTION] == 0)(lambda: write(first, received))
    pl.when(ids[SECTION] == 1)(lambda: write(received, second))


def own_kernel(ids, table, gathered_0, gathered_1, own_0, own_1, mine, swapped):
    me, section = ids[REPLICA], ids[SECTION]
    row = iota((16, HEAD), 0)
    for layer, (gathered, own) in enumerate(((gathered_0, own_0), (gathered_1, own_1))):
        own_rows = own[...].astype(F32)
        total = jnp.zeros((16, HEAD), F32)
        for r in range(ROWS_DEV):
            source = table[SOURCE + r]
            anchor = over_six(source)
            held = source - anchor * ROWS_DEV
            slot = held - section * TRIO
            here = (slot >= 0) & (slot < TRIO)
            stays = jnp.where(here & (anchor == me), 1.0, 0.0)
            moves = jnp.where(here & (anchor != me), 1.0, 0.0)
            pair = gathered[anchor, USED - 16 : USED, :].astype(F32)
            kept_key = jnp.sum(jnp.where(row == slot, own_rows, 0.0), axis=0, keepdims=True)
            kept_value = jnp.sum(jnp.where(row == slot + 8, own_rows, 0.0), axis=0, keepdims=True)
            new_key = kept_key * stays + pair[8:9] * moves
            new_value = kept_value * stays + pair[9:10] * moves
            total = jnp.where(row == r, new_key, jnp.where(row == r + 8, new_value, total))
        total = total.astype(BF16)

        @pl.when(section == layer)
        def _():
            mine[...] = total

        @pl.when(section != layer)
        def _():
            swapped[...] = total


def cache_kernel(
    ids, table, keys, values, mine, received, gathered, key_out, value_out, done, pieces
):
    me = ids[REPLICA]
    position = iota((CONTEXT, HEAD), 0)
    own = mine[...].astype(F32) + received[...].astype(F32)
    done[...] = own[:8]
    for p in range(N_DP):
        pieces[pl.ds(p * MOVES * PIECES, MOVES * PIECES), :] = gathered[p, USED:, :].astype(F32)
    count = jnp.int32(0)
    for r in range(ROWS_DEV):
        source = table[SOURCE + r]
        anchor = over_six(source)
        written = position == table[NEW_LEN + r]
        moves = anchor != me

        def write(key_rows, value_rows):
            key_out[r] = jnp.where(written, own[r : r + 1], key_rows).astype(BF16)
            value_out[r] = jnp.where(written, own[r + 8 : r + 9], value_rows).astype(BF16)

        @pl.when(anchor == me)
        def _():
            held = source - anchor * ROWS_DEV
            write(keys[held].astype(F32), values[held].astype(F32))

        @pl.when(moves)
        def _():
            parts = [
                pieces[pl.ds(count * PIECES + i, N_DP, stride=MOVES * PIECES), :]
                for i in range(PIECES)
            ]
            write(jnp.concatenate(parts[:2], 0), jnp.concatenate(parts[2:], 0))

        count = count + jnp.where(moves, 1, 0)


def call(kernel, name, specs, out_shapes, operands, scratch=()):
    spec_of = {"s": SMEM_SPEC, "v": VMEM_SPEC, "h": HBM_SPEC, "a": pl.BlockSpec(memory_space=pl.ANY)}
    return pl.pallas_call(
        kernel,
        out_shape=out_shapes,
        in_specs=[spec_of[letter] for letter in specs],
        out_specs=jax.tree.map(lambda _: VMEM_SPEC, out_shapes),
        scratch_shapes=list(scratch),
        compiler_params=pltpu.CompilerParams(vmem_limit_bytes=8 * 1024 * 1024),
        name=name,
    )(*operands)


def exchange(value, axis):
    return lax.all_to_all(value, axis, split_axis=0, concat_axis=0, tiled=True)


def swap(value):
    return lax.ppermute(value, "section", [(0, 1), (1, 0)])


def shape(*dims):
    return jax.ShapeDtypeStruct(dims, BF16)


def on_device(
    hidden_in,
    norm_gain,
    w_query,
    w_key,
    w_value,
    w_out,
    key_cache,
    value_cache,
    context_len,
    dest_replica,
    dest_slot,
):
    me = lax.axis_index("dp")
    section = lax.axis_index("section")
    ids = jnp.stack([section, me]).astype(jnp.int32)
    keys, values = key_cache[0], value_cache[0]
    new_index = (dest_replica * ROWS_DEV + dest_slot)[None, :]
    row = jnp.arange(ROWS, dtype=jnp.int32)
    leaves = dest_replica != row // ROWS_DEV
    before = (row[None, :] // ROWS_DEV == row[:, None] // ROWS_DEV) & (row[None, :] < row[:, None])
    rank = jnp.sum(jnp.where(before & leaves[None, :], 1, 0), 1)
    before = (dest_replica[None, :] == dest_replica[:, None]) & (
        dest_slot[None, :] < dest_slot[:, None]
    )
    place = jnp.sum(jnp.where(before & leaves[None, :], 1, 0), 1)
    arrival = jnp.where(leaves, dest_replica * MOVES + place, -1)
    chosen = arrival[None, :] == jnp.arange(N_DP * MOVES, dtype=jnp.int32)[:, None]
    route = jnp.sum(jnp.where(chosen, (row // ROWS_DEV * MOVES + rank)[None, :], 0), 1)[None, :]
    entry = jnp.arange(4 * ROWS_DEV, dtype=jnp.int32)[:, None]
    kind = entry // ROWS_DEV
    wanted = me * ROWS_DEV + entry % ROWS_DEV
    found = jnp.where(kind < 2, row[None, :], new_index) == wanted
    chosen = jnp.where(
        kind == 0, dest_replica[None, :], jnp.where(kind == 3, row[None, :], context_len[None, :])
    )
    table = jnp.sum(jnp.where(found, chosen, 0), 1)

    half = HEAD // 2
    inverse_freq = ROPE_BASE ** (-(jnp.arange(half, dtype=F32) * (2.0 / HEAD)))
    held_len = jnp.concatenate([table[HELD_LEN : HELD_LEN + ROWS_DEV], jnp.zeros((2,), jnp.int32)])
    angles = held_len.astype(F32)[:, None] * jnp.concatenate([inverse_freq, inverse_freq])[None, :]
    cosine = jnp.cos(angles)
    sine = jnp.sin(angles) * jnp.where(jnp.arange(HEAD) < half, -1.0, 1.0)[None, :]

    kept, shipped, residual, to_slots = call(
        first_kernel,
        "first",
        "svhhhhh",
        (shape(N_DP, USED, HEAD), shape(N_DP, USED, HEAD), shape(HALF_ROWS, WIDTH), shape(ROWS, ROWS)),
        (ids, new_index, hidden_in, norm_gain, w_query, w_key, w_value),
        [
            pltpu.VMEM((2 * USED * N_DP, HEAD), F32),
            pltpu.VMEM((ROWS, WIDTH), BF16),
            pltpu.VMEM((1, WIDTH), F32),
            pltpu.VMEM((WIDTH, GROUP * HEAD), BF16),
            pltpu.VMEM((WIDTH, HEAD), BF16),
            pltpu.VMEM((WIDTH, HEAD), BF16),
            pltpu.SemaphoreType.DMA((5,)),
        ],
    )
    payload = call(
        join_kernel,
        "join",
        "ssvvvv",
        shape(N_DP, BLOCK, HEAD),
        (ids, table, kept, swap(shipped), keys, values),
        [pltpu.VMEM((MOVES * PIECES * N_DP, HEAD), F32)],
    )
    first = exchange(payload, "dp")

    late_keys, late_values, late_key, late_value, late_gain, late_query, late_out, _ = (
        lax.optimization_barrier(
            (keys, values, w_key[0], w_value[0], norm_gain, w_query[0], w_out[0], payload)
        )
    )
    packed = swap(
        call(
            pack_kernel,
            "pack",
            "svvvvv",
            shape(GAIN_ROW + 16, WIDTH),
            (ids, late_keys, late_values, late_key, late_value, late_gain),
        )
    )

    def choose(layer, local, other):
        return call(
            lambda *refs: choose_kernel(layer, *refs),
            "choose",
            "svv",
            shape(*local.shape),
            (ids, local, other),
        )

    def attend(layer, received, *more):
        return call(
            lambda *refs: attend_kernel(layer, *refs),
            "attend",
            "ssvvvvvv" + "v" * len(more),
            (shape(N_DP, USED if layer else BLOCK, HEAD), shape(16, HEAD)),
            (ids, table, cosine, sine, received, keys, values, packed, *more),
            [] if layer else [pltpu.VMEM((N_DP * MOVES * PIECES, HEAD), F32)] * 2,
        )

    def output(received, weight):
        return call(
            output_kernel,
            "output",
            "vv",
            shape(N_TENSOR, HALF_ROWS, WIDTH),
            (received, weight),
            [pltpu.VMEM((N_DP * USED, HEAD), F32), pltpu.VMEM((HALF_ROWS, GROUP * HEAD), BF16)],
        )

    payload, own_0 = attend(0, first, route)
    second = exchange(payload, "dp")
    out_other = swap(late_out)
    sums = exchange(output(second, choose(0, late_out, out_other)), "tensor")
    query = choose(1, late_query, swap(late_query))
    payload, result_0 = call(
        second_kernel,
        "second",
        "svvvvvvv",
        (shape(N_DP, USED, HEAD), shape(HALF_ROWS, WIDTH)),
        (ids, sums, residual, late_gain, query, late_key, late_value, packed),
        [pltpu.VMEM((USED * N_DP, HEAD), F32)],
    )
    third = exchange(payload, "dp")
    payload, own_1 = attend(1, third)
    fourth = exchange(payload, "dp")
    sums = exchange(output(fourth, choose(1, late_out, out_other)), "tensor")
    mine, swapped_own = call(
        own_kernel,
        "own",
        "ssvvvv",
        (shape(16, HEAD), shape(16, HEAD)),
        (ids, table, second, fourth, own_0, own_1),
    )
    key_out, value_out, done = call(
        cache_kernel,
        "caches",
        "ssvvvvv",
        (
            shape(ROWS_DEV, CONTEXT, HEAD),
            shape(ROWS_DEV, CONTEXT, HEAD),
            jax.ShapeDtypeStruct((8, HEAD), F32),
        ),
        (ids, table, keys, values, mine, swap(swapped_own), second),
        [pltpu.VMEM((N_DP * MOVES * PIECES, HEAD), F32)],
    )
    result_1, swapped = call(
        last_kernel,
        "last",
        "svva",
        (shape(HALF_ROWS, WIDTH), shape(HALF_ROWS, WIDTH)),
        (ids, sums, result_0, done),
    )
    layer_out = call(
        order_kernel,
        "order",
        "svvvv",
        shape(ROWS, WIDTH),
        (ids, to_slots, result_0, result_1, swap(swapped)),
    )
    return layer_out[None], key_out[None], value_out[None]


def solution(mesh):
    return jax.shard_map(
        on_device,
        mesh=mesh,
        in_specs=(
            P(None, "dp"),
            P("section", "dp"),
            P("section", "dp", "tensor"),
            P("section", "dp", "tensor"),
            P("section", "dp", "tensor"),
            P("section", "tensor", "dp"),
            P("section", "dp", None, "tensor"),
            P("section", "dp", None, "tensor"),
            P(),
            P(),
            P(),
        ),
        out_specs=(
            P("section", None, "dp"),
            P("section", "dp", None, "tensor"),
            P("section", "dp", None, "tensor"),
        ),
        check_vma=False,
    )
```

```python
import jax
import jax.numpy as jnp
from jax import lax
from jax.experimental import pallas as pl
from jax.experimental.pallas import tpu as pltpu
from jax.sharding import PartitionSpec as P

N_DP = 32
N_TENSOR = 8
ROWS_DEV = 6
ROWS = 192
TRIO = 3
HALF_ROWS = N_DP * TRIO
CONTEXT = 64
MOVES = 4
PIECES = 4
HEAD = 128
GROUP = 8
PARTS = GROUP + 2
USED = 32
BLOCK = USED + MOVES * PIECES
WIDTH = 256
MODEL = 8192
CACHE_ROWS = TRIO * CONTEXT
QUERY = GROUP * HEAD
ALL_PARTS = PARTS * HEAD
EPSILON = 1e-06
ROPE_BASE = 1000000.0
F32 = jnp.float32
BF16 = jnp.bfloat16

SECTION, REPLICA = 0, 1
DEST, HELD_LEN, NEW_LEN, SOURCE = 0, 6, 12, 18

SMEM_SPEC = pl.BlockSpec(memory_space=pltpu.SMEM)
VMEM_SPEC = pl.BlockSpec(memory_space=pltpu.VMEM)
HBM_SPEC = pl.BlockSpec(memory_space=pltpu.HBM)


def iota(shape, dim):
    return lax.broadcasted_iota(jnp.int32, shape, dim)


def pick(condition):
    return jnp.where(condition, 1.0, 0.0).astype(BF16)


def over_six(index):
    return (index * 171) >> 10


def over_ten(index):
    return (index * 205) >> 11


def dot(left, right, contract=((1,), (0,))):
    return lax.dot_general(left, right, (contract, ((), ())), preferred_element_type=F32)


def to_new_order(new_index):
    return pick(iota((ROWS, ROWS), 0) == new_index)


def project(rows, weights, spread):
    by_slot = rows.astype(F32)
    terms = weights[WIDTH:, :WIDTH].astype(F32)
    gain = terms[0:1] + terms[1:2] + terms[2:3]
    scaled = (by_slot * gain).astype(BF16)
    for pair in range(PARTS // 2):
        product = dot(scaled, weights[:WIDTH, pair * 2 * HEAD : (pair + 1) * 2 * HEAD])
        for s in range(TRIO):
            for side in range(2):
                row = s * PARTS + 2 * pair + side
                spread[pl.ds(row * N_DP, N_DP), :] = product[
                    s * N_DP : (s + 1) * N_DP, side * HEAD : (side + 1) * HEAD
                ]


def spread_squares(rows, spread):
    by_slot = rows.astype(F32)
    square = jnp.sum(by_slot * by_slot, axis=1, keepdims=True)
    lane = iota((N_DP, HEAD), 1)
    squares = jnp.zeros((N_DP, HEAD), F32)
    for s in range(TRIO):
        squares = jnp.where(lane == s, square[s * N_DP : (s + 1) * N_DP], squares)
    high = squares.astype(BF16).astype(F32)
    row = TRIO * PARTS
    spread[pl.ds(row * N_DP, N_DP), :] = high
    spread[pl.ds((row + 1) * N_DP, N_DP), :] = squares - high


def load_kernel(query_in, key_in, value_in, gain_in, weights, gain, arrived):
    copies = [
        pltpu.make_async_copy(source, target, arrived.at[i])
        for i, (source, target) in enumerate(
            (
                (gain_in, gain),
                (query_in.at[0], weights.at[:WIDTH, :QUERY]),
                (key_in.at[0], weights.at[:WIDTH, QUERY : QUERY + HEAD]),
                (value_in.at[0], weights.at[:WIDTH, QUERY + HEAD :]),
            )
        )
    ]
    for copy in copies:
        copy.start()
    copies[0].wait()
    high = gain[...].astype(BF16).astype(F32)
    middle = (gain[...] - high).astype(BF16).astype(F32)
    low = gain[...] - high - middle
    row = iota((16, WIDTH), 0)
    terms = jnp.where(row == 0, high, jnp.where(row == 1, middle, jnp.where(row == 2, low, 0.0)))
    weights[WIDTH:, :WIDTH] = terms.astype(BF16)
    weights[WIDTH:, WIDTH:] = jnp.zeros((16, ALL_PARTS - WIDTH), BF16)
    for copy in copies[1:]:
        copy.wait()


def prepare_kernel(ids, new_index, hidden, residual, to_slots_out):
    row, column = iota((ROWS, ROWS), 0), iota((ROWS, ROWS), 1)
    by_slot_order = pick(column == (row & (N_DP - 1)) * ROWS_DEV + (row >> 5))
    to_slots = dot(by_slot_order, to_new_order(new_index[...]), ((1,), (1,))).astype(BF16)
    to_slots_out[...] = to_slots
    by_slot = dot(to_slots, hidden[...]).astype(BF16)

    @pl.when(ids[SECTION] == 0)
    def _():
        residual[...] = by_slot[:HALF_ROWS]

    @pl.when(ids[SECTION] == 1)
    def _():
        residual[...] = by_slot[HALF_ROWS:]


def first_kernel(ids, table, rows, weights, other, keys, values, payload, spread):
    count = jnp.int32(0)
    for s in range(ROWS_DEV):
        leaves = table[DEST + s] != ids[REPLICA]

        @pl.when(leaves)
        def _():
            base = pl.multiple_of(USED * N_DP + count * (PIECES * N_DP), N_DP)
            spread[pl.ds(base, CONTEXT), :] = keys[s].astype(F32)
            spread[pl.ds(base + CONTEXT, CONTEXT), :] = values[s].astype(F32)

        count = count + jnp.where(leaves, 1, 0)
    spread_squares(rows[...], spread)
    pl.when(ids[SECTION] == 0)(lambda: project(rows[...], weights, spread))
    pl.when(ids[SECTION] == 1)(lambda: project(rows[...], other, spread))
    for p in range(N_DP):
        payload[p] = spread[pl.ds(p, BLOCK, stride=N_DP), :].astype(BF16)


def pack_kernel(ids, keys, values, packed):
    other = (1 - ids[SECTION]) * TRIO
    for s in range(TRIO):
        packed[s * CONTEXT : (s + 1) * CONTEXT, :HEAD] = keys[other + s]
        packed[s * CONTEXT : (s + 1) * CONTEXT, HEAD:] = values[other + s]


def forward(route, received, payload, pieces, sorted_pieces):
    count = N_DP * MOVES
    for p in range(N_DP):
        pieces[pl.ds(p * MOVES * PIECES, MOVES * PIECES), :] = received[p, USED:, :].astype(F32)
    to_replica = pick(iota((count, count), 0) == route[...])
    for i in range(PIECES):
        part = pieces[pl.ds(i, count, stride=PIECES), :].astype(BF16)
        sorted_pieces[pl.ds(i, count, stride=PIECES), :] = dot(to_replica, part, ((0,), (0,)))
    for p in range(N_DP):
        payload[p, USED:, :] = sorted_pieces[
            pl.ds(p * MOVES * PIECES, MOVES * PIECES), :
        ].astype(BF16)


def attend_kernel(
    layer, ids, table, cosine, sine, received, keys, values, packed, *refs
):
    if layer == 0:
        route, _, payload, own, pieces, sorted_pieces = refs
        forward(route, received, payload, pieces, sorted_pieces)
    else:
        payload, own = refs
    section = ids[SECTION]

    def attend(all_keys, all_values):
        total = received[0, :USED, :].astype(F32)
        for p in range(1, N_DP):
            total = total + received[p, :USED, :].astype(F32)
        row = iota((USED, HEAD), 0)
        lane = iota((USED, HEAD), 1)
        slot = over_ten(row)
        part = row - slot * PARTS
        tail = TRIO * PARTS
        squares = total[tail : tail + 1] + total[tail + 1 : tail + 2]
        square = jnp.sum(jnp.where(lane == slot, squares, 0.0), axis=1, keepdims=True)
        projected = total * lax.rsqrt(square / MODEL + EPSILON)
        cos_rows = jnp.ones((USED, HEAD), F32)
        sin_rows = jnp.zeros((USED, HEAD), F32)
        for s in range(TRIO):
            turned = (slot == s) & (part <= GROUP)
            cos_rows = jnp.where(turned, cosine[pl.ds(section * TRIO + s, 1), :], cos_rows)
            sin_rows = jnp.where(turned, sine[pl.ds(section * TRIO + s, 1), :], sin_rows)
        vectors = (
            projected * cos_rows + pltpu.roll(projected, HEAD // 2, 1) * sin_rows
        ).astype(BF16)

        scale = HEAD ** (-0.5)
        scores = dot(vectors, all_keys, ((1,), (1,))) * scale
        among = dot(vectors, vectors, ((1,), (1,))) * scale
        wide = (USED, CACHE_ROWS)
        wide_slot = over_ten(iota(wide, 0))
        column = iota(wide, 1)
        live = column < 0
        for s in range(TRIO):
            live = live | (
                (wide_slot == s)
                & (column >= s * CONTEXT)
                & (column < s * CONTEXT + table[HELD_LEN + section * TRIO + s])
            )
        scores = jnp.where(live, scores, -1e30)
        small_slot = over_ten(iota((USED, USED), 0))
        small_column = iota((USED, USED), 1)
        own_score = jnp.sum(
            jnp.where(small_column == small_slot * PARTS + GROUP, among, 0.0), axis=1, keepdims=True
        )
        highest = jnp.maximum(jnp.max(scores, axis=1, keepdims=True), own_score)
        terms = jnp.exp(scores - highest)
        own_term = jnp.exp(own_score - highest)
        denominator = jnp.sum(terms, axis=1, keepdims=True) + own_term
        weights = (terms / denominator).astype(BF16)
        own_weights = jnp.where(
            small_column == small_slot * PARTS + GROUP + 1, own_term / denominator, 0.0
        ).astype(BF16)
        attended = (dot(weights, all_values) + dot(own_weights, vectors)).astype(BF16)

        out_row, in_row = iota((USED, USED), 0), iota((USED, USED), 1)
        out_slot = out_row >> 3
        order = pick((in_row == out_slot * PARTS + (out_row & 7)) & (out_slot < TRIO))
        block = dot(order, attended)
        own_row, own_in = iota((16, USED), 0), iota((16, USED), 1)
        own_slot = own_row & 7
        own_pick = pick(
            (own_in == own_slot * PARTS + GROUP + (own_row >> 3)) & (own_slot < TRIO)
        )
        own_pair = dot(own_pick, vectors)
        own[...] = own_pair.astype(BF16)
        block_out = block.astype(BF16)
        for p in range(N_DP):
            payload[p, :USED, :] = block_out
        for s in range(TRIO):
            with_own = jnp.where(row == TRIO * 8, own_pair[s : s + 1], block)
            with_own = jnp.where(row == TRIO * 8 + 1, own_pair[8 + s : 9 + s], with_own)
            payload[table[DEST + section * TRIO + s], :USED, :] = with_own.astype(BF16)

    @pl.when(section == layer)
    def _():
        first = layer * TRIO
        attend(
            keys[first : first + TRIO].reshape(CACHE_ROWS, HEAD),
            values[first : first + TRIO].reshape(CACHE_ROWS, HEAD),
        )

    @pl.when(section != layer)
    def _():
        attend(packed[:, :HEAD], packed[:, HEAD:])


def output_kernel(layer, ids, received, w_out, w_other, payload, wide, rows):
    for p in range(N_DP):
        wide[pl.ds(p * USED, USED), :] = received[p, :USED, :].astype(F32)
    for s in range(TRIO):
        for h in range(GROUP):
            rows[s * N_DP : (s + 1) * N_DP, h * HEAD : (h + 1) * HEAD] = wide[
                pl.ds(s * 8 + h, N_DP, stride=USED), :
            ].astype(BF16)

    def write(weight):
        product = dot(rows[...], weight[...]).astype(BF16)
        for t in range(N_TENSOR):
            payload[t] = product

    pl.when(ids[SECTION] == layer)(lambda: write(w_out))
    pl.when(ids[SECTION] != layer)(lambda: write(w_other))


def summed(received, residual):
    total = received[0].astype(F32)
    for t in range(1, N_TENSOR):
        total = total + received[t].astype(F32)
    return (residual[...].astype(F32) + total).astype(BF16)


def second_kernel(ids, received, residual, weights, other, payload, result, spread):
    rows = summed(received, residual)
    result[...] = rows
    spread_squares(rows, spread)
    pl.when(ids[SECTION] == 1)(lambda: project(rows, weights, spread))
    pl.when(ids[SECTION] == 0)(lambda: project(rows, other, spread))
    for p in range(N_DP):
        payload[p] = spread[pl.ds(p, USED, stride=N_DP), :].astype(BF16)


def last_kernel(ids, received, before, done, result, swapped):
    rows = summed(received, before)
    result[...] = rows

    @pl.when(ids[SECTION] == 0)
    def _():
        swapped[...] = rows

    @pl.when(ids[SECTION] == 1)
    def _():
        swapped[...] = before[...]


def order_kernel(ids, to_slots, first, second, received, out):
    def write(low, high):
        out[...] = (
            dot(to_slots[:HALF_ROWS, :], low[...], ((0,), (0,)))
            + dot(to_slots[HALF_ROWS:, :], high[...], ((0,), (0,)))
        ).astype(BF16)

    pl.when(ids[SECTION] == 0)(lambda: write(first, received))
    pl.when(ids[SECTION] == 1)(lambda: write(received, second))


def own_kernel(ids, table, gathered_0, gathered_1, own_0, own_1, mine, swapped):
    me, section = ids[REPLICA], ids[SECTION]
    row = iota((16, HEAD), 0)
    for layer, (gathered, own) in enumerate(((gathered_0, own_0), (gathered_1, own_1))):
        own_rows = own[...].astype(F32)
        total = jnp.zeros((16, HEAD), F32)
        for r in range(ROWS_DEV):
            source = table[SOURCE + r]
            anchor = over_six(source)
            held = source - anchor * ROWS_DEV
            slot = held - section * TRIO
            here = (slot >= 0) & (slot < TRIO)
            stays = jnp.where(here & (anchor == me), 1.0, 0.0)
            moves = jnp.where(here & (anchor != me), 1.0, 0.0)
            pair = gathered[anchor, USED - 16 : USED, :].astype(F32)
            kept_key = jnp.sum(jnp.where(row == slot, own_rows, 0.0), axis=0, keepdims=True)
            kept_value = jnp.sum(jnp.where(row == slot + 8, own_rows, 0.0), axis=0, keepdims=True)
            new_key = kept_key * stays + pair[8:9] * moves
            new_value = kept_value * stays + pair[9:10] * moves
            total = jnp.where(row == r, new_key, jnp.where(row == r + 8, new_value, total))
        total = total.astype(BF16)

        @pl.when(section == layer)
        def _():
            mine[...] = total

        @pl.when(section != layer)
        def _():
            swapped[...] = total


def cache_kernel(
    ids, table, keys, values, mine, received, gathered, key_out, value_out, done, pieces
):
    me = ids[REPLICA]
    position = iota((CONTEXT, HEAD), 0)
    own = mine[...].astype(F32) + received[...].astype(F32)
    done[...] = own[:8]
    for p in range(N_DP):
        pieces[pl.ds(p * MOVES * PIECES, MOVES * PIECES), :] = gathered[p, USED:, :].astype(F32)
    count = jnp.int32(0)
    for r in range(ROWS_DEV):
        source = table[SOURCE + r]
        anchor = over_six(source)
        written = position == table[NEW_LEN + r]
        moves = anchor != me

        def write(key_rows, value_rows):
            key_out[r] = jnp.where(written, own[r : r + 1], key_rows).astype(BF16)
            value_out[r] = jnp.where(written, own[r + 8 : r + 9], value_rows).astype(BF16)

        @pl.when(anchor == me)
        def _():
            held = source - anchor * ROWS_DEV
            write(keys[held].astype(F32), values[held].astype(F32))

        @pl.when(moves)
        def _():
            parts = [
                pieces[pl.ds(count * PIECES + i, N_DP, stride=MOVES * PIECES), :]
                for i in range(PIECES)
            ]
            write(jnp.concatenate(parts[:2], 0), jnp.concatenate(parts[2:], 0))

        count = count + jnp.where(moves, 1, 0)


def call(kernel, name, specs, out_shapes, operands, scratch=(), limit=8):
    spec_of = {"s": SMEM_SPEC, "v": VMEM_SPEC, "h": HBM_SPEC, "a": pl.BlockSpec(memory_space=pl.ANY)}
    return pl.pallas_call(
        kernel,
        out_shape=out_shapes,
        in_specs=[spec_of[letter] for letter in specs],
        out_specs=jax.tree.map(lambda _: VMEM_SPEC, out_shapes),
        scratch_shapes=list(scratch),
        compiler_params=pltpu.CompilerParams(vmem_limit_bytes=limit * 1024 * 1024),
        name=name,
    )(*operands)


def exchange(value, axis):
    return lax.all_to_all(value, axis, split_axis=0, concat_axis=0, tiled=True)


def swap(value):
    return lax.ppermute(value, "section", [(0, 1), (1, 0)])


def shape(*dims):
    return jax.ShapeDtypeStruct(dims, BF16)


def on_device(
    hidden_in,
    norm_gain,
    w_query,
    w_key,
    w_value,
    w_out,
    key_cache,
    value_cache,
    context_len,
    dest_replica,
    dest_slot,
):
    me = lax.axis_index("dp")
    section = lax.axis_index("section")
    ids = jnp.stack([section, me]).astype(jnp.int32)
    keys, values = key_cache[0], value_cache[0]
    new_index = (dest_replica * ROWS_DEV + dest_slot)[None, :]
    row = jnp.arange(ROWS, dtype=jnp.int32)
    entry = jnp.arange(4 * ROWS_DEV, dtype=jnp.int32)[:, None]
    kind = entry // ROWS_DEV
    wanted = me * ROWS_DEV + entry % ROWS_DEV
    found = jnp.where(kind < 2, row[None, :], new_index) == wanted
    chosen = jnp.where(
        kind == 0, dest_replica[None, :], jnp.where(kind == 3, row[None, :], context_len[None, :])
    )
    table = jnp.sum(jnp.where(found, chosen, 0), 1)

    half = HEAD // 2
    inverse_freq = ROPE_BASE ** (-(jnp.arange(half, dtype=F32) * (2.0 / HEAD)))
    held_len = jnp.concatenate([table[HELD_LEN : HELD_LEN + ROWS_DEV], jnp.zeros((2,), jnp.int32)])
    angles = held_len.astype(F32)[:, None] * jnp.concatenate([inverse_freq, inverse_freq])[None, :]
    cosine = jnp.cos(angles)
    sine = jnp.sin(angles) * jnp.where(jnp.arange(HEAD) < half, -1.0, 1.0)[None, :]

    weights = call(
        load_kernel,
        "load",
        "hhhh",
        shape(WIDTH + 16, ALL_PARTS),
        (w_query, w_key, w_value, norm_gain),
        [pltpu.VMEM((1, WIDTH), F32), pltpu.SemaphoreType.DMA((4,))],
        8,
    )
    other = swap(weights)
    residual, to_slots = call(
        prepare_kernel,
        "prepare",
        "svv",
        (shape(HALF_ROWS, WIDTH), shape(ROWS, ROWS)),
        (ids, new_index, hidden_in),
    )
    payload = call(
        first_kernel,
        "first",
        "ssvvvvv",
        shape(N_DP, BLOCK, HEAD),
        (ids, table, residual, weights, other, keys, values),
        [pltpu.VMEM((BLOCK * N_DP, HEAD), F32)],
    )
    first = exchange(payload, "dp")

    late_keys, late_values, late_out, late_replica, late_slot, _ = lax.optimization_barrier(
        (keys, values, w_out[0], dest_replica, dest_slot, payload)
    )
    packed = swap(
        call(pack_kernel, "pack", "svv", shape(CACHE_ROWS, WIDTH), (ids, late_keys, late_values))
    )
    out_other = swap(late_out)
    leaves = late_replica != row // ROWS_DEV
    before = (row[None, :] // ROWS_DEV == row[:, None] // ROWS_DEV) & (row[None, :] < row[:, None])
    rank = jnp.sum(jnp.where(before & leaves[None, :], 1, 0), 1)
    before = (late_replica[None, :] == late_replica[:, None]) & (
        late_slot[None, :] < late_slot[:, None]
    )
    place = jnp.sum(jnp.where(before & leaves[None, :], 1, 0), 1)
    arrival = jnp.where(leaves, late_replica * MOVES + place, -1)
    chosen = arrival[None, :] == jnp.arange(N_DP * MOVES, dtype=jnp.int32)[:, None]
    route = jnp.sum(jnp.where(chosen, (row // ROWS_DEV * MOVES + rank)[None, :], 0), 1)[None, :]

    def attend(layer, received, specs="", *more):
        return call(
            lambda *refs: attend_kernel(layer, *refs),
            "attend",
            "ssvvvvvv" + specs,
            (shape(N_DP, USED if layer else BLOCK, HEAD), shape(16, HEAD)),
            (ids, table, cosine, sine, received, keys, values, packed, *more),
            [] if layer else [pltpu.VMEM((N_DP * MOVES * PIECES, HEAD), F32)] * 2,
        )

    def output(layer, received):
        return call(
            lambda *refs: output_kernel(layer, *refs),
            "output",
            "svvv",
            shape(N_TENSOR, HALF_ROWS, WIDTH),
            (ids, received, w_out[0], out_other),
            [pltpu.VMEM((N_DP * USED, HEAD), F32), pltpu.VMEM((HALF_ROWS, GROUP * HEAD), BF16)],
        )

    payload, own_0 = attend(0, first, "va", route, out_other)
    second = exchange(payload, "dp")
    sums = exchange(output(0, second), "tensor")
    payload, result_0 = call(
        second_kernel,
        "second",
        "svvvv",
        (shape(N_DP, USED, HEAD), shape(HALF_ROWS, WIDTH)),
        (ids, sums, residual, weights, other),
        [pltpu.VMEM((USED * N_DP, HEAD), F32)],
    )
    third = exchange(payload, "dp")
    payload, own_1 = attend(1, third)
    fourth = exchange(payload, "dp")
    sums = exchange(output(1, fourth), "tensor")
    mine, swapped_own = call(
        own_kernel,
        "own",
        "ssvvvv",
        (shape(16, HEAD), shape(16, HEAD)),
        (ids, table, second, fourth, own_0, own_1),
    )
    key_out, value_out, done = call(
        cache_kernel,
        "caches",
        "ssvvvvv",
        (
            shape(ROWS_DEV, CONTEXT, HEAD),
            shape(ROWS_DEV, CONTEXT, HEAD),
            jax.ShapeDtypeStruct((8, HEAD), F32),
        ),
        (ids, table, keys, values, mine, swap(swapped_own), second),
        [pltpu.VMEM((N_DP * MOVES * PIECES, HEAD), F32)],
    )
    result_1, swapped = call(
        last_kernel,
        "last",
        "svva",
        (shape(HALF_ROWS, WIDTH), shape(HALF_ROWS, WIDTH)),
        (ids, sums, result_0, done),
    )
    layer_out = call(
        order_kernel,
        "order",
        "svvvv",
        shape(ROWS, WIDTH),
        (ids, to_slots, result_0, result_1, swap(swapped)),
    )
    return layer_out[None], key_out[None], value_out[None]


def solution(mesh):
    return jax.shard_map(
        on_device,
        mesh=mesh,
        in_specs=(
            P(None, "dp"),
            P("section", "dp"),
            P("section", "dp", "tensor"),
            P("section", "dp", "tensor"),
            P("section", "dp", "tensor"),
            P("section", "tensor", "dp"),
            P("section", "dp", None, "tensor"),
            P("section", "dp", None, "tensor"),
            P(),
            P(),
            P(),
        ),
        out_specs=(
            P("section", None, "dp"),
            P("section", "dp", None, "tensor"),
            P("section", "dp", None, "tensor"),
        ),
        check_vma=False,
    )
```

```python
import jax
import jax.numpy as jnp
from jax import lax
from jax.experimental import pallas as pl
from jax.experimental.pallas import tpu as pltpu
from jax.sharding import PartitionSpec as P

N_DP = 32
N_TENSOR = 8
ROWS_DEV = 6
ROWS = 192
TRIO = 3
HALF_ROWS = N_DP * TRIO
CONTEXT = 64
MOVES = 4
PIECES = 4
HEAD = 128
GROUP = 8
PARTS = GROUP + 2
USED = 32
BLOCK = USED + MOVES * PIECES
WIDTH = 256
MODEL = 8192
CACHE_ROWS = TRIO * CONTEXT
QUERY = GROUP * HEAD
ALL_PARTS = PARTS * HEAD
EPSILON = 1e-06
ROPE_BASE = 1000000.0
F32 = jnp.float32
BF16 = jnp.bfloat16

SECTION, REPLICA = 0, 1
DEST, HELD_LEN, NEW_LEN, SOURCE = 0, 6, 12, 18

SMEM_SPEC = pl.BlockSpec(memory_space=pltpu.SMEM)
VMEM_SPEC = pl.BlockSpec(memory_space=pltpu.VMEM)


def iota(shape, dim):
    return lax.broadcasted_iota(jnp.int32, shape, dim)


def pick(condition):
    return jnp.where(condition, 1.0, 0.0).astype(BF16)


def over_six(index):
    return (index * 171) >> 10


def over_ten(index):
    return (index * 205) >> 11


def dot(left, right, contract=((1,), (0,))):
    return lax.dot_general(left, right, (contract, ((), ())), preferred_element_type=F32)


def to_new_order(new_index):
    return pick(iota((ROWS, ROWS), 0) == new_index)


def project(rows, weights, spread):
    by_slot = rows.astype(F32)
    terms = weights[WIDTH:, QUERY:].astype(F32)
    gain = terms[0:1] + terms[1:2] + terms[2:3]
    scaled = (by_slot * gain).astype(BF16)
    for pair in range(PARTS // 2):
        product = dot(scaled, weights[:WIDTH, pair * 2 * HEAD : (pair + 1) * 2 * HEAD])
        for s in range(TRIO):
            for side in range(2):
                row = s * PARTS + 2 * pair + side
                spread[pl.ds(row * N_DP, N_DP), :] = product[
                    s * N_DP : (s + 1) * N_DP, side * HEAD : (side + 1) * HEAD
                ]


def spread_squares(rows, spread):
    by_slot = rows.astype(F32)
    square = jnp.sum(by_slot * by_slot, axis=1, keepdims=True)
    lane = iota((N_DP, HEAD), 1)
    squares = jnp.zeros((N_DP, HEAD), F32)
    for s in range(TRIO):
        squares = jnp.where(lane == s, square[s * N_DP : (s + 1) * N_DP], squares)
    high = squares.astype(BF16).astype(F32)
    row = TRIO * PARTS
    spread[pl.ds(row * N_DP, N_DP), :] = high
    spread[pl.ds((row + 1) * N_DP, N_DP), :] = squares - high


def load_kernel(query, rest, weights):
    weights[:WIDTH, :QUERY] = query[0]
    weights[WIDTH:, :QUERY] = jnp.zeros((16, QUERY), BF16)
    weights[:, QUERY:] = rest[...]


def prepare_kernel(ids, new_index, hidden, residual, to_slots_out):
    row, column = iota((ROWS, ROWS), 0), iota((ROWS, ROWS), 1)
    by_slot_order = pick(column == (row & (N_DP - 1)) * ROWS_DEV + (row >> 5))
    to_slots = dot(by_slot_order, to_new_order(new_index[...]), ((1,), (1,))).astype(BF16)
    to_slots_out[...] = to_slots
    by_slot = dot(to_slots, hidden[...]).astype(BF16)

    @pl.when(ids[SECTION] == 0)
    def _():
        residual[...] = by_slot[:HALF_ROWS]

    @pl.when(ids[SECTION] == 1)
    def _():
        residual[...] = by_slot[HALF_ROWS:]


def first_kernel(ids, table, rows, weights, other, keys, values, payload, spread):
    count = jnp.int32(0)
    for s in range(ROWS_DEV):
        leaves = table[DEST + s] != ids[REPLICA]

        @pl.when(leaves)
        def _():
            base = pl.multiple_of(USED * N_DP + count * (PIECES * N_DP), N_DP)
            spread[pl.ds(base, CONTEXT), :] = keys[s].astype(F32)
            spread[pl.ds(base + CONTEXT, CONTEXT), :] = values[s].astype(F32)

        count = count + jnp.where(leaves, 1, 0)
    spread_squares(rows[...], spread)
    pl.when(ids[SECTION] == 0)(lambda: project(rows[...], weights, spread))
    pl.when(ids[SECTION] == 1)(lambda: project(rows[...], other, spread))
    for p in range(N_DP):
        payload[p] = spread[pl.ds(p, BLOCK, stride=N_DP), :].astype(BF16)


def pack_kernel(ids, keys, values, packed):
    other = (1 - ids[SECTION]) * TRIO
    for s in range(TRIO):
        packed[s * CONTEXT : (s + 1) * CONTEXT, :HEAD] = keys[other + s]
        packed[s * CONTEXT : (s + 1) * CONTEXT, HEAD:] = values[other + s]


def forward(route, received, payload, pieces, sorted_pieces):
    count = N_DP * MOVES
    for p in range(N_DP):
        pieces[pl.ds(p * MOVES * PIECES, MOVES * PIECES), :] = received[p, USED:, :].astype(F32)
    to_replica = pick(iota((count, count), 0) == route[...])
    for i in range(PIECES):
        part = pieces[pl.ds(i, count, stride=PIECES), :].astype(BF16)
        sorted_pieces[pl.ds(i, count, stride=PIECES), :] = dot(to_replica, part, ((0,), (0,)))
    for p in range(N_DP):
        payload[p, USED:, :] = sorted_pieces[
            pl.ds(p * MOVES * PIECES, MOVES * PIECES), :
        ].astype(BF16)


def attend_kernel(
    layer, ids, table, cosine, sine, received, keys, values, packed, *refs
):
    if layer == 0:
        route, _, payload, own, pieces, sorted_pieces = refs
        forward(route, received, payload, pieces, sorted_pieces)
    else:
        payload, own = refs
    section = ids[SECTION]

    def attend(all_keys, all_values):
        total = received[0, :USED, :].astype(F32)
        for p in range(1, N_DP):
            total = total + received[p, :USED, :].astype(F32)
        row = iota((USED, HEAD), 0)
        lane = iota((USED, HEAD), 1)
        slot = over_ten(row)
        part = row - slot * PARTS
        tail = TRIO * PARTS
        squares = total[tail : tail + 1] + total[tail + 1 : tail + 2]
        square = jnp.sum(jnp.where(lane == slot, squares, 0.0), axis=1, keepdims=True)
        projected = total * lax.rsqrt(square / MODEL + EPSILON)
        cos_rows = jnp.ones((USED, HEAD), F32)
        sin_rows = jnp.zeros((USED, HEAD), F32)
        for s in range(TRIO):
            turned = (slot == s) & (part <= GROUP)
            cos_rows = jnp.where(turned, cosine[pl.ds(section * TRIO + s, 1), :], cos_rows)
            sin_rows = jnp.where(turned, sine[pl.ds(section * TRIO + s, 1), :], sin_rows)
        vectors = (
            projected * cos_rows + pltpu.roll(projected, HEAD // 2, 1) * sin_rows
        ).astype(BF16)

        scale = HEAD ** (-0.5)
        scores = dot(vectors, all_keys, ((1,), (1,))) * scale
        among = dot(vectors, vectors, ((1,), (1,))) * scale
        wide = (USED, CACHE_ROWS)
        wide_slot = over_ten(iota(wide, 0))
        column = iota(wide, 1)
        live = column < 0
        for s in range(TRIO):
            live = live | (
                (wide_slot == s)
                & (column >= s * CONTEXT)
                & (column < s * CONTEXT + table[HELD_LEN + section * TRIO + s])
            )
        scores = jnp.where(live, scores, -1e30)
        small_slot = over_ten(iota((USED, USED), 0))
        small_column = iota((USED, USED), 1)
        own_score = jnp.sum(
            jnp.where(small_column == small_slot * PARTS + GROUP, among, 0.0), axis=1, keepdims=True
        )
        highest = jnp.maximum(jnp.max(scores, axis=1, keepdims=True), own_score)
        terms = jnp.exp(scores - highest)
        own_term = jnp.exp(own_score - highest)
        denominator = jnp.sum(terms, axis=1, keepdims=True) + own_term
        weights = (terms / denominator).astype(BF16)
        own_weights = jnp.where(
            small_column == small_slot * PARTS + GROUP + 1, own_term / denominator, 0.0
        ).astype(BF16)
        attended = (dot(weights, all_values) + dot(own_weights, vectors)).astype(BF16)

        out_row, in_row = iota((USED, USED), 0), iota((USED, USED), 1)
        out_slot = out_row >> 3
        order = pick((in_row == out_slot * PARTS + (out_row & 7)) & (out_slot < TRIO))
        block = dot(order, attended)
        own_row, own_in = iota((16, USED), 0), iota((16, USED), 1)
        own_slot = own_row & 7
        own_pick = pick(
            (own_in == own_slot * PARTS + GROUP + (own_row >> 3)) & (own_slot < TRIO)
        )
        own_pair = dot(own_pick, vectors)
        own[...] = own_pair.astype(BF16)
        block_out = block.astype(BF16)
        for p in range(N_DP):
            payload[p, :USED, :] = block_out
        for s in range(TRIO):
            with_own = jnp.where(row == TRIO * 8, own_pair[s : s + 1], block)
            with_own = jnp.where(row == TRIO * 8 + 1, own_pair[8 + s : 9 + s], with_own)
            payload[table[DEST + section * TRIO + s], :USED, :] = with_own.astype(BF16)

    @pl.when(section == layer)
    def _():
        first = layer * TRIO
        attend(
            keys[first : first + TRIO].reshape(CACHE_ROWS, HEAD),
            values[first : first + TRIO].reshape(CACHE_ROWS, HEAD),
        )

    @pl.when(section != layer)
    def _():
        attend(packed[:, :HEAD], packed[:, HEAD:])


def output_kernel(layer, ids, received, w_out, w_other, payload, wide, rows):
    for p in range(N_DP):
        wide[pl.ds(p * USED, USED), :] = received[p, :USED, :].astype(F32)
    for s in range(TRIO):
        for h in range(GROUP):
            rows[s * N_DP : (s + 1) * N_DP, h * HEAD : (h + 1) * HEAD] = wide[
                pl.ds(s * 8 + h, N_DP, stride=USED), :
            ].astype(BF16)

    def write(weight):
        product = dot(rows[...], weight[...]).astype(BF16)
        for t in range(N_TENSOR):
            payload[t] = product

    pl.when(ids[SECTION] == layer)(lambda: write(w_out))
    pl.when(ids[SECTION] != layer)(lambda: write(w_other))


def summed(received, residual):
    total = received[0].astype(F32)
    for t in range(1, N_TENSOR):
        total = total + received[t].astype(F32)
    return (residual[...].astype(F32) + total).astype(BF16)


def second_kernel(ids, received, residual, weights, other, payload, result, spread):
    rows = summed(received, residual)
    result[...] = rows
    spread_squares(rows, spread)
    pl.when(ids[SECTION] == 1)(lambda: project(rows, weights, spread))
    pl.when(ids[SECTION] == 0)(lambda: project(rows, other, spread))
    for p in range(N_DP):
        payload[p] = spread[pl.ds(p, USED, stride=N_DP), :].astype(BF16)


def last_kernel(
    ids, table, received, before, gathered_0, gathered_1, own_0, own_1, result, mine, swapped
):
    rows = summed(received, before)
    result[...] = rows

    @pl.when(ids[SECTION] == 0)
    def _():
        swapped[:HALF_ROWS, :] = rows

    @pl.when(ids[SECTION] == 1)
    def _():
        swapped[:HALF_ROWS, :] = before[...]

    me, section = ids[REPLICA], ids[SECTION]
    row = iota((16, HEAD), 0)
    swapped[HALF_ROWS:, HEAD:] = jnp.zeros((16, WIDTH - HEAD), BF16)
    for layer, (gathered, own) in enumerate(((gathered_0, own_0), (gathered_1, own_1))):
        own_rows = own[...].astype(F32)
        total = jnp.zeros((16, HEAD), F32)
        for r in range(ROWS_DEV):
            source = table[SOURCE + r]
            anchor = over_six(source)
            held = source - anchor * ROWS_DEV
            slot = held - section * TRIO
            here = (slot >= 0) & (slot < TRIO)
            stays = jnp.where(here & (anchor == me), 1.0, 0.0)
            moves = jnp.where(here & (anchor != me), 1.0, 0.0)
            pair = gathered[anchor, USED - 16 : USED, :].astype(F32)
            kept_key = jnp.sum(jnp.where(row == slot, own_rows, 0.0), axis=0, keepdims=True)
            kept_value = jnp.sum(jnp.where(row == slot + 8, own_rows, 0.0), axis=0, keepdims=True)
            new_key = kept_key * stays + pair[8:9] * moves
            new_value = kept_value * stays + pair[9:10] * moves
            total = jnp.where(row == r, new_key, jnp.where(row == r + 8, new_value, total))
        total = total.astype(BF16)

        @pl.when(section == layer)
        def _():
            mine[...] = total

        @pl.when(section != layer)
        def _():
            swapped[HALF_ROWS:, :HEAD] = total


def final_kernel(
    ids, table, to_slots, first, second, received, keys, values, mine, gathered,
    out, key_out, value_out, pieces
):
    def write_rows(low, high):
        out[...] = (
            dot(to_slots[:HALF_ROWS, :], low, ((0,), (0,)))
            + dot(to_slots[HALF_ROWS:, :], high, ((0,), (0,)))
        ).astype(BF16)

    others = received[:HALF_ROWS, :]
    pl.when(ids[SECTION] == 0)(lambda: write_rows(first[...], others))
    pl.when(ids[SECTION] == 1)(lambda: write_rows(others, second[...]))

    me = ids[REPLICA]
    position = iota((CONTEXT, HEAD), 0)
    own = mine[...].astype(F32) + received[HALF_ROWS:, :HEAD].astype(F32)
    for p in range(N_DP):
        pieces[pl.ds(p * MOVES * PIECES, MOVES * PIECES), :] = gathered[p, USED:, :].astype(F32)
    count = jnp.int32(0)
    for r in range(ROWS_DEV):
        source = table[SOURCE + r]
        anchor = over_six(source)
        written = position == table[NEW_LEN + r]
        moves = anchor != me

        def write(key_rows, value_rows):
            key_out[r] = jnp.where(written, own[r : r + 1], key_rows).astype(BF16)
            value_out[r] = jnp.where(written, own[r + 8 : r + 9], value_rows).astype(BF16)

        @pl.when(anchor == me)
        def _():
            held = source - anchor * ROWS_DEV
            write(keys[held].astype(F32), values[held].astype(F32))

        @pl.when(moves)
        def _():
            parts = [
                pieces[pl.ds(count * PIECES + i, N_DP, stride=MOVES * PIECES), :]
                for i in range(PIECES)
            ]
            write(jnp.concatenate(parts[:2], 0), jnp.concatenate(parts[2:], 0))

        count = count + jnp.where(moves, 1, 0)


def call(kernel, name, specs, out_shapes, operands, scratch=()):
    spec_of = {"s": SMEM_SPEC, "v": VMEM_SPEC, "a": pl.BlockSpec(memory_space=pl.ANY)}
    return pl.pallas_call(
        kernel,
        out_shape=out_shapes,
        in_specs=[spec_of[letter] for letter in specs],
        out_specs=jax.tree.map(lambda _: VMEM_SPEC, out_shapes),
        scratch_shapes=list(scratch),
        compiler_params=pltpu.CompilerParams(vmem_limit_bytes=8 * 1024 * 1024),
        name=name,
    )(*operands)


def exchange(value, axis):
    return lax.all_to_all(value, axis, split_axis=0, concat_axis=0, tiled=True)


def swap(value):
    return lax.ppermute(value, "section", [(0, 1), (1, 0)])


def shape(*dims):
    return jax.ShapeDtypeStruct(dims, BF16)


def on_device(
    hidden_in,
    norm_gain,
    w_query,
    w_key,
    w_value,
    w_out,
    key_cache,
    value_cache,
    context_len,
    dest_replica,
    dest_slot,
):
    me = lax.axis_index("dp")
    section = lax.axis_index("section")
    ids = jnp.stack([section, me]).astype(jnp.int32)
    keys, values = key_cache[0], value_cache[0]
    new_index = (dest_replica * ROWS_DEV + dest_slot)[None, :]
    row = jnp.arange(ROWS, dtype=jnp.int32)
    entry = jnp.arange(4 * ROWS_DEV, dtype=jnp.int32)[:, None]
    kind = entry // ROWS_DEV
    wanted = me * ROWS_DEV + entry % ROWS_DEV
    found = jnp.where(kind < 2, row[None, :], new_index) == wanted
    chosen = jnp.where(
        kind == 0, dest_replica[None, :], jnp.where(kind == 3, row[None, :], context_len[None, :])
    )
    table = jnp.sum(jnp.where(found, chosen, 0), 1)

    half = HEAD // 2
    inverse_freq = ROPE_BASE ** (-(jnp.arange(half, dtype=F32) * (2.0 / HEAD)))
    held_len = jnp.concatenate([table[HELD_LEN : HELD_LEN + ROWS_DEV], jnp.zeros((2,), jnp.int32)])
    angles = held_len.astype(F32)[:, None] * jnp.concatenate([inverse_freq, inverse_freq])[None, :]
    cosine = jnp.cos(angles)
    sine = jnp.sin(angles) * jnp.where(jnp.arange(HEAD) < half, -1.0, 1.0)[None, :]

    high = norm_gain.astype(BF16).astype(F32)
    middle = (norm_gain - high).astype(BF16).astype(F32)
    low = norm_gain - high - middle
    term = jnp.arange(16, dtype=jnp.int32)[:, None]
    terms = jnp.where(term == 0, high, jnp.where(term == 1, middle, jnp.where(term == 2, low, 0.0)))
    rest = (
        jnp.pad(w_key[0], ((0, 16), (0, HEAD)))
        + jnp.pad(w_value[0], ((0, 16), (HEAD, 0)))
        + jnp.pad(terms.astype(BF16), ((WIDTH, 0), (0, 0)))
    )
    weights = call(load_kernel, "load", "vv", shape(WIDTH + 16, ALL_PARTS), (w_query, rest))
    other = swap(weights)
    residual, to_slots = call(
        prepare_kernel,
        "prepare",
        "svv",
        (shape(HALF_ROWS, WIDTH), shape(ROWS, ROWS)),
        (ids, new_index, hidden_in),
    )
    payload = call(
        first_kernel,
        "first",
        "ssvvvvv",
        shape(N_DP, BLOCK, HEAD),
        (ids, table, residual, weights, other, keys, values),
        [pltpu.VMEM((BLOCK * N_DP, HEAD), F32)],
    )
    first = exchange(payload, "dp")

    late_keys, late_values, late_out, late_replica, late_slot, _ = lax.optimization_barrier(
        (keys, values, w_out[0], dest_replica, dest_slot, payload)
    )
    packed = swap(
        call(pack_kernel, "pack", "svv", shape(CACHE_ROWS, WIDTH), (ids, late_keys, late_values))
    )
    out_other = swap(late_out)
    leaves = late_replica != row // ROWS_DEV
    before = (row[None, :] // ROWS_DEV == row[:, None] // ROWS_DEV) & (row[None, :] < row[:, None])
    rank = jnp.sum(jnp.where(before & leaves[None, :], 1, 0), 1)
    before = (late_replica[None, :] == late_replica[:, None]) & (
        late_slot[None, :] < late_slot[:, None]
    )
    place = jnp.sum(jnp.where(before & leaves[None, :], 1, 0), 1)
    arrival = jnp.where(leaves, late_replica * MOVES + place, -1)
    chosen = arrival[None, :] == jnp.arange(N_DP * MOVES, dtype=jnp.int32)[:, None]
    route = jnp.sum(jnp.where(chosen, (row // ROWS_DEV * MOVES + rank)[None, :], 0), 1)[None, :]

    def attend(layer, received, specs="", *more):
        return call(
            lambda *refs: attend_kernel(layer, *refs),
            "attend",
            "ssvvvvvv" + specs,
            (shape(N_DP, USED if layer else BLOCK, HEAD), shape(16, HEAD)),
            (ids, table, cosine, sine, received, keys, values, packed, *more),
            [] if layer else [pltpu.VMEM((N_DP * MOVES * PIECES, HEAD), F32)] * 2,
        )

    def output(layer, received):
        return call(
            lambda *refs: output_kernel(layer, *refs),
            "output",
            "svvv",
            shape(N_TENSOR, HALF_ROWS, WIDTH),
            (ids, received, w_out[0], out_other),
            [pltpu.VMEM((N_DP * USED, HEAD), F32), pltpu.VMEM((HALF_ROWS, GROUP * HEAD), BF16)],
        )

    payload, own_0 = attend(0, first, "va", route, out_other)
    second = exchange(payload, "dp")
    sums = exchange(output(0, second), "tensor")
    payload, result_0 = call(
        second_kernel,
        "second",
        "svvvv",
        (shape(N_DP, USED, HEAD), shape(HALF_ROWS, WIDTH)),
        (ids, sums, residual, weights, other),
        [pltpu.VMEM((USED * N_DP, HEAD), F32)],
    )
    third = exchange(payload, "dp")
    payload, own_1 = attend(1, third)
    fourth = exchange(payload, "dp")
    sums = exchange(output(1, fourth), "tensor")
    result_1, mine, swapped = call(
        last_kernel,
        "last",
        "ssvvvvvv",
        (shape(HALF_ROWS, WIDTH), shape(16, HEAD), shape(HALF_ROWS + 16, WIDTH)),
        (ids, table, sums, result_0, second, fourth, own_0, own_1),
    )
    layer_out, key_out, value_out = call(
        final_kernel,
        "final",
        "ssvvvvvvvv",
        (shape(ROWS, WIDTH), shape(ROWS_DEV, CONTEXT, HEAD), shape(ROWS_DEV, CONTEXT, HEAD)),
        (ids, table, to_slots, result_0, result_1, swap(swapped), keys, values, mine, second),
        [pltpu.VMEM((N_DP * MOVES * PIECES, HEAD), F32)],
    )
    return layer_out[None], key_out[None], value_out[None]


def solution(mesh):
    return jax.shard_map(
        on_device,
        mesh=mesh,
        in_specs=(
            P(None, "dp"),
            P("section", "dp"),
            P("section", "dp", "tensor"),
            P("section", "dp", "tensor"),
            P("section", "dp", "tensor"),
            P("section", "tensor", "dp"),
            P("section", "dp", None, "tensor"),
            P("section", "dp", None, "tensor"),
            P(),
            P(),
            P(),
        ),
        out_specs=(
            P("section", None, "dp"),
            P("section", "dp", None, "tensor"),
            P("section", "dp", None, "tensor"),
        ),
        check_vma=False,
    )
```

```python
import jax
import jax.numpy as jnp
from jax import lax
from jax.experimental import pallas as pl
from jax.experimental.pallas import tpu as pltpu
from jax.sharding import PartitionSpec as P

N_DP = 32
N_TENSOR = 8
ROWS_DEV = 6
ROWS = 192
TRIO = 3
HALF_ROWS = N_DP * TRIO
CONTEXT = 64
MOVES = 4
PIECES = 4
HEAD = 128
GROUP = 8
PARTS = GROUP + 2
USED = 32
BLOCK = USED + MOVES * PIECES
TILE = 8
TILES = 3 * TILE
WIDTH = 256
MODEL = 8192
CACHE_ROWS = TRIO * CONTEXT
QUERY = GROUP * HEAD
ALL_PARTS = PARTS * HEAD
EPSILON = 1e-06
ROPE_BASE = 1000000.0
F32 = jnp.float32
BF16 = jnp.bfloat16

SECTION, REPLICA = 0, 1
DEST, HELD_LEN, NEW_LEN, SOURCE = 0, 6, 12, 18

SMEM_SPEC = pl.BlockSpec(memory_space=pltpu.SMEM)
VMEM_SPEC = pl.BlockSpec(memory_space=pltpu.VMEM)


def iota(shape, dim):
    return lax.broadcasted_iota(jnp.int32, shape, dim)


def pick(condition):
    return jnp.where(condition, 1.0, 0.0).astype(BF16)


def over_six(index):
    return (index * 171) >> 10


def over_ten(index):
    return (index * 205) >> 11


def dot(left, right, contract=((1,), (0,))):
    return lax.dot_general(left, right, (contract, ((), ())), preferred_element_type=F32)


def to_new_order(new_index):
    return pick(iota((ROWS, ROWS), 0) == new_index)


def project(rows, weights, spread):
    by_slot = rows.astype(F32)
    terms = weights[WIDTH:, QUERY:].astype(F32)
    gain = terms[0:1] + terms[1:2] + terms[2:3]
    scaled = (by_slot * gain).astype(BF16)
    for pair in range(PARTS // 2):
        product = dot(scaled, weights[:WIDTH, pair * 2 * HEAD : (pair + 1) * 2 * HEAD])
        for s in range(TRIO):
            for side in range(2):
                row = s * PARTS + 2 * pair + side
                spread[pl.ds(row * N_DP, N_DP), :] = product[
                    s * N_DP : (s + 1) * N_DP, side * HEAD : (side + 1) * HEAD
                ]


def spread_squares(rows, spread):
    by_slot = rows.astype(F32)
    square = jnp.sum(by_slot * by_slot, axis=1, keepdims=True)
    lane = iota((N_DP, HEAD), 1)
    squares = jnp.zeros((N_DP, HEAD), F32)
    for s in range(TRIO):
        squares = jnp.where(lane == s, square[s * N_DP : (s + 1) * N_DP], squares)
    high = squares.astype(BF16).astype(F32)
    row = TRIO * PARTS
    spread[pl.ds(row * N_DP, N_DP), :] = high
    spread[pl.ds((row + 1) * N_DP, N_DP), :] = squares - high


def load_kernel(query, rest, weights):
    weights[:WIDTH, :QUERY] = query[0]
    weights[WIDTH:, :QUERY] = jnp.zeros((16, QUERY), BF16)
    weights[:, QUERY:] = rest[...]


def prepare_kernel(ids, new_index, hidden, residual, to_slots_out):
    row, column = iota((ROWS, ROWS), 0), iota((ROWS, ROWS), 1)
    by_slot_order = pick(column == (row & (N_DP - 1)) * ROWS_DEV + (row >> 5))
    to_slots = dot(by_slot_order, to_new_order(new_index[...]), ((1,), (1,))).astype(BF16)
    to_slots_out[...] = to_slots
    by_slot = dot(to_slots, hidden[...]).astype(BF16)

    @pl.when(ids[SECTION] == 0)
    def _():
        residual[...] = by_slot[:HALF_ROWS]

    @pl.when(ids[SECTION] == 1)
    def _():
        residual[...] = by_slot[HALF_ROWS:]


def first_kernel(ids, table, rows, weights, other, keys, values, payload, spread):
    count = jnp.int32(0)
    for s in range(ROWS_DEV):
        leaves = table[DEST + s] != ids[REPLICA]

        @pl.when(leaves)
        def _():
            base = pl.multiple_of(USED * N_DP + count * (PIECES * N_DP), N_DP)
            spread[pl.ds(base, CONTEXT), :] = keys[s].astype(F32)
            spread[pl.ds(base + CONTEXT, CONTEXT), :] = values[s].astype(F32)

        count = count + jnp.where(leaves, 1, 0)
    spread_squares(rows[...], spread)
    pl.when(ids[SECTION] == 0)(lambda: project(rows[...], weights, spread))
    pl.when(ids[SECTION] == 1)(lambda: project(rows[...], other, spread))
    for p in range(N_DP):
        payload[p] = spread[pl.ds(p, BLOCK, stride=N_DP), :].astype(BF16)


def pack_kernel(ids, keys, values, packed):
    other = (1 - ids[SECTION]) * TRIO
    for s in range(TRIO):
        packed[s * CONTEXT : (s + 1) * CONTEXT, :HEAD] = keys[other + s]
        packed[s * CONTEXT : (s + 1) * CONTEXT, HEAD:] = values[other + s]


def tile_row(piece):
    return piece + jnp.where(piece < 14, 2, 4)


def forward(route, received, pieces, tiles):
    count = N_DP * MOVES
    for p in range(N_DP):
        pieces[pl.ds(p * MOVES * PIECES, MOVES * PIECES), :] = received[p, USED:, :].astype(F32)
        tiles[pl.ds(p * TILES, TILE), :] = jnp.zeros((TILE, HEAD), F32)
        tiles[pl.ds(p * TILES + 2 * TILE, TILE), :] = jnp.zeros((TILE, HEAD), F32)
    to_replica = pick(iota((count, count), 0) == route[...])
    for i in range(PIECES):
        part = pieces[pl.ds(i, count, stride=PIECES), :].astype(BF16)
        sorted_part = dot(to_replica, part, ((0,), (0,)))
        for m in range(MOVES):
            piece = m * PIECES + i
            row = piece + (2 if piece < 14 else 4)
            tiles[pl.ds(row, N_DP, stride=TILES), :] = sorted_part[m * N_DP : (m + 1) * N_DP]


def attend_kernel(
    layer, ids, table, cosine, sine, received, keys, values, packed, *refs
):
    if layer == 0:
        route, _, payload, own, later, pieces, tiles = refs
        forward(route, received, pieces, tiles)
        for p in range(N_DP):
            later[p] = tiles[pl.ds(p * TILES + TILE, 2 * TILE), :].astype(BF16)
    else:
        later, payload, own, tiles = refs
        for p in range(N_DP):
            tiles[pl.ds(p * TILE, TILE), :] = later[p].astype(F32)[TILE:]
    section = ids[SECTION]

    def attend(all_keys, all_values):
        total = received[0, :USED, :].astype(F32)
        for p in range(1, N_DP):
            total = total + received[p, :USED, :].astype(F32)
        row = iota((USED, HEAD), 0)
        lane = iota((USED, HEAD), 1)
        slot = over_ten(row)
        part = row - slot * PARTS
        tail = TRIO * PARTS
        squares = total[tail : tail + 1] + total[tail + 1 : tail + 2]
        square = jnp.sum(jnp.where(lane == slot, squares, 0.0), axis=1, keepdims=True)
        projected = total * lax.rsqrt(square / MODEL + EPSILON)
        cos_rows = jnp.ones((USED, HEAD), F32)
        sin_rows = jnp.zeros((USED, HEAD), F32)
        for s in range(TRIO):
            turned = (slot == s) & (part <= GROUP)
            cos_rows = jnp.where(turned, cosine[pl.ds(section * TRIO + s, 1), :], cos_rows)
            sin_rows = jnp.where(turned, sine[pl.ds(section * TRIO + s, 1), :], sin_rows)
        vectors = (
            projected * cos_rows + pltpu.roll(projected, HEAD // 2, 1) * sin_rows
        ).astype(BF16)

        scale = HEAD ** (-0.5)
        scores = dot(vectors, all_keys, ((1,), (1,))) * scale
        among = dot(vectors, vectors, ((1,), (1,))) * scale
        wide = (USED, CACHE_ROWS)
        wide_slot = over_ten(iota(wide, 0))
        column = iota(wide, 1)
        live = column < 0
        for s in range(TRIO):
            live = live | (
                (wide_slot == s)
                & (column >= s * CONTEXT)
                & (column < s * CONTEXT + table[HELD_LEN + section * TRIO + s])
            )
        scores = jnp.where(live, scores, -1e30)
        small_slot = over_ten(iota((USED, USED), 0))
        small_column = iota((USED, USED), 1)
        own_score = jnp.sum(
            jnp.where(small_column == small_slot * PARTS + GROUP, among, 0.0), axis=1, keepdims=True
        )
        highest = jnp.maximum(jnp.max(scores, axis=1, keepdims=True), own_score)
        terms = jnp.exp(scores - highest)
        own_term = jnp.exp(own_score - highest)
        denominator = jnp.sum(terms, axis=1, keepdims=True) + own_term
        weights = (terms / denominator).astype(BF16)
        own_weights = jnp.where(
            small_column == small_slot * PARTS + GROUP + 1, own_term / denominator, 0.0
        ).astype(BF16)
        attended = (dot(weights, all_values) + dot(own_weights, vectors)).astype(BF16)

        out_row, in_row = iota((USED, USED), 0), iota((USED, USED), 1)
        out_slot = out_row >> 3
        order = pick((in_row == out_slot * PARTS + (out_row & 7)) & (out_slot < TRIO))
        block = dot(order, attended)
        own_row, own_in = iota((16, USED), 0), iota((16, USED), 1)
        own_slot = own_row & 7
        own_pick = pick(
            (own_in == own_slot * PARTS + GROUP + (own_row >> 3)) & (own_slot < TRIO)
        )
        own_pair = dot(own_pick, vectors)
        own[...] = own_pair.astype(BF16)
        stride = TILES if layer == 0 else TILE
        for s in range(TRIO):
            first = table[DEST + section * TRIO + s] * stride
            tiles[pl.ds(first, 1), :] = own_pair[s : s + 1]
            tiles[pl.ds(first + 1, 1), :] = own_pair[8 + s : 9 + s]
        low, high = block[:16].astype(BF16), block[16 : 16 + TILE]
        for p in range(N_DP):
            payload[p, :16, :] = low
            payload[p, 16:, :] = jnp.concatenate(
                [high, tiles[pl.ds(p * stride, TILE), :]], 0
            ).astype(BF16)

    @pl.when(section == layer)
    def _():
        first = layer * TRIO
        attend(
            keys[first : first + TRIO].reshape(CACHE_ROWS, HEAD),
            values[first : first + TRIO].reshape(CACHE_ROWS, HEAD),
        )

    @pl.when(section != layer)
    def _():
        attend(packed[:, :HEAD], packed[:, HEAD:])


def output_kernel(layer, ids, received, w_out, w_other, payload, wide, rows):
    for p in range(N_DP):
        wide[pl.ds(p * USED, USED), :] = received[p, :USED, :].astype(F32)
    for s in range(TRIO):
        for h in range(GROUP):
            rows[s * N_DP : (s + 1) * N_DP, h * HEAD : (h + 1) * HEAD] = wide[
                pl.ds(s * 8 + h, N_DP, stride=USED), :
            ].astype(BF16)

    def write(weight):
        product = dot(rows[...], weight[...]).astype(BF16)
        for t in range(N_TENSOR):
            payload[t] = product

    pl.when(ids[SECTION] == layer)(lambda: write(w_out))
    pl.when(ids[SECTION] != layer)(lambda: write(w_other))


def summed(received, residual):
    total = received[0].astype(F32)
    for t in range(1, N_TENSOR):
        total = total + received[t].astype(F32)
    return (residual[...].astype(F32) + total).astype(BF16)


def second_kernel(ids, received, residual, weights, other, later, payload, result, spread):
    rows = summed(received, residual)
    result[...] = rows
    spread_squares(rows, spread)
    pl.when(ids[SECTION] == 1)(lambda: project(rows, weights, spread))
    pl.when(ids[SECTION] == 0)(lambda: project(rows, other, spread))
    for p in range(N_DP):
        payload[p, :USED, :] = spread[pl.ds(p, USED, stride=N_DP), :].astype(BF16)
        payload[p, USED:, :] = later[p].astype(F32)[:TILE].astype(BF16)


def last_kernel(
    ids, table, received, before, gathered_0, gathered_1, own_0, own_1, result, mine, swapped
):
    rows = summed(received, before)
    result[...] = rows

    @pl.when(ids[SECTION] == 0)
    def _():
        swapped[:HALF_ROWS, :] = rows

    @pl.when(ids[SECTION] == 1)
    def _():
        swapped[:HALF_ROWS, :] = before[...]

    me, section = ids[REPLICA], ids[SECTION]
    row = iota((16, HEAD), 0)
    swapped[HALF_ROWS:, HEAD:] = jnp.zeros((16, WIDTH - HEAD), BF16)
    for layer, (gathered, own) in enumerate(((gathered_0, own_0), (gathered_1, own_1))):
        own_rows = own[...].astype(F32)
        total = jnp.zeros((16, HEAD), F32)
        for r in range(ROWS_DEV):
            source = table[SOURCE + r]
            anchor = over_six(source)
            held = source - anchor * ROWS_DEV
            slot = held - section * TRIO
            here = (slot >= 0) & (slot < TRIO)
            stays = here & (anchor == me)
            moves = here & (anchor != me)
            pair = gathered[anchor, USED - 16 : USED, :].astype(F32)
            kept_key = jnp.sum(jnp.where(row == slot, own_rows, 0.0), axis=0, keepdims=True)
            kept_value = jnp.sum(jnp.where(row == slot + 8, own_rows, 0.0), axis=0, keepdims=True)
            new_key = jnp.where(stays, kept_key, jnp.where(moves, pair[8:9], 0.0))
            new_value = jnp.where(stays, kept_value, jnp.where(moves, pair[9:10], 0.0))
            total = jnp.where(row == r, new_key, jnp.where(row == r + 8, new_value, total))
        total = total.astype(BF16)

        @pl.when(section == layer)
        def _():
            mine[...] = total

        @pl.when(section != layer)
        def _():
            swapped[HALF_ROWS:, :HEAD] = total


def final_kernel(
    ids, table, to_slots, first, second, received, keys, values, mine, second_in, third_in, fourth_in,
    out, key_out, value_out, pieces
):
    def write_rows(low, high):
        out[...] = (
            dot(to_slots[:HALF_ROWS, :], low, ((0,), (0,)))
            + dot(to_slots[HALF_ROWS:, :], high, ((0,), (0,)))
        ).astype(BF16)

    others = received[:HALF_ROWS, :]
    pl.when(ids[SECTION] == 0)(lambda: write_rows(first[...], others))
    pl.when(ids[SECTION] == 1)(lambda: write_rows(others, second[...]))

    me = ids[REPLICA]
    position = iota((CONTEXT, HEAD), 0)
    own = mine[...].astype(F32) + received[HALF_ROWS:, :HEAD].astype(F32)
    for p in range(N_DP):
        for i, (gathered, first_row) in enumerate(
            ((second_in, USED - 16), (third_in, USED - TILE), (fourth_in, USED - 16))
        ):
            pieces[pl.ds(p * TILES + i * TILE, TILE), :] = gathered[
                p, first_row : first_row + 16, :
            ].astype(F32)[TILE:]
    count = jnp.int32(0)
    for r in range(ROWS_DEV):
        source = table[SOURCE + r]
        anchor = over_six(source)
        written = position == table[NEW_LEN + r]
        moves = anchor != me

        def write(key_rows, value_rows):
            key_out[r] = jnp.where(written, own[r : r + 1], key_rows).astype(BF16)
            value_out[r] = jnp.where(written, own[r + 8 : r + 9], value_rows).astype(BF16)

        @pl.when(anchor == me)
        def _():
            held = source - anchor * ROWS_DEV
            write(keys[held].astype(F32), values[held].astype(F32))

        @pl.when(moves)
        def _():
            parts = [
                pieces[pl.ds(tile_row(count * PIECES + i), N_DP, stride=TILES), :]
                for i in range(PIECES)
            ]
            write(jnp.concatenate(parts[:2], 0), jnp.concatenate(parts[2:], 0))

        count = count + jnp.where(moves, 1, 0)


def call(kernel, name, specs, out_shapes, operands, scratch=()):
    spec_of = {"s": SMEM_SPEC, "v": VMEM_SPEC, "a": pl.BlockSpec(memory_space=pl.ANY)}
    return pl.pallas_call(
        kernel,
        out_shape=out_shapes,
        in_specs=[spec_of[letter] for letter in specs],
        out_specs=jax.tree.map(lambda _: VMEM_SPEC, out_shapes),
        scratch_shapes=list(scratch),
        compiler_params=pltpu.CompilerParams(vmem_limit_bytes=8 * 1024 * 1024),
        name=name,
    )(*operands)


def exchange(value, axis):
    return lax.all_to_all(value, axis, split_axis=0, concat_axis=0, tiled=True)


def swap(value):
    return lax.ppermute(value, "section", [(0, 1), (1, 0)])


def shape(*dims):
    return jax.ShapeDtypeStruct(dims, BF16)


def on_device(
    hidden_in,
    norm_gain,
    w_query,
    w_key,
    w_value,
    w_out,
    key_cache,
    value_cache,
    context_len,
    dest_replica,
    dest_slot,
):
    me = lax.axis_index("dp")
    section = lax.axis_index("section")
    ids = jnp.stack([section, me]).astype(jnp.int32)
    keys, values = key_cache[0], value_cache[0]
    new_index = (dest_replica * ROWS_DEV + dest_slot)[None, :]
    row = jnp.arange(ROWS, dtype=jnp.int32)
    entry = jnp.arange(4 * ROWS_DEV, dtype=jnp.int32)[:, None]
    kind = entry // ROWS_DEV
    wanted = me * ROWS_DEV + entry % ROWS_DEV
    found = jnp.where(kind < 2, row[None, :], new_index) == wanted
    chosen = jnp.where(
        kind == 0, dest_replica[None, :], jnp.where(kind == 3, row[None, :], context_len[None, :])
    )
    table = jnp.sum(jnp.where(found, chosen, 0), 1)

    half = HEAD // 2
    inverse_freq = ROPE_BASE ** (-(jnp.arange(half, dtype=F32) * (2.0 / HEAD)))
    held_len = jnp.concatenate([table[HELD_LEN : HELD_LEN + ROWS_DEV], jnp.zeros((2,), jnp.int32)])
    angles = held_len.astype(F32)[:, None] * jnp.concatenate([inverse_freq, inverse_freq])[None, :]
    cosine = jnp.cos(angles)
    sine = jnp.sin(angles) * jnp.where(jnp.arange(HEAD) < half, -1.0, 1.0)[None, :]

    high = lax.reduce_precision(norm_gain, 8, 7)
    middle = lax.reduce_precision(norm_gain - high, 8, 7)
    low = norm_gain - high - middle
    term = jnp.arange(16, dtype=jnp.int32)[:, None]
    terms = jnp.where(term == 0, high, jnp.where(term == 1, middle, jnp.where(term == 2, low, 0.0)))
    rest = (
        jnp.pad(w_key[0], ((0, 16), (0, HEAD)))
        + jnp.pad(w_value[0], ((0, 16), (HEAD, 0)))
        + jnp.pad(terms.astype(BF16), ((WIDTH, 0), (0, 0)))
    )
    weights = call(load_kernel, "load", "vv", shape(WIDTH + 16, ALL_PARTS), (w_query, rest))
    other = swap(weights)
    residual, to_slots = call(
        prepare_kernel,
        "prepare",
        "svv",
        (shape(HALF_ROWS, WIDTH), shape(ROWS, ROWS)),
        (ids, new_index, hidden_in),
    )
    payload = call(
        first_kernel,
        "first",
        "ssvvvvv",
        shape(N_DP, BLOCK, HEAD),
        (ids, table, residual, weights, other, keys, values),
        [pltpu.VMEM((BLOCK * N_DP, HEAD), F32)],
    )
    first = exchange(payload, "dp")

    late_keys, late_values, late_out, late_replica, late_slot, _ = lax.optimization_barrier(
        (keys, values, w_out[0], dest_replica, dest_slot, payload)
    )
    packed = swap(
        call(pack_kernel, "pack", "svv", shape(CACHE_ROWS, WIDTH), (ids, late_keys, late_values))
    )
    out_other = swap(late_out)
    leaves = late_replica != row // ROWS_DEV
    before = (row[None, :] // ROWS_DEV == row[:, None] // ROWS_DEV) & (row[None, :] < row[:, None])
    rank = jnp.sum(jnp.where(before & leaves[None, :], 1, 0), 1)
    before = (late_replica[None, :] == late_replica[:, None]) & (
        late_slot[None, :] < late_slot[:, None]
    )
    place = jnp.sum(jnp.where(before & leaves[None, :], 1, 0), 1)
    arrival = jnp.where(leaves, place * N_DP + late_replica, -1)
    chosen = arrival[None, :] == jnp.arange(N_DP * MOVES, dtype=jnp.int32)[:, None]
    route = jnp.sum(jnp.where(chosen, (row // ROWS_DEV * MOVES + rank)[None, :], 0), 1)[None, :]

    def attend(layer, received, specs="", *more):
        return call(
            lambda *refs: attend_kernel(layer, *refs),
            "attend",
            "ssvvvvvv" + specs,
            (shape(N_DP, USED, HEAD), shape(16, HEAD))
            + (() if layer else (shape(N_DP, 2 * TILE, HEAD),)),
            (ids, table, cosine, sine, received, keys, values, packed, *more),
            [pltpu.VMEM((N_DP * TILE, HEAD), F32)]
            if layer
            else [
                pltpu.VMEM((N_DP * MOVES * PIECES, HEAD), F32),
                pltpu.VMEM((N_DP * TILES, HEAD), F32),
            ],
        )

    def output(layer, received):
        return call(
            lambda *refs: output_kernel(layer, *refs),
            "output",
            "svvv",
            shape(N_TENSOR, HALF_ROWS, WIDTH),
            (ids, received, w_out[0], out_other),
            [pltpu.VMEM((N_DP * USED, HEAD), F32), pltpu.VMEM((HALF_ROWS, GROUP * HEAD), BF16)],
        )

    payload, own_0, later = attend(0, first, "va", route, out_other)
    second = exchange(payload, "dp")
    sums = exchange(output(0, second), "tensor")
    payload, result_0 = call(
        second_kernel,
        "second",
        "svvvvv",
        (shape(N_DP, USED + TILE, HEAD), shape(HALF_ROWS, WIDTH)),
        (ids, sums, residual, weights, other, later),
        [pltpu.VMEM((USED * N_DP, HEAD), F32)],
    )
    third = exchange(payload, "dp")
    payload, own_1 = attend(1, third, "v", later)
    fourth = exchange(payload, "dp")
    sums = exchange(output(1, fourth), "tensor")
    result_1, mine, swapped = call(
        last_kernel,
        "last",
        "ssvvvvvv",
        (shape(HALF_ROWS, WIDTH), shape(16, HEAD), shape(HALF_ROWS + 16, WIDTH)),
        (ids, table, sums, result_0, second, fourth, own_0, own_1),
    )
    layer_out, key_out, value_out = call(
        final_kernel,
        "final",
        "ssvvvvvvvvvv",
        (shape(ROWS, WIDTH), shape(ROWS_DEV, CONTEXT, HEAD), shape(ROWS_DEV, CONTEXT, HEAD)),
        (ids, table, to_slots, result_0, result_1, swap(swapped), keys, values, mine,
         second, third, fourth),
        [pltpu.VMEM((N_DP * TILES, HEAD), F32)],
    )
    return layer_out[None], key_out[None], value_out[None]


def solution(mesh):
    return jax.shard_map(
        on_device,
        mesh=mesh,
        in_specs=(
            P(None, "dp"),
            P("section", "dp"),
            P("section", "dp", "tensor"),
            P("section", "dp", "tensor"),
            P("section", "dp", "tensor"),
            P("section", "tensor", "dp"),
            P("section", "dp", None, "tensor"),
            P("section", "dp", None, "tensor"),
            P(),
            P(),
            P(),
        ),
        out_specs=(
            P("section", None, "dp"),
            P("section", "dp", None, "tensor"),
            P("section", "dp", None, "tensor"),
        ),
        check_vma=False,
    )
```

```python
import jax
import jax.numpy as jnp
from jax import lax
from jax.experimental import pallas as pl
from jax.experimental.pallas import tpu as pltpu
from jax.sharding import PartitionSpec as P

N_DP = 32
N_TENSOR = 8
ROWS_DEV = 6
ROWS = 192
TRIO = 3
HALF_ROWS = N_DP * TRIO
CONTEXT = 64
MOVES = 4
PIECES = 4
HEAD = 128
GROUP = 8
PARTS = GROUP + 2
USED = 32
BLOCK = USED + MOVES * PIECES
TILE = 8
TILES = 3 * TILE
WIDTH = 256
MODEL = 8192
CACHE_ROWS = TRIO * CONTEXT
QUERY = GROUP * HEAD
ALL_PARTS = PARTS * HEAD
PACKED = ALL_PARTS + 2 * HEAD
EPSILON = 1e-06
ROPE_BASE = 1000000.0
F32 = jnp.float32
BF16 = jnp.bfloat16

SECTION, REPLICA = 0, 1
DEST, HELD_LEN, NEW_LEN, SOURCE = 0, 6, 12, 18

SMEM_SPEC = pl.BlockSpec(memory_space=pltpu.SMEM)
VMEM_SPEC = pl.BlockSpec(memory_space=pltpu.VMEM)


def iota(shape, dim):
    return lax.broadcasted_iota(jnp.int32, shape, dim)


def pick(condition):
    return jnp.where(condition, 1.0, 0.0).astype(BF16)


def over_six(index):
    return (index * 171) >> 10


def over_ten(index):
    return (index * 205) >> 11


def dot(left, right, contract=((1,), (0,))):
    return lax.dot_general(left, right, (contract, ((), ())), preferred_element_type=F32)


def to_new_order(new_index):
    return pick(iota((ROWS, ROWS), 0) == new_index)


def project(rows, weights, spread):
    by_slot = rows.astype(F32)
    terms = weights[WIDTH:, QUERY:ALL_PARTS].astype(F32)
    gain = terms[0:1] + terms[1:2] + terms[2:3]
    scaled = (by_slot * gain).astype(BF16)
    for pair in range(PARTS // 2):
        product = dot(scaled, weights[:WIDTH, pair * 2 * HEAD : (pair + 1) * 2 * HEAD])
        for s in range(TRIO):
            for side in range(2):
                row = s * PARTS + 2 * pair + side
                spread[pl.ds(row * N_DP, N_DP), :] = product[
                    s * N_DP : (s + 1) * N_DP, side * HEAD : (side + 1) * HEAD
                ]


def spread_squares(rows, spread):
    by_slot = rows.astype(F32)
    square = jnp.sum(by_slot * by_slot, axis=1, keepdims=True)
    lane = iota((N_DP, HEAD), 1)
    squares = jnp.zeros((N_DP, HEAD), F32)
    for s in range(TRIO):
        squares = jnp.where(lane == s, square[s * N_DP : (s + 1) * N_DP], squares)
    high = squares.astype(BF16).astype(F32)
    row = TRIO * PARTS
    spread[pl.ds(row * N_DP, N_DP), :] = high
    spread[pl.ds((row + 1) * N_DP, N_DP), :] = squares - high


def load_kernel(query, rest, gain, weights):
    weights[:WIDTH, :QUERY] = query[0]
    weights[WIDTH:, :QUERY] = jnp.zeros((16, QUERY), BF16)
    weights[:WIDTH, QUERY:] = rest[...]
    high = gain[...].astype(BF16).astype(F32)
    middle = (gain[...] - high).astype(BF16).astype(F32)
    low = gain[...] - high - middle
    row = iota((16, WIDTH), 0)
    terms = jnp.where(row == 0, high, jnp.where(row == 1, middle, jnp.where(row == 2, low, 0.0)))
    weights[WIDTH:, QUERY:ALL_PARTS] = terms.astype(BF16)
    weights[WIDTH:, ALL_PARTS:] = jnp.zeros((16, 2 * HEAD), BF16)


def prepare_kernel(ids, new_index, hidden, residual, to_slots_out):
    row, column = iota((ROWS, ROWS), 0), iota((ROWS, ROWS), 1)
    by_slot_order = pick(column == (row & (N_DP - 1)) * ROWS_DEV + (row >> 5))
    to_slots = dot(by_slot_order, to_new_order(new_index[...]), ((1,), (1,))).astype(BF16)
    to_slots_out[...] = to_slots
    by_slot = dot(to_slots, hidden[...]).astype(BF16)

    @pl.when(ids[SECTION] == 0)
    def _():
        residual[...] = by_slot[:HALF_ROWS]

    @pl.when(ids[SECTION] == 1)
    def _():
        residual[...] = by_slot[HALF_ROWS:]


def first_kernel(ids, table, rows, weights, other, keys, values, payload, spread):
    count = jnp.int32(0)
    for s in range(ROWS_DEV):
        leaves = table[DEST + s] != ids[REPLICA]

        @pl.when(leaves)
        def _():
            base = pl.multiple_of(USED * N_DP + count * (PIECES * N_DP), N_DP)
            spread[pl.ds(base, CONTEXT), :] = keys[s].astype(F32)
            spread[pl.ds(base + CONTEXT, CONTEXT), :] = values[s].astype(F32)

        count = count + jnp.where(leaves, 1, 0)
    spread_squares(rows[...], spread)
    pl.when(ids[SECTION] == 0)(lambda: project(rows[...], weights, spread))
    pl.when(ids[SECTION] == 1)(lambda: project(rows[...], other, spread))
    for p in range(N_DP):
        payload[p] = spread[pl.ds(p, BLOCK, stride=N_DP), :].astype(BF16)


def tile_row(piece):
    return piece + jnp.where(piece < 14, 2, 4)


def forward(route, received, pieces, tiles):
    count = N_DP * MOVES
    for p in range(N_DP):
        pieces[pl.ds(p * MOVES * PIECES, MOVES * PIECES), :] = received[p, USED:, :].astype(F32)
        tiles[pl.ds(p * TILES, TILE), :] = jnp.zeros((TILE, HEAD), F32)
        tiles[pl.ds(p * TILES + 2 * TILE, TILE), :] = jnp.zeros((TILE, HEAD), F32)
    to_replica = pick(iota((count, count), 0) == route[...])
    for i in range(PIECES):
        part = pieces[pl.ds(i, count, stride=PIECES), :].astype(BF16)
        sorted_part = dot(to_replica, part, ((0,), (0,)))
        for m in range(MOVES):
            piece = m * PIECES + i
            row = piece + (2 if piece < 14 else 4)
            tiles[pl.ds(row, N_DP, stride=TILES), :] = sorted_part[m * N_DP : (m + 1) * N_DP]


def attend_kernel(
    layer, ids, table, cosine, sine, received, keys, values, other, *refs
):
    if layer == 0:
        route, _, payload, own, later, pieces, tiles = refs
        forward(route, received, pieces, tiles)
        for p in range(N_DP):
            later[p] = tiles[pl.ds(p * TILES + TILE, 2 * TILE), :].astype(BF16)
    else:
        later, payload, own, tiles = refs
        for p in range(N_DP):
            tiles[pl.ds(p * TILE, TILE), :] = later[p].astype(F32)[TILE:]
    section = ids[SECTION]

    def attend(all_keys, all_values):
        total = received[0, :USED, :].astype(F32)
        for p in range(1, N_DP):
            total = total + received[p, :USED, :].astype(F32)
        row = iota((USED, HEAD), 0)
        lane = iota((USED, HEAD), 1)
        slot = over_ten(row)
        part = row - slot * PARTS
        tail = TRIO * PARTS
        squares = total[tail : tail + 1] + total[tail + 1 : tail + 2]
        square = jnp.sum(jnp.where(lane == slot, squares, 0.0), axis=1, keepdims=True)
        projected = total * lax.rsqrt(square / MODEL + EPSILON)
        cos_rows = jnp.ones((USED, HEAD), F32)
        sin_rows = jnp.zeros((USED, HEAD), F32)
        for s in range(TRIO):
            turned = (slot == s) & (part <= GROUP)
            cos_rows = jnp.where(turned, cosine[pl.ds(section * TRIO + s, 1), :], cos_rows)
            sin_rows = jnp.where(turned, sine[pl.ds(section * TRIO + s, 1), :], sin_rows)
        vectors = (
            projected * cos_rows + pltpu.roll(projected, HEAD // 2, 1) * sin_rows
        ).astype(BF16)

        scale = HEAD ** (-0.5)
        scores = dot(vectors, all_keys, ((1,), (1,))) * scale
        among = dot(vectors, vectors, ((1,), (1,))) * scale
        wide = (USED, CACHE_ROWS)
        wide_slot = over_ten(iota(wide, 0))
        column = iota(wide, 1)
        live = column < 0
        for s in range(TRIO):
            live = live | (
                (wide_slot == s)
                & (column >= s * CONTEXT)
                & (column < s * CONTEXT + table[HELD_LEN + section * TRIO + s])
            )
        scores = jnp.where(live, scores, -1e30)
        small_slot = over_ten(iota((USED, USED), 0))
        small_column = iota((USED, USED), 1)
        own_score = jnp.sum(
            jnp.where(small_column == small_slot * PARTS + GROUP, among, 0.0), axis=1, keepdims=True
        )
        highest = jnp.maximum(jnp.max(scores, axis=1, keepdims=True), own_score)
        terms = jnp.exp(scores - highest)
        own_term = jnp.exp(own_score - highest)
        denominator = jnp.sum(terms, axis=1, keepdims=True) + own_term
        weights = (terms / denominator).astype(BF16)
        own_weights = jnp.where(
            small_column == small_slot * PARTS + GROUP + 1, own_term / denominator, 0.0
        ).astype(BF16)
        attended = (dot(weights, all_values) + dot(own_weights, vectors)).astype(BF16)

        out_row, in_row = iota((USED, USED), 0), iota((USED, USED), 1)
        out_slot = out_row >> 3
        order = pick((in_row == out_slot * PARTS + (out_row & 7)) & (out_slot < TRIO))
        block = dot(order, attended)
        own_row, own_in = iota((16, USED), 0), iota((16, USED), 1)
        own_slot = own_row & 7
        own_pick = pick(
            (own_in == own_slot * PARTS + GROUP + (own_row >> 3)) & (own_slot < TRIO)
        )
        own_pair = dot(own_pick, vectors)
        own[...] = own_pair.astype(BF16)
        stride = TILES if layer == 0 else TILE
        for s in range(TRIO):
            first = table[DEST + section * TRIO + s] * stride
            tiles[pl.ds(first, 1), :] = own_pair[s : s + 1]
            tiles[pl.ds(first + 1, 1), :] = own_pair[8 + s : 9 + s]
        low, high = block[:16].astype(BF16), block[16 : 16 + TILE]
        for p in range(N_DP):
            payload[p, :16, :] = low
            payload[p, 16:, :] = jnp.concatenate(
                [high, tiles[pl.ds(p * stride, TILE), :]], 0
            ).astype(BF16)

    @pl.when(section == layer)
    def _():
        first = layer * TRIO
        attend(
            keys[first : first + TRIO].reshape(CACHE_ROWS, HEAD),
            values[first : first + TRIO].reshape(CACHE_ROWS, HEAD),
        )

    @pl.when(section != layer)
    def _():
        attend(other[:CACHE_ROWS, ALL_PARTS : ALL_PARTS + HEAD], other[:CACHE_ROWS, ALL_PARTS + HEAD :])


def output_kernel(layer, ids, received, w_out, w_other, payload, wide, rows):
    for p in range(N_DP):
        wide[pl.ds(p * USED, USED), :] = received[p, :USED, :].astype(F32)
    for s in range(TRIO):
        for h in range(GROUP):
            rows[s * N_DP : (s + 1) * N_DP, h * HEAD : (h + 1) * HEAD] = wide[
                pl.ds(s * 8 + h, N_DP, stride=USED), :
            ].astype(BF16)

    def write(weight):
        product = dot(rows[...], weight[...]).astype(BF16)
        for t in range(N_TENSOR):
            payload[t] = product

    pl.when(ids[SECTION] == layer)(lambda: write(w_out))
    pl.when(ids[SECTION] != layer)(lambda: write(w_other))


def summed(received, residual):
    total = received[0].astype(F32)
    for t in range(1, N_TENSOR):
        total = total + received[t].astype(F32)
    return (residual[...].astype(F32) + total).astype(BF16)


def second_kernel(ids, received, residual, weights, other, later, payload, result, spread):
    rows = summed(received, residual)
    result[...] = rows
    spread_squares(rows, spread)
    pl.when(ids[SECTION] == 1)(lambda: project(rows, weights, spread))
    pl.when(ids[SECTION] == 0)(lambda: project(rows, other, spread))
    for p in range(N_DP):
        payload[p, :USED, :] = spread[pl.ds(p, USED, stride=N_DP), :].astype(BF16)
        payload[p, USED:, :] = later[p].astype(F32)[:TILE].astype(BF16)


def last_kernel(
    ids, table, received, before, gathered_0, gathered_1, own_0, own_1, result, mine, swapped
):
    rows = summed(received, before)
    result[...] = rows

    @pl.when(ids[SECTION] == 0)
    def _():
        swapped[:HALF_ROWS, :] = rows

    @pl.when(ids[SECTION] == 1)
    def _():
        swapped[:HALF_ROWS, :] = before[...]

    me, section = ids[REPLICA], ids[SECTION]
    row = iota((16, HEAD), 0)
    swapped[HALF_ROWS:, HEAD:] = jnp.zeros((16, WIDTH - HEAD), BF16)
    for layer, (gathered, own) in enumerate(((gathered_0, own_0), (gathered_1, own_1))):
        own_rows = own[...].astype(F32)
        total = jnp.zeros((16, HEAD), F32)
        for r in range(ROWS_DEV):
            source = table[SOURCE + r]
            anchor = over_six(source)
            held = source - anchor * ROWS_DEV
            slot = held - section * TRIO
            here = (slot >= 0) & (slot < TRIO)
            stays = here & (anchor == me)
            moves = here & (anchor != me)
            pair = gathered[anchor, USED - 16 : USED, :].astype(F32)
            kept_key = jnp.sum(jnp.where(row == slot, own_rows, 0.0), axis=0, keepdims=True)
            kept_value = jnp.sum(jnp.where(row == slot + 8, own_rows, 0.0), axis=0, keepdims=True)
            new_key = jnp.where(stays, kept_key, jnp.where(moves, pair[8:9], 0.0))
            new_value = jnp.where(stays, kept_value, jnp.where(moves, pair[9:10], 0.0))
            total = jnp.where(row == r, new_key, jnp.where(row == r + 8, new_value, total))
        total = total.astype(BF16)

        @pl.when(section == layer)
        def _():
            mine[...] = total

        @pl.when(section != layer)
        def _():
            swapped[HALF_ROWS:, :HEAD] = total


def final_kernel(
    ids, table, to_slots, first, second, received, keys, values, mine, second_in, third_in, fourth_in,
    out, key_out, value_out, pieces
):
    def write_rows(low, high):
        out[...] = (
            dot(to_slots[:HALF_ROWS, :], low, ((0,), (0,)))
            + dot(to_slots[HALF_ROWS:, :], high, ((0,), (0,)))
        ).astype(BF16)

    others = received[:HALF_ROWS, :]
    pl.when(ids[SECTION] == 0)(lambda: write_rows(first[...], others))
    pl.when(ids[SECTION] == 1)(lambda: write_rows(others, second[...]))

    me = ids[REPLICA]
    position = iota((CONTEXT, HEAD), 0)
    own = mine[...].astype(F32) + received[HALF_ROWS:, :HEAD].astype(F32)
    for p in range(N_DP):
        for i, (gathered, first_row) in enumerate(
            ((second_in, USED - 16), (third_in, USED - TILE), (fourth_in, USED - 16))
        ):
            pieces[pl.ds(p * TILES + i * TILE, TILE), :] = gathered[
                p, first_row : first_row + 16, :
            ].astype(F32)[TILE:]
    count = jnp.int32(0)
    for r in range(ROWS_DEV):
        source = table[SOURCE + r]
        anchor = over_six(source)
        written = position == table[NEW_LEN + r]
        moves = anchor != me

        def write(key_rows, value_rows):
            key_out[r] = jnp.where(written, own[r : r + 1], key_rows).astype(BF16)
            value_out[r] = jnp.where(written, own[r + 8 : r + 9], value_rows).astype(BF16)

        @pl.when(anchor == me)
        def _():
            held = source - anchor * ROWS_DEV
            write(keys[held].astype(F32), values[held].astype(F32))

        @pl.when(moves)
        def _():
            parts = [
                pieces[pl.ds(tile_row(count * PIECES + i), N_DP, stride=TILES), :]
                for i in range(PIECES)
            ]
            write(jnp.concatenate(parts[:2], 0), jnp.concatenate(parts[2:], 0))

        count = count + jnp.where(moves, 1, 0)


def call(kernel, name, specs, out_shapes, operands, scratch=()):
    spec_of = {"s": SMEM_SPEC, "v": VMEM_SPEC, "a": pl.BlockSpec(memory_space=pl.ANY)}
    return pl.pallas_call(
        kernel,
        out_shape=out_shapes,
        in_specs=[spec_of[letter] for letter in specs],
        out_specs=jax.tree.map(lambda _: VMEM_SPEC, out_shapes),
        scratch_shapes=list(scratch),
        compiler_params=pltpu.CompilerParams(vmem_limit_bytes=8 * 1024 * 1024),
        name=name,
    )(*operands)


def exchange(value, axis):
    return lax.all_to_all(value, axis, split_axis=0, concat_axis=0, tiled=True)


def swap(value):
    return lax.ppermute(value, "section", [(0, 1), (1, 0)])


def shape(*dims):
    return jax.ShapeDtypeStruct(dims, BF16)


def on_device(
    hidden_in,
    norm_gain,
    w_query,
    w_key,
    w_value,
    w_out,
    key_cache,
    value_cache,
    context_len,
    dest_replica,
    dest_slot,
):
    me = lax.axis_index("dp")
    section = lax.axis_index("section")
    ids = jnp.stack([section, me]).astype(jnp.int32)
    keys, values = key_cache[0], value_cache[0]
    new_index = (dest_replica * ROWS_DEV + dest_slot)[None, :]
    row = jnp.arange(ROWS, dtype=jnp.int32)
    entry = jnp.arange(4 * ROWS_DEV, dtype=jnp.int32)[:, None]
    kind = entry // ROWS_DEV
    wanted = me * ROWS_DEV + entry % ROWS_DEV
    found = jnp.where(kind < 2, row[None, :], new_index) == wanted
    chosen = jnp.where(
        kind == 0, dest_replica[None, :], jnp.where(kind == 3, row[None, :], context_len[None, :])
    )
    table = jnp.sum(jnp.where(found, chosen, 0), 1)

    half = HEAD // 2
    inverse_freq = ROPE_BASE ** (-(jnp.arange(half, dtype=F32) * (2.0 / HEAD)))
    held_len = jnp.concatenate([table[HELD_LEN : HELD_LEN + ROWS_DEV], jnp.zeros((2,), jnp.int32)])
    angles = held_len.astype(F32)[:, None] * jnp.concatenate([inverse_freq, inverse_freq])[None, :]
    cosine = jnp.cos(angles)
    sine = jnp.sin(angles) * jnp.where(jnp.arange(HEAD) < half, -1.0, 1.0)[None, :]

    sent_keys, sent_values = (
        jnp.pad(
            lax.dynamic_slice_in_dim(cache, (1 - section) * TRIO, TRIO).reshape(CACHE_ROWS, HEAD),
            ((0, WIDTH - CACHE_ROWS), (left, 3 * HEAD - left)),
        )
        for cache, left in ((keys, 2 * HEAD), (values, 3 * HEAD))
    )
    rest = (
        jnp.pad(w_key[0], ((0, 0), (0, 3 * HEAD)))
        + jnp.pad(w_value[0], ((0, 0), (HEAD, 2 * HEAD)))
        + sent_keys
        + sent_values
    )
    weights = call(
        load_kernel, "load", "vvv", shape(WIDTH + 16, PACKED), (w_query, rest, norm_gain)
    )
    other = swap(weights)
    residual, to_slots = call(
        prepare_kernel,
        "prepare",
        "svv",
        (shape(HALF_ROWS, WIDTH), shape(ROWS, ROWS)),
        (ids, new_index, hidden_in),
    )
    payload = call(
        first_kernel,
        "first",
        "ssvvvvv",
        shape(N_DP, BLOCK, HEAD),
        (ids, table, residual, weights, other, keys, values),
        [pltpu.VMEM((BLOCK * N_DP, HEAD), F32)],
    )
    first = exchange(payload, "dp")

    late_out, late_replica, late_slot, _ = lax.optimization_barrier(
        (w_out[0], dest_replica, dest_slot, payload)
    )
    out_other = swap(late_out)
    leaves = late_replica != row // ROWS_DEV
    before = (row[None, :] // ROWS_DEV == row[:, None] // ROWS_DEV) & (row[None, :] < row[:, None])
    rank = jnp.sum(jnp.where(before & leaves[None, :], 1, 0), 1)
    before = (late_replica[None, :] == late_replica[:, None]) & (
        late_slot[None, :] < late_slot[:, None]
    )
    place = jnp.sum(jnp.where(before & leaves[None, :], 1, 0), 1)
    arrival = jnp.where(leaves, place * N_DP + late_replica, -1)
    chosen = arrival[None, :] == jnp.arange(N_DP * MOVES, dtype=jnp.int32)[:, None]
    route = jnp.sum(jnp.where(chosen, (row // ROWS_DEV * MOVES + rank)[None, :], 0), 1)[None, :]

    def attend(layer, received, specs="", *more):
        return call(
            lambda *refs: attend_kernel(layer, *refs),
            "attend",
            "ssvvvvvv" + specs,
            (shape(N_DP, USED, HEAD), shape(16, HEAD))
            + (() if layer else (shape(N_DP, 2 * TILE, HEAD),)),
            (ids, table, cosine, sine, received, keys, values, other, *more),
            [pltpu.VMEM((N_DP * TILE, HEAD), F32)]
            if layer
            else [
                pltpu.VMEM((N_DP * MOVES * PIECES, HEAD), F32),
                pltpu.VMEM((N_DP * TILES, HEAD), F32),
            ],
        )

    def output(layer, received):
        return call(
            lambda *refs: output_kernel(layer, *refs),
            "output",
            "svvv",
            shape(N_TENSOR, HALF_ROWS, WIDTH),
            (ids, received, w_out[0], out_other),
            [pltpu.VMEM((N_DP * USED, HEAD), F32), pltpu.VMEM((HALF_ROWS, GROUP * HEAD), BF16)],
        )

    payload, own_0, later = attend(0, first, "va", route, out_other)
    second = exchange(payload, "dp")
    sums = exchange(output(0, second), "tensor")
    payload, result_0 = call(
        second_kernel,
        "second",
        "svvvvv",
        (shape(N_DP, USED + TILE, HEAD), shape(HALF_ROWS, WIDTH)),
        (ids, sums, residual, weights, other, later),
        [pltpu.VMEM((USED * N_DP, HEAD), F32)],
    )
    third = exchange(payload, "dp")
    payload, own_1 = attend(1, third, "v", later)
    fourth = exchange(payload, "dp")
    sums = exchange(output(1, fourth), "tensor")
    result_1, mine, swapped = call(
        last_kernel,
        "last",
        "ssvvvvvv",
        (shape(HALF_ROWS, WIDTH), shape(16, HEAD), shape(HALF_ROWS + 16, WIDTH)),
        (ids, table, sums, result_0, second, fourth, own_0, own_1),
    )
    layer_out, key_out, value_out = call(
        final_kernel,
        "final",
        "ssvvvvvvvvvv",
        (shape(ROWS, WIDTH), shape(ROWS_DEV, CONTEXT, HEAD), shape(ROWS_DEV, CONTEXT, HEAD)),
        (ids, table, to_slots, result_0, result_1, swap(swapped), keys, values, mine,
         second, third, fourth),
        [pltpu.VMEM((N_DP * TILES, HEAD), F32)],
    )
    return layer_out[None], key_out[None], value_out[None]


def solution(mesh):
    return jax.shard_map(
        on_device,
        mesh=mesh,
        in_specs=(
            P(None, "dp"),
            P("section", "dp"),
            P("section", "dp", "tensor"),
            P("section", "dp", "tensor"),
            P("section", "dp", "tensor"),
            P("section", "tensor", "dp"),
            P("section", "dp", None, "tensor"),
            P("section", "dp", None, "tensor"),
            P(),
            P(),
            P(),
        ),
        out_specs=(
            P("section", None, "dp"),
            P("section", "dp", None, "tensor"),
            P("section", "dp", None, "tensor"),
        ),
        check_vma=False,
    )
```

```python
import jax
import jax.numpy as jnp
from jax import lax
from jax.experimental import pallas as pl
from jax.experimental.pallas import tpu as pltpu
from jax.sharding import PartitionSpec as P

N_DP = 32
N_TENSOR = 8
ROWS_DEV = 6
ROWS = 192
TRIO = 3
HALF_ROWS = N_DP * TRIO
CONTEXT = 64
MOVES = 4
PIECES = 4
HEAD = 128
GROUP = 8
PARTS = GROUP + 2
USED = 32
BLOCK = USED + MOVES * PIECES
TILE = 8
TILES = 3 * TILE
WIDTH = 256
MODEL = 8192
CACHE_ROWS = TRIO * CONTEXT
QUERY = GROUP * HEAD
ALL_PARTS = PARTS * HEAD
PACKED = ALL_PARTS + 2 * HEAD
EPSILON = 1e-06
ROPE_BASE = 1000000.0
F32 = jnp.float32
BF16 = jnp.bfloat16

SECTION, REPLICA = 0, 1
DEST, HELD_LEN, NEW_LEN, SOURCE = 0, 6, 12, 18

SMEM_SPEC = pl.BlockSpec(memory_space=pltpu.SMEM)
VMEM_SPEC = pl.BlockSpec(memory_space=pltpu.VMEM)


def iota(shape, dim):
    return lax.broadcasted_iota(jnp.int32, shape, dim)


def pick(condition):
    return jnp.where(condition, 1.0, 0.0).astype(BF16)


def over_six(index):
    return (index * 171) >> 10


def over_ten(index):
    return (index * 205) >> 11


def dot(left, right, contract=((1,), (0,))):
    return lax.dot_general(left, right, (contract, ((), ())), preferred_element_type=F32)


def to_new_order(new_index):
    return pick(iota((ROWS, ROWS), 0) == new_index)


def project(rows, weights, spread):
    by_slot = rows.astype(F32)
    terms = weights[WIDTH:, QUERY:ALL_PARTS].astype(F32)
    gain = terms[0:1] + terms[1:2] + terms[2:3]
    scaled = (by_slot * gain).astype(BF16)
    for pair in range(PARTS // 2):
        product = dot(scaled, weights[:WIDTH, pair * 2 * HEAD : (pair + 1) * 2 * HEAD])
        for s in range(TRIO):
            for side in range(2):
                row = s * PARTS + 2 * pair + side
                spread[pl.ds(row * N_DP, N_DP), :] = product[
                    s * N_DP : (s + 1) * N_DP, side * HEAD : (side + 1) * HEAD
                ]


def spread_squares(rows, spread):
    by_slot = rows.astype(F32)
    square = jnp.sum(by_slot * by_slot, axis=1, keepdims=True)
    lane = iota((N_DP, HEAD), 1)
    squares = jnp.zeros((N_DP, HEAD), F32)
    for s in range(TRIO):
        squares = jnp.where(lane == s, square[s * N_DP : (s + 1) * N_DP], squares)
    high = squares.astype(BF16).astype(F32)
    row = TRIO * PARTS
    spread[pl.ds(row * N_DP, N_DP), :] = high
    spread[pl.ds((row + 1) * N_DP, N_DP), :] = squares - high


def load_kernel(query, rest, gain, weights):
    weights[:WIDTH, :QUERY] = query[0]
    weights[WIDTH:, :QUERY] = jnp.zeros((16, QUERY), BF16)
    weights[:WIDTH, QUERY:] = rest[...]
    high = gain[...].astype(BF16).astype(F32)
    middle = (gain[...] - high).astype(BF16).astype(F32)
    low = gain[...] - high - middle
    row = iota((16, WIDTH), 0)
    terms = jnp.where(row == 0, high, jnp.where(row == 1, middle, jnp.where(row == 2, low, 0.0)))
    weights[WIDTH:, QUERY:ALL_PARTS] = terms.astype(BF16)
    weights[WIDTH:, ALL_PARTS:] = jnp.zeros((16, 2 * HEAD), BF16)


def prepare_kernel(ids, new_index, hidden, residual, to_slots_out):
    row, column = iota((ROWS, ROWS), 0), iota((ROWS, ROWS), 1)
    by_slot_order = pick(column == (row & (N_DP - 1)) * ROWS_DEV + (row >> 5))
    to_slots = dot(by_slot_order, to_new_order(new_index[...]), ((1,), (1,))).astype(BF16)
    to_slots_out[...] = to_slots
    by_slot = dot(to_slots, hidden[...]).astype(BF16)

    @pl.when(ids[SECTION] == 0)
    def _():
        residual[...] = by_slot[:HALF_ROWS]

    @pl.when(ids[SECTION] == 1)
    def _():
        residual[...] = by_slot[HALF_ROWS:]


def first_kernel(ids, table, rows, weights, other, keys, values, payload, spread):
    count = jnp.int32(0)
    for s in range(ROWS_DEV):
        leaves = table[DEST + s] != ids[REPLICA]

        @pl.when(leaves)
        def _():
            base = pl.multiple_of(USED * N_DP + count * (PIECES * N_DP), N_DP)
            spread[pl.ds(base, CONTEXT), :] = keys[s].astype(F32)
            spread[pl.ds(base + CONTEXT, CONTEXT), :] = values[s].astype(F32)

        count = count + jnp.where(leaves, 1, 0)
    spread_squares(rows[...], spread)
    pl.when(ids[SECTION] == 0)(lambda: project(rows[...], weights, spread))
    pl.when(ids[SECTION] == 1)(lambda: project(rows[...], other, spread))
    for p in range(N_DP):
        payload[p] = spread[pl.ds(p, BLOCK, stride=N_DP), :].astype(BF16)


def tile_row(piece):
    return piece + jnp.where(piece < 14, 2, 4)


def forward(route, received, pieces, tiles):
    count = N_DP * MOVES
    for p in range(N_DP):
        pieces[pl.ds(p * MOVES * PIECES, MOVES * PIECES), :] = received[p, USED:, :].astype(F32)
        tiles[pl.ds(p * TILES, TILE), :] = jnp.zeros((TILE, HEAD), F32)
        tiles[pl.ds(p * TILES + 2 * TILE, TILE), :] = jnp.zeros((TILE, HEAD), F32)
    to_replica = pick(iota((count, count), 0) == route[...])
    for i in range(PIECES):
        part = pieces[pl.ds(i, count, stride=PIECES), :].astype(BF16)
        sorted_part = dot(to_replica, part, ((0,), (0,)))
        for m in range(MOVES):
            piece = m * PIECES + i
            row = piece + (2 if piece < 14 else 4)
            tiles[pl.ds(row, N_DP, stride=TILES), :] = sorted_part[m * N_DP : (m + 1) * N_DP]


def attend_kernel(
    layer, ids, table, cosine, sine, received, keys, values, other, *refs
):
    if layer == 0:
        route, _, payload, own, later, pieces, tiles = refs
        forward(route, received, pieces, tiles)
        for p in range(N_DP):
            later[p] = tiles[pl.ds(p * TILES + TILE, 2 * TILE), :].astype(BF16)
    else:
        later, payload, own, tiles = refs
        for p in range(N_DP):
            tiles[pl.ds(p * TILE, TILE), :] = later[p].astype(F32)[TILE:]
    section = ids[SECTION]

    def attend(all_keys, all_values):
        total = received[0, :USED, :].astype(F32)
        for p in range(1, N_DP):
            total = total + received[p, :USED, :].astype(F32)
        row = iota((USED, HEAD), 0)
        lane = iota((USED, HEAD), 1)
        slot = over_ten(row)
        part = row - slot * PARTS
        tail = TRIO * PARTS
        squares = total[tail : tail + 1] + total[tail + 1 : tail + 2]
        square = jnp.sum(jnp.where(lane == slot, squares, 0.0), axis=1, keepdims=True)
        projected = total * lax.rsqrt(square / MODEL + EPSILON)
        cos_rows = jnp.ones((USED, HEAD), F32)
        sin_rows = jnp.zeros((USED, HEAD), F32)
        for s in range(TRIO):
            turned = (slot == s) & (part <= GROUP)
            cos_rows = jnp.where(turned, cosine[pl.ds(section * TRIO + s, 1), :], cos_rows)
            sin_rows = jnp.where(turned, sine[pl.ds(section * TRIO + s, 1), :], sin_rows)
        vectors = (
            projected * cos_rows + pltpu.roll(projected, HEAD // 2, 1) * sin_rows
        ).astype(BF16)

        scale = HEAD ** (-0.5)
        scores = dot(vectors, all_keys, ((1,), (1,))) * scale
        among = dot(vectors, vectors, ((1,), (1,))) * scale
        wide = (USED, CACHE_ROWS)
        wide_slot = over_ten(iota(wide, 0))
        column = iota(wide, 1)
        live = column < 0
        for s in range(TRIO):
            live = live | (
                (wide_slot == s)
                & (column >= s * CONTEXT)
                & (column < s * CONTEXT + table[HELD_LEN + section * TRIO + s])
            )
        scores = jnp.where(live, scores, -1e30)
        small_slot = over_ten(iota((USED, USED), 0))
        small_column = iota((USED, USED), 1)
        own_score = jnp.sum(
            jnp.where(small_column == small_slot * PARTS + GROUP, among, 0.0), axis=1, keepdims=True
        )
        highest = jnp.maximum(jnp.max(scores, axis=1, keepdims=True), own_score)
        terms = jnp.exp(scores - highest)
        own_term = jnp.exp(own_score - highest)
        denominator = jnp.sum(terms, axis=1, keepdims=True) + own_term
        weights = (terms / denominator).astype(BF16)
        own_weights = jnp.where(
            small_column == small_slot * PARTS + GROUP + 1, own_term / denominator, 0.0
        ).astype(BF16)
        attended = (dot(weights, all_values) + dot(own_weights, vectors)).astype(BF16)

        out_row, in_row = iota((USED, USED), 0), iota((USED, USED), 1)
        out_slot = out_row >> 3
        order = pick((in_row == out_slot * PARTS + (out_row & 7)) & (out_slot < TRIO))
        block = dot(order, attended)
        own_row, own_in = iota((16, USED), 0), iota((16, USED), 1)
        own_slot = own_row & 7
        own_pick = pick(
            (own_in == own_slot * PARTS + GROUP + (own_row >> 3)) & (own_slot < TRIO)
        )
        own_pair = dot(own_pick, vectors)
        own[...] = own_pair.astype(BF16)
        stride = TILES if layer == 0 else TILE
        for s in range(TRIO):
            first = table[DEST + section * TRIO + s] * stride
            tiles[pl.ds(first, 1), :] = own_pair[s : s + 1]
            tiles[pl.ds(first + 1, 1), :] = own_pair[8 + s : 9 + s]
        low, high = block[:16].astype(BF16), block[16 : 16 + TILE]
        for p in range(N_DP):
            payload[p, :16, :] = low
            payload[p, 16:, :] = jnp.concatenate(
                [high, tiles[pl.ds(p * stride, TILE), :]], 0
            ).astype(BF16)

    @pl.when(section == layer)
    def _():
        first = layer * TRIO
        attend(
            keys[first : first + TRIO].reshape(CACHE_ROWS, HEAD),
            values[first : first + TRIO].reshape(CACHE_ROWS, HEAD),
        )

    @pl.when(section != layer)
    def _():
        attend(other[:CACHE_ROWS, ALL_PARTS : ALL_PARTS + HEAD], other[:CACHE_ROWS, ALL_PARTS + HEAD :])


def output_kernel(layer, ids, received, w_out, w_other, payload, wide, rows):
    for p in range(N_DP):
        wide[pl.ds(p * USED, USED), :] = received[p, :USED, :].astype(F32)
    for s in range(TRIO):
        for h in range(GROUP):
            rows[s * N_DP : (s + 1) * N_DP, h * HEAD : (h + 1) * HEAD] = wide[
                pl.ds(s * 8 + h, N_DP, stride=USED), :
            ].astype(BF16)

    def write(weight):
        product = dot(rows[...], weight[...]).astype(BF16)
        for t in range(N_TENSOR):
            payload[t] = product

    pl.when(ids[SECTION] == layer)(lambda: write(w_out))
    pl.when(ids[SECTION] != layer)(lambda: write(w_other))


def summed(received, residual):
    total = received[0].astype(F32)
    for t in range(1, N_TENSOR):
        total = total + received[t].astype(F32)
    return (residual[...].astype(F32) + total).astype(BF16)


def second_kernel(ids, received, residual, weights, other, later, payload, result, spread):
    rows = summed(received, residual)
    result[...] = rows
    spread_squares(rows, spread)
    pl.when(ids[SECTION] == 1)(lambda: project(rows, weights, spread))
    pl.when(ids[SECTION] == 0)(lambda: project(rows, other, spread))
    for p in range(N_DP):
        payload[p, :USED, :] = spread[pl.ds(p, USED, stride=N_DP), :].astype(BF16)
        payload[p, USED:, :] = later[p].astype(F32)[:TILE].astype(BF16)


def last_kernel(
    ids, table, received, before, gathered_0, gathered_1, own_0, own_1, result, mine, swapped
):
    rows = summed(received, before)
    result[...] = rows

    @pl.when(ids[SECTION] == 0)
    def _():
        swapped[:HALF_ROWS, :] = rows

    @pl.when(ids[SECTION] == 1)
    def _():
        swapped[:HALF_ROWS, :] = before[...]

    me, section = ids[REPLICA], ids[SECTION]
    row = iota((16, HEAD), 0)
    swapped[HALF_ROWS:, HEAD:] = jnp.zeros((16, WIDTH - HEAD), BF16)
    for layer, (gathered, own) in enumerate(((gathered_0, own_0), (gathered_1, own_1))):
        own_rows = own[...].astype(F32)
        total = jnp.zeros((16, HEAD), F32)
        for r in range(ROWS_DEV):
            source = table[SOURCE + r]
            anchor = over_six(source)
            held = source - anchor * ROWS_DEV
            slot = held - section * TRIO
            here = (slot >= 0) & (slot < TRIO)
            stays = here & (anchor == me)
            moves = here & (anchor != me)
            pair = gathered[anchor, USED - 16 : USED, :].astype(F32)
            kept_key = jnp.sum(jnp.where(row == slot, own_rows, 0.0), axis=0, keepdims=True)
            kept_value = jnp.sum(jnp.where(row == slot + 8, own_rows, 0.0), axis=0, keepdims=True)
            new_key = jnp.where(stays, kept_key, jnp.where(moves, pair[8:9], 0.0))
            new_value = jnp.where(stays, kept_value, jnp.where(moves, pair[9:10], 0.0))
            total = jnp.where(row == r, new_key, jnp.where(row == r + 8, new_value, total))
        total = total.astype(BF16)

        @pl.when(section == layer)
        def _():
            mine[...] = total

        @pl.when(section != layer)
        def _():
            swapped[HALF_ROWS:, :HEAD] = total


def arrive_kernel(
    ids, table, to_slots, first, second, keys, values, second_in, third_in, fourth_in,
    part, key_rows, value_rows, pieces
):
    def write_rows(order, rows):
        part[...] = dot(order, rows[...], ((0,), (0,)))

    pl.when(ids[SECTION] == 0)(lambda: write_rows(to_slots[:HALF_ROWS, :], first))
    pl.when(ids[SECTION] == 1)(lambda: write_rows(to_slots[HALF_ROWS:, :], second))
    for p in range(N_DP):
        for i, (gathered, first_row) in enumerate(
            ((second_in, USED - 16), (third_in, USED - TILE), (fourth_in, USED - 16))
        ):
            pieces[pl.ds(p * TILES + i * TILE, TILE), :] = gathered[
                p, first_row : first_row + 16, :
            ].astype(F32)[TILE:]
    count = jnp.int32(0)
    for r in range(ROWS_DEV):
        source = table[SOURCE + r]
        anchor = over_six(source)
        moves = anchor != ids[REPLICA]

        @pl.when(anchor == ids[REPLICA])
        def _():
            held = source - anchor * ROWS_DEV
            key_rows[r] = keys[held]
            value_rows[r] = values[held]

        @pl.when(moves)
        def _():
            parts = [
                pieces[pl.ds(tile_row(count * PIECES + i), N_DP, stride=TILES), :].astype(BF16)
                for i in range(PIECES)
            ]
            key_rows[r] = jnp.concatenate(parts[:2], 0)
            value_rows[r] = jnp.concatenate(parts[2:], 0)

        count = count + jnp.where(moves, 1, 0)


def final_kernel(
    ids, table, to_slots, part, key_rows, value_rows, received, mine, out, key_out, value_out
):
    def write_rows(order):
        out[...] = (part[...] + dot(order, received[:HALF_ROWS, :], ((0,), (0,)))).astype(BF16)

    pl.when(ids[SECTION] == 0)(lambda: write_rows(to_slots[HALF_ROWS:, :]))
    pl.when(ids[SECTION] == 1)(lambda: write_rows(to_slots[:HALF_ROWS, :]))
    position = iota((CONTEXT, HEAD), 0)
    own = mine[...].astype(F32) + received[HALF_ROWS:, :HEAD].astype(F32)
    for r in range(ROWS_DEV):
        written = position == table[NEW_LEN + r]
        for rows, target, row in ((key_rows, key_out, r), (value_rows, value_out, r + 8)):
            target[r] = jnp.where(written, own[row : row + 1], rows[r].astype(F32)).astype(BF16)


def call(kernel, name, specs, out_shapes, operands, scratch=()):
    spec_of = {"s": SMEM_SPEC, "v": VMEM_SPEC, "a": pl.BlockSpec(memory_space=pl.ANY)}
    return pl.pallas_call(
        kernel,
        out_shape=out_shapes,
        in_specs=[spec_of[letter] for letter in specs],
        out_specs=jax.tree.map(lambda _: VMEM_SPEC, out_shapes),
        scratch_shapes=list(scratch),
        compiler_params=pltpu.CompilerParams(vmem_limit_bytes=8 * 1024 * 1024),
        name=name,
    )(*operands)


def exchange(value, axis):
    return lax.all_to_all(value, axis, split_axis=0, concat_axis=0, tiled=True)


def swap(value):
    return lax.ppermute(value, "section", [(0, 1), (1, 0)])


def shape(*dims):
    return jax.ShapeDtypeStruct(dims, BF16)


def on_device(
    hidden_in,
    norm_gain,
    w_query,
    w_key,
    w_value,
    w_out,
    key_cache,
    value_cache,
    context_len,
    dest_replica,
    dest_slot,
):
    me = lax.axis_index("dp")
    section = lax.axis_index("section")
    ids = jnp.stack([section, me]).astype(jnp.int32)
    keys, values = key_cache[0], value_cache[0]
    new_index = (dest_replica * ROWS_DEV + dest_slot)[None, :]
    row = jnp.arange(ROWS, dtype=jnp.int32)
    entry = jnp.arange(4 * ROWS_DEV, dtype=jnp.int32)[:, None]
    kind = entry // ROWS_DEV
    wanted = me * ROWS_DEV + entry % ROWS_DEV
    found = jnp.where(kind < 2, row[None, :], new_index) == wanted
    chosen = jnp.where(
        kind == 0, dest_replica[None, :], jnp.where(kind == 3, row[None, :], context_len[None, :])
    )
    table = jnp.sum(jnp.where(found, chosen, 0), 1)

    half = HEAD // 2
    inverse_freq = ROPE_BASE ** (-(jnp.arange(half, dtype=F32) * (2.0 / HEAD)))
    held_len = jnp.concatenate([table[HELD_LEN : HELD_LEN + ROWS_DEV], jnp.zeros((2,), jnp.int32)])
    angles = held_len.astype(F32)[:, None] * jnp.concatenate([inverse_freq, inverse_freq])[None, :]
    cosine = jnp.cos(angles)
    sine = jnp.sin(angles) * jnp.where(jnp.arange(HEAD) < half, -1.0, 1.0)[None, :]

    sent_keys, sent_values = (
        jnp.pad(
            lax.dynamic_slice_in_dim(cache, (1 - section) * TRIO, TRIO).reshape(CACHE_ROWS, HEAD),
            ((0, WIDTH - CACHE_ROWS), (left, 3 * HEAD - left)),
        )
        for cache, left in ((keys, 2 * HEAD), (values, 3 * HEAD))
    )
    rest = (
        jnp.pad(w_key[0], ((0, 0), (0, 3 * HEAD)))
        + jnp.pad(w_value[0], ((0, 0), (HEAD, 2 * HEAD)))
        + sent_keys
        + sent_values
    )
    weights = call(
        load_kernel, "load", "vvv", shape(WIDTH + 16, PACKED), (w_query, rest, norm_gain)
    )
    other = swap(weights)
    residual, to_slots = call(
        prepare_kernel,
        "prepare",
        "svv",
        (shape(HALF_ROWS, WIDTH), shape(ROWS, ROWS)),
        (ids, new_index, hidden_in),
    )
    payload = call(
        first_kernel,
        "first",
        "ssvvvvv",
        shape(N_DP, BLOCK, HEAD),
        (ids, table, residual, weights, other, keys, values),
        [pltpu.VMEM((BLOCK * N_DP, HEAD), F32)],
    )
    first = exchange(payload, "dp")

    late_out, late_replica, late_slot, _ = lax.optimization_barrier(
        (w_out[0], dest_replica, dest_slot, payload)
    )
    out_other = swap(late_out)
    leaves = late_replica != row // ROWS_DEV
    before = (row[None, :] // ROWS_DEV == row[:, None] // ROWS_DEV) & (row[None, :] < row[:, None])
    rank = jnp.sum(jnp.where(before & leaves[None, :], 1, 0), 1)
    before = (late_replica[None, :] == late_replica[:, None]) & (
        late_slot[None, :] < late_slot[:, None]
    )
    place = jnp.sum(jnp.where(before & leaves[None, :], 1, 0), 1)
    arrival = jnp.where(leaves, place * N_DP + late_replica, -1)
    chosen = arrival[None, :] == jnp.arange(N_DP * MOVES, dtype=jnp.int32)[:, None]
    route = jnp.sum(jnp.where(chosen, (row // ROWS_DEV * MOVES + rank)[None, :], 0), 1)[None, :]

    def attend(layer, received, specs="", *more):
        return call(
            lambda *refs: attend_kernel(layer, *refs),
            "attend",
            "ssvvvvvv" + specs,
            (shape(N_DP, USED, HEAD), shape(16, HEAD))
            + (() if layer else (shape(N_DP, 2 * TILE, HEAD),)),
            (ids, table, cosine, sine, received, keys, values, other, *more),
            [pltpu.VMEM((N_DP * TILE, HEAD), F32)]
            if layer
            else [
                pltpu.VMEM((N_DP * MOVES * PIECES, HEAD), F32),
                pltpu.VMEM((N_DP * TILES, HEAD), F32),
            ],
        )

    def output(layer, received):
        return call(
            lambda *refs: output_kernel(layer, *refs),
            "output",
            "svvv",
            shape(N_TENSOR, HALF_ROWS, WIDTH),
            (ids, received, w_out[0], out_other),
            [pltpu.VMEM((N_DP * USED, HEAD), F32), pltpu.VMEM((HALF_ROWS, GROUP * HEAD), BF16)],
        )

    payload, own_0, later = attend(0, first, "va", route, out_other)
    second = exchange(payload, "dp")
    sums = exchange(output(0, second), "tensor")
    payload, result_0 = call(
        second_kernel,
        "second",
        "svvvvv",
        (shape(N_DP, USED + TILE, HEAD), shape(HALF_ROWS, WIDTH)),
        (ids, sums, residual, weights, other, later),
        [pltpu.VMEM((USED * N_DP, HEAD), F32)],
    )
    third = exchange(payload, "dp")
    payload, own_1 = attend(1, third, "v", later)
    fourth = exchange(payload, "dp")
    sums = exchange(output(1, fourth), "tensor")
    result_1, mine, swapped = call(
        last_kernel,
        "last",
        "ssvvvvvv",
        (shape(HALF_ROWS, WIDTH), shape(16, HEAD), shape(HALF_ROWS + 16, WIDTH)),
        (ids, table, sums, result_0, second, fourth, own_0, own_1),
    )
    cache_shape = shape(ROWS_DEV, CONTEXT, HEAD)
    received = swap(swapped)
    part, key_rows, value_rows = call(
        arrive_kernel,
        "arrive",
        "ssvvvvvvvv",
        (jax.ShapeDtypeStruct((ROWS, WIDTH), F32), cache_shape, cache_shape),
        (ids, table, to_slots, result_0, result_1, keys, values, second, third, fourth),
        [pltpu.VMEM(((N_DP + 1) * TILES, HEAD), F32)],
    )
    layer_out, key_out, value_out = call(
        final_kernel,
        "final",
        "ssvvvvvv",
        (shape(ROWS, WIDTH), cache_shape, cache_shape),
        (ids, table, to_slots, part, key_rows, value_rows, received, mine),
    )
    return layer_out[None], key_out[None], value_out[None]


def solution(mesh):
    return jax.shard_map(
        on_device,
        mesh=mesh,
        in_specs=(
            P(None, "dp"),
            P("section", "dp"),
            P("section", "dp", "tensor"),
            P("section", "dp", "tensor"),
            P("section", "dp", "tensor"),
            P("section", "tensor", "dp"),
            P("section", "dp", None, "tensor"),
            P("section", "dp", None, "tensor"),
            P(),
            P(),
            P(),
        ),
        out_specs=(
            P("section", None, "dp"),
            P("section", "dp", None, "tensor"),
            P("section", "dp", None, "tensor"),
        ),
        check_vma=False,
    )
```

```python
import jax
import jax.numpy as jnp
from jax import lax
from jax.experimental import pallas as pl
from jax.experimental.pallas import tpu as pltpu
from jax.sharding import PartitionSpec as P

N_DP = 32
N_TENSOR = 8
ROWS_DEV = 6
ROWS = 192
TRIO = 3
HALF_ROWS = N_DP * TRIO
CONTEXT = 64
MOVES = 4
PIECES = 4
HEAD = 128
GROUP = 8
PARTS = GROUP + 2
USED = 32
BLOCK = USED + MOVES * PIECES
TILE = 8
TILES = 3 * TILE
WIDTH = 256
MODEL = 8192
CACHE_ROWS = TRIO * CONTEXT
QUERY = GROUP * HEAD
ALL_PARTS = PARTS * HEAD
PACKED = ALL_PARTS + 2 * HEAD
EPSILON = 1e-06
ROPE_BASE = 1000000.0
F32 = jnp.float32
BF16 = jnp.bfloat16

SECTION, REPLICA = 0, 1
DEST, HELD_LEN, NEW_LEN, SOURCE = 0, 6, 12, 18

SMEM_SPEC = pl.BlockSpec(memory_space=pltpu.SMEM)
VMEM_SPEC = pl.BlockSpec(memory_space=pltpu.VMEM)


def iota(shape, dim):
    return lax.broadcasted_iota(jnp.int32, shape, dim)


def pick(condition):
    return jnp.where(condition, 1.0, 0.0).astype(BF16)


def over_six(index):
    return (index * 171) >> 10


def over_ten(index):
    return (index * 205) >> 11


def dot(left, right, contract=((1,), (0,))):
    return lax.dot_general(left, right, (contract, ((), ())), preferred_element_type=F32)


def to_new_order(new_index):
    return pick(iota((ROWS, ROWS), 0) == new_index)


def project(rows, weights, spread):
    by_slot = rows.astype(F32)
    terms = weights[WIDTH:, QUERY:ALL_PARTS].astype(F32)
    gain = terms[0:1] + terms[1:2] + terms[2:3]
    scaled = (by_slot * gain).astype(BF16)
    for pair in range(PARTS // 2):
        product = dot(scaled, weights[:WIDTH, pair * 2 * HEAD : (pair + 1) * 2 * HEAD])
        for s in range(TRIO):
            for side in range(2):
                row = s * PARTS + 2 * pair + side
                spread[pl.ds(row * N_DP, N_DP), :] = product[
                    s * N_DP : (s + 1) * N_DP, side * HEAD : (side + 1) * HEAD
                ]


def spread_squares(rows, spread, row=TRIO * PARTS):
    by_slot = rows.astype(F32)
    square = jnp.sum(by_slot * by_slot, axis=1, keepdims=True)
    lane = iota((N_DP, HEAD), 1)
    squares = jnp.zeros((N_DP, HEAD), F32)
    for s in range(TRIO):
        squares = jnp.where(lane == s, square[s * N_DP : (s + 1) * N_DP], squares)
    high = squares.astype(BF16).astype(F32)
    spread[pl.ds(row * N_DP, N_DP), :] = high
    spread[pl.ds((row + 1) * N_DP, N_DP), :] = squares - high


def load_kernel(query, rest, gain, weights):
    weights[:WIDTH, :QUERY] = query[0]
    weights[WIDTH:, :QUERY] = jnp.zeros((16, QUERY), BF16)
    weights[:WIDTH, QUERY:] = rest[...]
    high = gain[...].astype(BF16).astype(F32)
    middle = (gain[...] - high).astype(BF16).astype(F32)
    low = gain[...] - high - middle
    row = iota((16, WIDTH), 0)
    terms = jnp.where(row == 0, high, jnp.where(row == 1, middle, jnp.where(row == 2, low, 0.0)))
    weights[WIDTH:, QUERY:ALL_PARTS] = terms.astype(BF16)
    weights[WIDTH:, ALL_PARTS:] = jnp.zeros((16, 2 * HEAD), BF16)


def prepare_kernel(
    ids, table, new_index, hidden, keys, values, residual, to_slots_out, squares, cut, spread
):
    row, column = iota((ROWS, ROWS), 0), iota((ROWS, ROWS), 1)
    by_slot_order = pick(column == (row & (N_DP - 1)) * ROWS_DEV + (row >> 5))
    to_slots = dot(by_slot_order, to_new_order(new_index[...]), ((1,), (1,))).astype(BF16)
    to_slots_out[...] = to_slots
    by_slot = dot(to_slots, hidden[...]).astype(BF16)

    @pl.when(ids[SECTION] == 0)
    def _():
        residual[...] = by_slot[:HALF_ROWS]
        spread_squares(by_slot[:HALF_ROWS], squares, 0)

    @pl.when(ids[SECTION] == 1)
    def _():
        residual[...] = by_slot[HALF_ROWS:]
        spread_squares(by_slot[HALF_ROWS:], squares, 0)

    count = jnp.int32(0)
    for s in range(ROWS_DEV):
        leaves = table[DEST + s] != ids[REPLICA]

        @pl.when(leaves)
        def _():
            base = pl.multiple_of(count * (PIECES * N_DP), N_DP)
            spread[pl.ds(base, CONTEXT), :] = keys[s].astype(F32)
            spread[pl.ds(base + CONTEXT, CONTEXT), :] = values[s].astype(F32)

        count = count + jnp.where(leaves, 1, 0)
    for p in range(N_DP):
        cut[p] = spread[pl.ds(p, MOVES * PIECES, stride=N_DP), :].astype(BF16)


def first_kernel(ids, rows, squares, cut, weights, other, payload, spread):
    spread[pl.ds(TRIO * PARTS * N_DP, 2 * N_DP), :] = squares[...]
    pl.when(ids[SECTION] == 0)(lambda: project(rows[...], weights, spread))
    pl.when(ids[SECTION] == 1)(lambda: project(rows[...], other, spread))
    for p in range(N_DP):
        payload[p, :USED, :] = spread[pl.ds(p, USED, stride=N_DP), :].astype(BF16)
        payload[p, USED:, :] = cut[p]


def tile_row(piece):
    return piece + jnp.where(piece < 14, 2, 4)


def forward(route, received, pieces, tiles):
    count = N_DP * MOVES
    for p in range(N_DP):
        pieces[pl.ds(p * MOVES * PIECES, MOVES * PIECES), :] = received[p, USED:, :].astype(F32)
        tiles[pl.ds(p * TILES, TILE), :] = jnp.zeros((TILE, HEAD), F32)
        tiles[pl.ds(p * TILES + 2 * TILE, TILE), :] = jnp.zeros((TILE, HEAD), F32)
    to_replica = pick(iota((count, count), 0) == route[...])
    for i in range(PIECES):
        part = pieces[pl.ds(i, count, stride=PIECES), :].astype(BF16)
        sorted_part = dot(to_replica, part, ((0,), (0,)))
        for m in range(MOVES):
            piece = m * PIECES + i
            row = piece + (2 if piece < 14 else 4)
            tiles[pl.ds(row, N_DP, stride=TILES), :] = sorted_part[m * N_DP : (m + 1) * N_DP]


def attend_kernel(
    layer, ids, table, cosine, sine, received, keys, values, other, *refs
):
    if layer == 0:
        route, _, payload, own, later, pieces, tiles = refs
        forward(route, received, pieces, tiles)
        for p in range(N_DP):
            later[p] = tiles[pl.ds(p * TILES + TILE, 2 * TILE), :].astype(BF16)
    else:
        later, payload, own, tiles = refs
        for p in range(N_DP):
            tiles[pl.ds(p * TILE, TILE), :] = later[p].astype(F32)[TILE:]
    section = ids[SECTION]

    def attend(all_keys, all_values):
        total = received[0, :USED, :].astype(F32)
        for p in range(1, N_DP):
            total = total + received[p, :USED, :].astype(F32)
        row = iota((USED, HEAD), 0)
        lane = iota((USED, HEAD), 1)
        slot = over_ten(row)
        part = row - slot * PARTS
        tail = TRIO * PARTS
        squares = total[tail : tail + 1] + total[tail + 1 : tail + 2]
        square = jnp.sum(jnp.where(lane == slot, squares, 0.0), axis=1, keepdims=True)
        projected = total * lax.rsqrt(square / MODEL + EPSILON)
        cos_rows = jnp.ones((USED, HEAD), F32)
        sin_rows = jnp.zeros((USED, HEAD), F32)
        for s in range(TRIO):
            turned = (slot == s) & (part <= GROUP)
            cos_rows = jnp.where(turned, cosine[pl.ds(section * TRIO + s, 1), :], cos_rows)
            sin_rows = jnp.where(turned, sine[pl.ds(section * TRIO + s, 1), :], sin_rows)
        vectors = (
            projected * cos_rows + pltpu.roll(projected, HEAD // 2, 1) * sin_rows
        ).astype(BF16)

        scale = HEAD ** (-0.5)
        scores = dot(vectors, all_keys, ((1,), (1,))) * scale
        among = dot(vectors, vectors, ((1,), (1,))) * scale
        wide = (USED, CACHE_ROWS)
        wide_slot = over_ten(iota(wide, 0))
        column = iota(wide, 1)
        live = column < 0
        for s in range(TRIO):
            live = live | (
                (wide_slot == s)
                & (column >= s * CONTEXT)
                & (column < s * CONTEXT + table[HELD_LEN + section * TRIO + s])
            )
        scores = jnp.where(live, scores, -1e30)
        small_slot = over_ten(iota((USED, USED), 0))
        small_column = iota((USED, USED), 1)
        own_score = jnp.sum(
            jnp.where(small_column == small_slot * PARTS + GROUP, among, 0.0), axis=1, keepdims=True
        )
        highest = jnp.maximum(jnp.max(scores, axis=1, keepdims=True), own_score)
        terms = jnp.exp(scores - highest)
        own_term = jnp.exp(own_score - highest)
        denominator = jnp.sum(terms, axis=1, keepdims=True) + own_term
        weights = (terms / denominator).astype(BF16)
        own_weights = jnp.where(
            small_column == small_slot * PARTS + GROUP + 1, own_term / denominator, 0.0
        ).astype(BF16)
        attended = (dot(weights, all_values) + dot(own_weights, vectors)).astype(BF16)

        out_row, in_row = iota((USED, USED), 0), iota((USED, USED), 1)
        out_slot = out_row >> 3
        order = pick((in_row == out_slot * PARTS + (out_row & 7)) & (out_slot < TRIO))
        block = dot(order, attended)
        own_row, own_in = iota((16, USED), 0), iota((16, USED), 1)
        own_slot = own_row & 7
        own_pick = pick(
            (own_in == own_slot * PARTS + GROUP + (own_row >> 3)) & (own_slot < TRIO)
        )
        own_pair = dot(own_pick, vectors)
        own[...] = own_pair.astype(BF16)
        stride = TILES if layer == 0 else TILE
        for s in range(TRIO):
            first = table[DEST + section * TRIO + s] * stride
            tiles[pl.ds(first, 1), :] = own_pair[s : s + 1]
            tiles[pl.ds(first + 1, 1), :] = own_pair[8 + s : 9 + s]
        low, high = block[:16].astype(BF16), block[16 : 16 + TILE]
        for p in range(N_DP):
            payload[p, :16, :] = low
            payload[p, 16:, :] = jnp.concatenate(
                [high, tiles[pl.ds(p * stride, TILE), :]], 0
            ).astype(BF16)

    @pl.when(section == layer)
    def _():
        first = layer * TRIO
        attend(
            keys[first : first + TRIO].reshape(CACHE_ROWS, HEAD),
            values[first : first + TRIO].reshape(CACHE_ROWS, HEAD),
        )

    @pl.when(section != layer)
    def _():
        attend(other[:CACHE_ROWS, ALL_PARTS : ALL_PARTS + HEAD], other[:CACHE_ROWS, ALL_PARTS + HEAD :])


def output_kernel(layer, ids, received, w_out, w_other, payload, wide, rows):
    for p in range(N_DP):
        wide[pl.ds(p * USED, USED), :] = received[p, :USED, :].astype(F32)
    for s in range(TRIO):
        for h in range(GROUP):
            rows[s * N_DP : (s + 1) * N_DP, h * HEAD : (h + 1) * HEAD] = wide[
                pl.ds(s * 8 + h, N_DP, stride=USED), :
            ].astype(BF16)

    def write(weight):
        product = dot(rows[...], weight[...]).astype(BF16)
        for t in range(N_TENSOR):
            payload[t] = product

    pl.when(ids[SECTION] == layer)(lambda: write(w_out))
    pl.when(ids[SECTION] != layer)(lambda: write(w_other))


def summed(received, residual):
    total = received[0].astype(F32)
    for t in range(1, N_TENSOR):
        total = total + received[t].astype(F32)
    return (residual[...].astype(F32) + total).astype(BF16)


def second_kernel(ids, received, residual, weights, other, later, payload, result, spread):
    rows = summed(received, residual)
    result[...] = rows
    spread_squares(rows, spread)
    pl.when(ids[SECTION] == 1)(lambda: project(rows, weights, spread))
    pl.when(ids[SECTION] == 0)(lambda: project(rows, other, spread))
    for p in range(N_DP):
        payload[p, :USED, :] = spread[pl.ds(p, USED, stride=N_DP), :].astype(BF16)
        payload[p, USED:, :] = later[p].astype(F32)[:TILE].astype(BF16)


def last_kernel(
    ids, table, received, before, gathered_0, gathered_1, own_0, own_1, result, mine, swapped
):
    rows = summed(received, before)
    result[...] = rows

    @pl.when(ids[SECTION] == 0)
    def _():
        swapped[:HALF_ROWS, :] = rows

    @pl.when(ids[SECTION] == 1)
    def _():
        swapped[:HALF_ROWS, :] = before[...]

    me, section = ids[REPLICA], ids[SECTION]
    row = iota((16, HEAD), 0)
    swapped[HALF_ROWS:, HEAD:] = jnp.zeros((16, WIDTH - HEAD), BF16)
    for layer, (gathered, own) in enumerate(((gathered_0, own_0), (gathered_1, own_1))):
        own_rows = own[...].astype(F32)
        total = jnp.zeros((16, HEAD), F32)
        for r in range(ROWS_DEV):
            source = table[SOURCE + r]
            anchor = over_six(source)
            held = source - anchor * ROWS_DEV
            slot = held - section * TRIO
            here = (slot >= 0) & (slot < TRIO)
            stays = here & (anchor == me)
            moves = here & (anchor != me)
            pair = gathered[anchor, USED - 16 : USED, :].astype(F32)
            kept_key = jnp.sum(jnp.where(row == slot, own_rows, 0.0), axis=0, keepdims=True)
            kept_value = jnp.sum(jnp.where(row == slot + 8, own_rows, 0.0), axis=0, keepdims=True)
            new_key = jnp.where(stays, kept_key, jnp.where(moves, pair[8:9], 0.0))
            new_value = jnp.where(stays, kept_value, jnp.where(moves, pair[9:10], 0.0))
            total = jnp.where(row == r, new_key, jnp.where(row == r + 8, new_value, total))
        total = total.astype(BF16)

        @pl.when(section == layer)
        def _():
            mine[...] = total

        @pl.when(section != layer)
        def _():
            swapped[HALF_ROWS:, :HEAD] = total


def arrive_kernel(
    ids, table, to_slots, first, second, keys, values, second_in, third_in, fourth_in,
    part, key_rows, value_rows, pieces
):
    def write_rows(order, rows):
        part[...] = dot(order, rows[...], ((0,), (0,)))

    pl.when(ids[SECTION] == 0)(lambda: write_rows(to_slots[:HALF_ROWS, :], first))
    pl.when(ids[SECTION] == 1)(lambda: write_rows(to_slots[HALF_ROWS:, :], second))
    for p in range(N_DP):
        for i, (gathered, first_row) in enumerate(
            ((second_in, USED - 16), (third_in, USED - TILE), (fourth_in, USED - 16))
        ):
            pieces[pl.ds(p * TILES + i * TILE, TILE), :] = gathered[
                p, first_row : first_row + 16, :
            ].astype(F32)[TILE:]
    count = jnp.int32(0)
    for r in range(ROWS_DEV):
        source = table[SOURCE + r]
        anchor = over_six(source)
        moves = anchor != ids[REPLICA]

        @pl.when(anchor == ids[REPLICA])
        def _():
            held = source - anchor * ROWS_DEV
            key_rows[r] = keys[held]
            value_rows[r] = values[held]

        @pl.when(moves)
        def _():
            parts = [
                pieces[pl.ds(tile_row(count * PIECES + i), N_DP, stride=TILES), :].astype(BF16)
                for i in range(PIECES)
            ]
            key_rows[r] = jnp.concatenate(parts[:2], 0)
            value_rows[r] = jnp.concatenate(parts[2:], 0)

        count = count + jnp.where(moves, 1, 0)


def final_kernel(
    ids, table, to_slots, part, key_rows, value_rows, received, mine, out, key_out, value_out
):
    def write_rows(order):
        out[...] = (part[...] + dot(order, received[:HALF_ROWS, :], ((0,), (0,)))).astype(BF16)

    pl.when(ids[SECTION] == 0)(lambda: write_rows(to_slots[HALF_ROWS:, :]))
    pl.when(ids[SECTION] == 1)(lambda: write_rows(to_slots[:HALF_ROWS, :]))
    position = iota((CONTEXT, HEAD), 0)
    own = mine[...].astype(F32) + received[HALF_ROWS:, :HEAD].astype(F32)
    for r in range(ROWS_DEV):
        written = position == table[NEW_LEN + r]
        for rows, target, row in ((key_rows, key_out, r), (value_rows, value_out, r + 8)):
            target[r] = jnp.where(written, own[row : row + 1], rows[r].astype(F32)).astype(BF16)


def call(kernel, name, specs, out_shapes, operands, scratch=()):
    spec_of = {"s": SMEM_SPEC, "v": VMEM_SPEC, "a": pl.BlockSpec(memory_space=pl.ANY)}
    return pl.pallas_call(
        kernel,
        out_shape=out_shapes,
        in_specs=[spec_of[letter] for letter in specs],
        out_specs=jax.tree.map(lambda _: VMEM_SPEC, out_shapes),
        scratch_shapes=list(scratch),
        compiler_params=pltpu.CompilerParams(vmem_limit_bytes=8 * 1024 * 1024),
        name=name,
    )(*operands)


def exchange(value, axis):
    return lax.all_to_all(value, axis, split_axis=0, concat_axis=0, tiled=True)


def swap(value):
    return lax.ppermute(value, "section", [(0, 1), (1, 0)])


def shape(*dims):
    return jax.ShapeDtypeStruct(dims, BF16)


def on_device(
    hidden_in,
    norm_gain,
    w_query,
    w_key,
    w_value,
    w_out,
    key_cache,
    value_cache,
    context_len,
    dest_replica,
    dest_slot,
):
    me = lax.axis_index("dp")
    section = lax.axis_index("section")
    ids = jnp.stack([section, me]).astype(jnp.int32)
    keys, values = key_cache[0], value_cache[0]
    new_index = (dest_replica * ROWS_DEV + dest_slot)[None, :]
    row = jnp.arange(ROWS, dtype=jnp.int32)
    entry = jnp.arange(4 * ROWS_DEV, dtype=jnp.int32)[:, None]
    kind = entry // ROWS_DEV
    wanted = me * ROWS_DEV + entry % ROWS_DEV
    found = jnp.where(kind < 2, row[None, :], new_index) == wanted
    chosen = jnp.where(
        kind == 0, dest_replica[None, :], jnp.where(kind == 3, row[None, :], context_len[None, :])
    )
    table = jnp.sum(jnp.where(found, chosen, 0), 1)

    half = HEAD // 2
    inverse_freq = ROPE_BASE ** (-(jnp.arange(half, dtype=F32) * (2.0 / HEAD)))
    held_len = jnp.concatenate([table[HELD_LEN : HELD_LEN + ROWS_DEV], jnp.zeros((2,), jnp.int32)])
    angles = held_len.astype(F32)[:, None] * jnp.concatenate([inverse_freq, inverse_freq])[None, :]
    cosine = jnp.cos(angles)
    sine = jnp.sin(angles) * jnp.where(jnp.arange(HEAD) < half, -1.0, 1.0)[None, :]

    sent_keys, sent_values = (
        jnp.pad(
            lax.dynamic_slice_in_dim(cache, (1 - section) * TRIO, TRIO).reshape(CACHE_ROWS, HEAD),
            ((0, WIDTH - CACHE_ROWS), (left, 3 * HEAD - left)),
        )
        for cache, left in ((keys, 2 * HEAD), (values, 3 * HEAD))
    )
    rest = (
        jnp.pad(w_key[0], ((0, 0), (0, 3 * HEAD)))
        + jnp.pad(w_value[0], ((0, 0), (HEAD, 2 * HEAD)))
        + sent_keys
        + sent_values
    )
    weights = call(
        load_kernel, "load", "vvv", shape(WIDTH + 16, PACKED), (w_query, rest, norm_gain)
    )
    other = swap(weights)
    residual, to_slots, squares, cut = call(
        prepare_kernel,
        "prepare",
        "ssvvvv",
        (
            shape(HALF_ROWS, WIDTH),
            shape(ROWS, ROWS),
            jax.ShapeDtypeStruct((2 * N_DP, HEAD), F32),
            shape(N_DP, MOVES * PIECES, HEAD),
        ),
        (ids, table, new_index, hidden_in, keys, values),
        [pltpu.VMEM((MOVES * PIECES * N_DP, HEAD), F32)],
    )
    payload = call(
        first_kernel,
        "first",
        "svvvvv",
        shape(N_DP, BLOCK, HEAD),
        (ids, residual, squares, cut, weights, other),
        [pltpu.VMEM((USED * N_DP, HEAD), F32)],
    )
    first = exchange(payload, "dp")

    late_out, late_replica, late_slot, _ = lax.optimization_barrier(
        (w_out[0], dest_replica, dest_slot, payload)
    )
    out_other = swap(late_out)
    leaves = late_replica != row // ROWS_DEV
    before = (row[None, :] // ROWS_DEV == row[:, None] // ROWS_DEV) & (row[None, :] < row[:, None])
    rank = jnp.sum(jnp.where(before & leaves[None, :], 1, 0), 1)
    before = (late_replica[None, :] == late_replica[:, None]) & (
        late_slot[None, :] < late_slot[:, None]
    )
    place = jnp.sum(jnp.where(before & leaves[None, :], 1, 0), 1)
    arrival = jnp.where(leaves, place * N_DP + late_replica, -1)
    chosen = arrival[None, :] == jnp.arange(N_DP * MOVES, dtype=jnp.int32)[:, None]
    route = jnp.sum(jnp.where(chosen, (row // ROWS_DEV * MOVES + rank)[None, :], 0), 1)[None, :]

    def attend(layer, received, specs="", *more):
        return call(
            lambda *refs: attend_kernel(layer, *refs),
            "attend",
            "ssvvvvvv" + specs,
            (shape(N_DP, USED, HEAD), shape(16, HEAD))
            + (() if layer else (shape(N_DP, 2 * TILE, HEAD),)),
            (ids, table, cosine, sine, received, keys, values, other, *more),
            [pltpu.VMEM((N_DP * TILE, HEAD), F32)]
            if layer
            else [
                pltpu.VMEM((N_DP * MOVES * PIECES, HEAD), F32),
                pltpu.VMEM((N_DP * TILES, HEAD), F32),
            ],
        )

    def output(layer, received):
        return call(
            lambda *refs: output_kernel(layer, *refs),
            "output",
            "svvv",
            shape(N_TENSOR, HALF_ROWS, WIDTH),
            (ids, received, w_out[0], out_other),
            [pltpu.VMEM((N_DP * USED, HEAD), F32), pltpu.VMEM((HALF_ROWS, GROUP * HEAD), BF16)],
        )

    payload, own_0, later = attend(0, first, "va", route, out_other)
    second = exchange(payload, "dp")
    sums = exchange(output(0, second), "tensor")
    payload, result_0 = call(
        second_kernel,
        "second",
        "svvvvv",
        (shape(N_DP, USED + TILE, HEAD), shape(HALF_ROWS, WIDTH)),
        (ids, sums, residual, weights, other, later),
        [pltpu.VMEM((USED * N_DP, HEAD), F32)],
    )
    third = exchange(payload, "dp")
    payload, own_1 = attend(1, third, "v", later)
    fourth = exchange(payload, "dp")
    sums = exchange(output(1, fourth), "tensor")
    result_1, mine, swapped = call(
        last_kernel,
        "last",
        "ssvvvvvv",
        (shape(HALF_ROWS, WIDTH), shape(16, HEAD), shape(HALF_ROWS + 16, WIDTH)),
        (ids, table, sums, result_0, second, fourth, own_0, own_1),
    )
    cache_shape = shape(ROWS_DEV, CONTEXT, HEAD)
    received = swap(swapped)
    part, key_rows, value_rows = call(
        arrive_kernel,
        "arrive",
        "ssvvvvvvvv",
        (jax.ShapeDtypeStruct((ROWS, WIDTH), F32), cache_shape, cache_shape),
        (ids, table, to_slots, result_0, result_1, keys, values, second, third, fourth),
        [pltpu.VMEM(((N_DP + 1) * TILES, HEAD), F32)],
    )
    layer_out, key_out, value_out = call(
        final_kernel,
        "final",
        "ssvvvvvv",
        (shape(ROWS, WIDTH), cache_shape, cache_shape),
        (ids, table, to_slots, part, key_rows, value_rows, received, mine),
    )
    return layer_out[None], key_out[None], value_out[None]


def solution(mesh):
    return jax.shard_map(
        on_device,
        mesh=mesh,
        in_specs=(
            P(None, "dp"),
            P("section", "dp"),
            P("section", "dp", "tensor"),
            P("section", "dp", "tensor"),
            P("section", "dp", "tensor"),
            P("section", "tensor", "dp"),
            P("section", "dp", None, "tensor"),
            P("section", "dp", None, "tensor"),
            P(),
            P(),
            P(),
        ),
        out_specs=(
            P("section", None, "dp"),
            P("section", "dp", None, "tensor"),
            P("section", "dp", None, "tensor"),
        ),
        check_vma=False,
    )
```

```python
import jax
import jax.numpy as jnp
from jax import lax
from jax.experimental import pallas as pl
from jax.experimental.pallas import tpu as pltpu
from jax.sharding import PartitionSpec as P

N_DP = 32
N_TENSOR = 8
ROWS_DEV = 6
ROWS = 192
TRIO = 3
HALF_ROWS = N_DP * TRIO
CONTEXT = 64
MOVES = 4
PIECES = 4
HEAD = 128
GROUP = 8
PARTS = GROUP + 2
USED = 32
BLOCK = USED + MOVES * PIECES
TILE = 8
TILES = 3 * TILE
WIDTH = 256
MODEL = 8192
CACHE_ROWS = TRIO * CONTEXT
QUERY = GROUP * HEAD
ALL_PARTS = PARTS * HEAD
PACKED = ALL_PARTS + 2 * HEAD
EPSILON = 1e-06
ROPE_BASE = 1000000.0
F32 = jnp.float32
BF16 = jnp.bfloat16

SECTION, REPLICA = 0, 1
DEST, HELD_LEN, NEW_LEN, SOURCE = 0, 6, 12, 18

SMEM_SPEC = pl.BlockSpec(memory_space=pltpu.SMEM)
VMEM_SPEC = pl.BlockSpec(memory_space=pltpu.VMEM)


def iota(shape, dim):
    return lax.broadcasted_iota(jnp.int32, shape, dim)


def pick(condition):
    return jnp.where(condition, 1.0, 0.0).astype(BF16)


def over_six(index):
    return (index * 171) >> 10


def over_ten(index):
    return (index * 205) >> 11


def dot(left, right, contract=((1,), (0,))):
    return lax.dot_general(left, right, (contract, ((), ())), preferred_element_type=F32)


def to_new_order(new_index):
    return pick(iota((ROWS, ROWS), 0) == new_index)


def project(rows, weights, spread):
    by_slot = rows.astype(F32)
    terms = weights[WIDTH:, QUERY:ALL_PARTS].astype(F32)
    gain = terms[0:1] + terms[1:2] + terms[2:3]
    scaled = (by_slot * gain).astype(BF16)
    for pair in range(PARTS // 2):
        product = dot(scaled, weights[:WIDTH, pair * 2 * HEAD : (pair + 1) * 2 * HEAD])
        for s in range(TRIO):
            for side in range(2):
                row = s * PARTS + 2 * pair + side
                spread[pl.ds(row * N_DP, N_DP), :] = product[
                    s * N_DP : (s + 1) * N_DP, side * HEAD : (side + 1) * HEAD
                ]


def spread_squares(rows, spread, row=TRIO * PARTS):
    by_slot = rows.astype(F32)
    square = jnp.sum(by_slot * by_slot, axis=1, keepdims=True)
    lane = iota((N_DP, HEAD), 1)
    squares = jnp.zeros((N_DP, HEAD), F32)
    for s in range(TRIO):
        squares = jnp.where(lane == s, square[s * N_DP : (s + 1) * N_DP], squares)
    high = squares.astype(BF16).astype(F32)
    spread[pl.ds(row * N_DP, N_DP), :] = high
    spread[pl.ds((row + 1) * N_DP, N_DP), :] = squares - high


def load_kernel(query, rest, gain, weights):
    weights[:WIDTH, :QUERY] = query[0]
    weights[WIDTH:, :QUERY] = jnp.zeros((16, QUERY), BF16)
    weights[:WIDTH, QUERY:] = rest[...]
    high = gain[...].astype(BF16).astype(F32)
    middle = (gain[...] - high).astype(BF16).astype(F32)
    low = gain[...] - high - middle
    row = iota((16, WIDTH), 0)
    terms = jnp.where(row == 0, high, jnp.where(row == 1, middle, jnp.where(row == 2, low, 0.0)))
    weights[WIDTH:, QUERY:ALL_PARTS] = terms.astype(BF16)
    weights[WIDTH:, ALL_PARTS:] = jnp.zeros((16, 2 * HEAD), BF16)


def prepare_kernel(
    ids, new_index, hidden, residual, to_slots_out, squares
):
    row, column = iota((ROWS, ROWS), 0), iota((ROWS, ROWS), 1)
    by_slot_order = pick(column == (row & (N_DP - 1)) * ROWS_DEV + (row >> 5))
    to_slots = dot(by_slot_order, to_new_order(new_index[...]), ((1,), (1,))).astype(BF16)
    to_slots_out[...] = to_slots
    by_slot = dot(to_slots, hidden[...]).astype(BF16)

    @pl.when(ids[SECTION] == 0)
    def _():
        residual[...] = by_slot[:HALF_ROWS]
        spread_squares(by_slot[:HALF_ROWS], squares, 0)

    @pl.when(ids[SECTION] == 1)
    def _():
        residual[...] = by_slot[HALF_ROWS:]
        spread_squares(by_slot[HALF_ROWS:], squares, 0)


def cut_kernel(ids, table, keys, values, after, cut, spread):
    count = jnp.int32(0)
    for s in range(ROWS_DEV):
        leaves = table[DEST + s] != ids[REPLICA]

        @pl.when(leaves)
        def _():
            base = pl.multiple_of(count * (PIECES * N_DP), N_DP)
            spread[pl.ds(base, CONTEXT), :] = keys[s].astype(F32)
            spread[pl.ds(base + CONTEXT, CONTEXT), :] = values[s].astype(F32)

        count = count + jnp.where(leaves, 1, 0)
    for p in range(N_DP):
        cut[p] = spread[pl.ds(p, MOVES * PIECES, stride=N_DP), :].astype(BF16)


def first_kernel(ids, rows, squares, cut, weights, other, payload, spread):
    spread[pl.ds(TRIO * PARTS * N_DP, 2 * N_DP), :] = squares[...]
    pl.when(ids[SECTION] == 0)(lambda: project(rows[...], weights, spread))
    pl.when(ids[SECTION] == 1)(lambda: project(rows[...], other, spread))
    for p in range(N_DP):
        payload[p, :USED, :] = spread[pl.ds(p, USED, stride=N_DP), :].astype(BF16)
        payload[p, USED:, :] = cut[p]


def tile_row(piece):
    return piece + jnp.where(piece < 14, 2, 4)


def forward(route, received, pieces, tiles):
    count = N_DP * MOVES
    for p in range(N_DP):
        pieces[pl.ds(p * MOVES * PIECES, MOVES * PIECES), :] = received[p, USED:, :].astype(F32)
        tiles[pl.ds(p * TILES, TILE), :] = jnp.zeros((TILE, HEAD), F32)
        tiles[pl.ds(p * TILES + 2 * TILE, TILE), :] = jnp.zeros((TILE, HEAD), F32)
    to_replica = pick(iota((count, count), 0) == route[...])
    for i in range(PIECES):
        part = pieces[pl.ds(i, count, stride=PIECES), :].astype(BF16)
        sorted_part = dot(to_replica, part, ((0,), (0,)))
        for m in range(MOVES):
            piece = m * PIECES + i
            row = piece + (2 if piece < 14 else 4)
            tiles[pl.ds(row, N_DP, stride=TILES), :] = sorted_part[m * N_DP : (m + 1) * N_DP]


def attend_kernel(
    layer, ids, table, cosine, sine, received, keys, values, other, *refs
):
    if layer == 0:
        route, _, payload, own, later, pieces, tiles = refs
        forward(route, received, pieces, tiles)
        for p in range(N_DP):
            later[p] = tiles[pl.ds(p * TILES + TILE, 2 * TILE), :].astype(BF16)
    else:
        later, payload, own, tiles = refs
        for p in range(N_DP):
            tiles[pl.ds(p * TILE, TILE), :] = later[p].astype(F32)[TILE:]
    section = ids[SECTION]

    def attend(all_keys, all_values):
        total = received[0, :USED, :].astype(F32)
        for p in range(1, N_DP):
            total = total + received[p, :USED, :].astype(F32)
        row = iota((USED, HEAD), 0)
        lane = iota((USED, HEAD), 1)
        slot = over_ten(row)
        part = row - slot * PARTS
        tail = TRIO * PARTS
        squares = total[tail : tail + 1] + total[tail + 1 : tail + 2]
        square = jnp.sum(jnp.where(lane == slot, squares, 0.0), axis=1, keepdims=True)
        projected = total * lax.rsqrt(square / MODEL + EPSILON)
        cos_rows = jnp.ones((USED, HEAD), F32)
        sin_rows = jnp.zeros((USED, HEAD), F32)
        for s in range(TRIO):
            turned = (slot == s) & (part <= GROUP)
            cos_rows = jnp.where(turned, cosine[pl.ds(section * TRIO + s, 1), :], cos_rows)
            sin_rows = jnp.where(turned, sine[pl.ds(section * TRIO + s, 1), :], sin_rows)
        vectors = (
            projected * cos_rows + pltpu.roll(projected, HEAD // 2, 1) * sin_rows
        ).astype(BF16)

        scale = HEAD ** (-0.5)
        scores = dot(vectors, all_keys, ((1,), (1,))) * scale
        among = dot(vectors, vectors, ((1,), (1,))) * scale
        wide = (USED, CACHE_ROWS)
        wide_slot = over_ten(iota(wide, 0))
        column = iota(wide, 1)
        live = column < 0
        for s in range(TRIO):
            live = live | (
                (wide_slot == s)
                & (column >= s * CONTEXT)
                & (column < s * CONTEXT + table[HELD_LEN + section * TRIO + s])
            )
        scores = jnp.where(live, scores, -1e30)
        small_slot = over_ten(iota((USED, USED), 0))
        small_column = iota((USED, USED), 1)
        own_score = jnp.sum(
            jnp.where(small_column == small_slot * PARTS + GROUP, among, 0.0), axis=1, keepdims=True
        )
        highest = jnp.maximum(jnp.max(scores, axis=1, keepdims=True), own_score)
        terms = jnp.exp(scores - highest)
        own_term = jnp.exp(own_score - highest)
        denominator = jnp.sum(terms, axis=1, keepdims=True) + own_term
        weights = (terms / denominator).astype(BF16)
        own_weights = jnp.where(
            small_column == small_slot * PARTS + GROUP + 1, own_term / denominator, 0.0
        ).astype(BF16)
        attended = (dot(weights, all_values) + dot(own_weights, vectors)).astype(BF16)

        out_row, in_row = iota((USED, USED), 0), iota((USED, USED), 1)
        out_slot = out_row >> 3
        order = pick((in_row == out_slot * PARTS + (out_row & 7)) & (out_slot < TRIO))
        block = dot(order, attended)
        own_row, own_in = iota((16, USED), 0), iota((16, USED), 1)
        own_slot = own_row & 7
        own_pick = pick(
            (own_in == own_slot * PARTS + GROUP + (own_row >> 3)) & (own_slot < TRIO)
        )
        own_pair = dot(own_pick, vectors)
        own[...] = own_pair.astype(BF16)
        stride = TILES if layer == 0 else TILE
        for s in range(TRIO):
            first = table[DEST + section * TRIO + s] * stride
            tiles[pl.ds(first, 1), :] = own_pair[s : s + 1]
            tiles[pl.ds(first + 1, 1), :] = own_pair[8 + s : 9 + s]
        low, high = block[:16].astype(BF16), block[16 : 16 + TILE]
        for p in range(N_DP):
            payload[p, :16, :] = low
            payload[p, 16:, :] = jnp.concatenate(
                [high, tiles[pl.ds(p * stride, TILE), :]], 0
            ).astype(BF16)

    @pl.when(section == layer)
    def _():
        first = layer * TRIO
        attend(
            keys[first : first + TRIO].reshape(CACHE_ROWS, HEAD),
            values[first : first + TRIO].reshape(CACHE_ROWS, HEAD),
        )

    @pl.when(section != layer)
    def _():
        attend(other[:CACHE_ROWS, ALL_PARTS : ALL_PARTS + HEAD], other[:CACHE_ROWS, ALL_PARTS + HEAD :])


def output_kernel(layer, ids, received, w_out, w_other, payload, wide, rows):
    for p in range(N_DP):
        wide[pl.ds(p * USED, USED), :] = received[p, :USED, :].astype(F32)
    for s in range(TRIO):
        for h in range(GROUP):
            rows[s * N_DP : (s + 1) * N_DP, h * HEAD : (h + 1) * HEAD] = wide[
                pl.ds(s * 8 + h, N_DP, stride=USED), :
            ].astype(BF16)

    def write(weight):
        product = dot(rows[...], weight[...]).astype(BF16)
        for t in range(N_TENSOR):
            payload[t] = product

    pl.when(ids[SECTION] == layer)(lambda: write(w_out))
    pl.when(ids[SECTION] != layer)(lambda: write(w_other))


def summed(received, residual):
    total = received[0].astype(F32)
    for t in range(1, N_TENSOR):
        total = total + received[t].astype(F32)
    return (residual[...].astype(F32) + total).astype(BF16)


def second_kernel(ids, received, residual, weights, other, later, payload, result, spread):
    rows = summed(received, residual)
    result[...] = rows
    spread_squares(rows, spread)
    pl.when(ids[SECTION] == 1)(lambda: project(rows, weights, spread))
    pl.when(ids[SECTION] == 0)(lambda: project(rows, other, spread))
    for p in range(N_DP):
        payload[p, :USED, :] = spread[pl.ds(p, USED, stride=N_DP), :].astype(BF16)
        payload[p, USED:, :] = later[p].astype(F32)[:TILE].astype(BF16)


def last_kernel(
    ids, table, received, before, gathered_0, gathered_1, own_0, own_1, result, mine, swapped
):
    rows = summed(received, before)
    result[...] = rows

    @pl.when(ids[SECTION] == 0)
    def _():
        swapped[:HALF_ROWS, :] = rows

    @pl.when(ids[SECTION] == 1)
    def _():
        swapped[:HALF_ROWS, :] = before[...]

    me, section = ids[REPLICA], ids[SECTION]
    row = iota((16, HEAD), 0)
    swapped[HALF_ROWS:, HEAD:] = jnp.zeros((16, WIDTH - HEAD), BF16)
    for layer, (gathered, own) in enumerate(((gathered_0, own_0), (gathered_1, own_1))):
        own_rows = own[...].astype(F32)
        total = jnp.zeros((16, HEAD), F32)
        for r in range(ROWS_DEV):
            source = table[SOURCE + r]
            anchor = over_six(source)
            held = source - anchor * ROWS_DEV
            slot = held - section * TRIO
            here = (slot >= 0) & (slot < TRIO)
            stays = here & (anchor == me)
            moves = here & (anchor != me)
            pair = gathered[anchor, USED - 16 : USED, :].astype(F32)
            kept_key = jnp.sum(jnp.where(row == slot, own_rows, 0.0), axis=0, keepdims=True)
            kept_value = jnp.sum(jnp.where(row == slot + 8, own_rows, 0.0), axis=0, keepdims=True)
            new_key = jnp.where(stays, kept_key, jnp.where(moves, pair[8:9], 0.0))
            new_value = jnp.where(stays, kept_value, jnp.where(moves, pair[9:10], 0.0))
            total = jnp.where(row == r, new_key, jnp.where(row == r + 8, new_value, total))
        total = total.astype(BF16)

        @pl.when(section == layer)
        def _():
            mine[...] = total

        @pl.when(section != layer)
        def _():
            swapped[HALF_ROWS:, :HEAD] = total


def arrive_kernel(
    ids, table, to_slots, first, second, keys, values, second_in, third_in, fourth_in,
    part, key_rows, value_rows, pieces
):
    def write_rows(order, rows):
        part[...] = dot(order, rows[...], ((0,), (0,)))

    pl.when(ids[SECTION] == 0)(lambda: write_rows(to_slots[:HALF_ROWS, :], first))
    pl.when(ids[SECTION] == 1)(lambda: write_rows(to_slots[HALF_ROWS:, :], second))
    for p in range(N_DP):
        for i, (gathered, first_row) in enumerate(
            ((second_in, USED - 16), (third_in, USED - TILE), (fourth_in, USED - 16))
        ):
            pieces[pl.ds(p * TILES + i * TILE, TILE), :] = gathered[
                p, first_row : first_row + 16, :
            ].astype(F32)[TILE:]
    count = jnp.int32(0)
    for r in range(ROWS_DEV):
        source = table[SOURCE + r]
        anchor = over_six(source)
        moves = anchor != ids[REPLICA]

        @pl.when(anchor == ids[REPLICA])
        def _():
            held = source - anchor * ROWS_DEV
            key_rows[r] = keys[held]
            value_rows[r] = values[held]

        @pl.when(moves)
        def _():
            parts = [
                pieces[pl.ds(tile_row(count * PIECES + i), N_DP, stride=TILES), :].astype(BF16)
                for i in range(PIECES)
            ]
            key_rows[r] = jnp.concatenate(parts[:2], 0)
            value_rows[r] = jnp.concatenate(parts[2:], 0)

        count = count + jnp.where(moves, 1, 0)


def final_kernel(
    ids, table, to_slots, part, key_rows, value_rows, received, mine, out, key_out, value_out
):
    def write_rows(order):
        out[...] = (part[...] + dot(order, received[:HALF_ROWS, :], ((0,), (0,)))).astype(BF16)

    pl.when(ids[SECTION] == 0)(lambda: write_rows(to_slots[HALF_ROWS:, :]))
    pl.when(ids[SECTION] == 1)(lambda: write_rows(to_slots[:HALF_ROWS, :]))
    position = iota((CONTEXT, HEAD), 0)
    own = mine[...].astype(F32) + received[HALF_ROWS:, :HEAD].astype(F32)
    for r in range(ROWS_DEV):
        written = position == table[NEW_LEN + r]
        for rows, target, row in ((key_rows, key_out, r), (value_rows, value_out, r + 8)):
            target[r] = jnp.where(written, own[row : row + 1], rows[r].astype(F32)).astype(BF16)


def call(kernel, name, specs, out_shapes, operands, scratch=()):
    spec_of = {"s": SMEM_SPEC, "v": VMEM_SPEC, "a": pl.BlockSpec(memory_space=pl.ANY)}
    return pl.pallas_call(
        kernel,
        out_shape=out_shapes,
        in_specs=[spec_of[letter] for letter in specs],
        out_specs=jax.tree.map(lambda _: VMEM_SPEC, out_shapes),
        scratch_shapes=list(scratch),
        compiler_params=pltpu.CompilerParams(vmem_limit_bytes=8 * 1024 * 1024),
        name=name,
    )(*operands)


def exchange(value, axis):
    return lax.all_to_all(value, axis, split_axis=0, concat_axis=0, tiled=True)


def swap(value):
    return lax.ppermute(value, "section", [(0, 1), (1, 0)])


def shape(*dims):
    return jax.ShapeDtypeStruct(dims, BF16)


def on_device(
    hidden_in,
    norm_gain,
    w_query,
    w_key,
    w_value,
    w_out,
    key_cache,
    value_cache,
    context_len,
    dest_replica,
    dest_slot,
):
    me = lax.axis_index("dp")
    section = lax.axis_index("section")
    ids = jnp.stack([section, me]).astype(jnp.int32)
    keys, values = key_cache[0], value_cache[0]
    new_index = (dest_replica * ROWS_DEV + dest_slot)[None, :]
    row = jnp.arange(ROWS, dtype=jnp.int32)
    entry = jnp.arange(4 * ROWS_DEV, dtype=jnp.int32)[:, None]
    kind = entry // ROWS_DEV
    wanted = me * ROWS_DEV + entry % ROWS_DEV
    found = jnp.where(kind < 2, row[None, :], new_index) == wanted
    chosen = jnp.where(
        kind == 0, dest_replica[None, :], jnp.where(kind == 3, row[None, :], context_len[None, :])
    )
    table = jnp.sum(jnp.where(found, chosen, 0), 1)

    half = HEAD // 2
    inverse_freq = ROPE_BASE ** (-(jnp.arange(half, dtype=F32) * (2.0 / HEAD)))
    held_len = jnp.concatenate([table[HELD_LEN : HELD_LEN + ROWS_DEV], jnp.zeros((2,), jnp.int32)])
    angles = held_len.astype(F32)[:, None] * jnp.concatenate([inverse_freq, inverse_freq])[None, :]
    cosine = jnp.cos(angles)
    sine = jnp.sin(angles) * jnp.where(jnp.arange(HEAD) < half, -1.0, 1.0)[None, :]

    sent_keys, sent_values = (
        jnp.pad(
            lax.dynamic_slice_in_dim(cache, (1 - section) * TRIO, TRIO).reshape(CACHE_ROWS, HEAD),
            ((0, WIDTH - CACHE_ROWS), (left, 3 * HEAD - left)),
        )
        for cache, left in ((keys, 2 * HEAD), (values, 3 * HEAD))
    )
    rest = (
        jnp.pad(w_key[0], ((0, 0), (0, 3 * HEAD)))
        + jnp.pad(w_value[0], ((0, 0), (HEAD, 2 * HEAD)))
        + sent_keys
        + sent_values
    )
    weights = call(
        load_kernel, "load", "vvv", shape(WIDTH + 16, PACKED), (w_query, rest, norm_gain)
    )
    other = swap(weights)
    residual, to_slots, squares = call(
        prepare_kernel,
        "prepare",
        "svv",
        (shape(HALF_ROWS, WIDTH), shape(ROWS, ROWS), jax.ShapeDtypeStruct((2 * N_DP, HEAD), F32)),
        (ids, new_index, hidden_in),
    )
    cut = call(
        cut_kernel,
        "cut",
        "ssvva",
        shape(N_DP, MOVES * PIECES, HEAD),
        (ids, table, keys, values, squares),
        [pltpu.VMEM((MOVES * PIECES * N_DP, HEAD), F32)],
    )
    payload = call(
        first_kernel,
        "first",
        "svvvvv",
        shape(N_DP, BLOCK, HEAD),
        (ids, residual, squares, cut, weights, other),
        [pltpu.VMEM((USED * N_DP, HEAD), F32)],
    )
    first = exchange(payload, "dp")

    late_out, late_replica, late_slot, _ = lax.optimization_barrier(
        (w_out[0], dest_replica, dest_slot, payload)
    )
    out_other = swap(late_out)
    leaves = late_replica != row // ROWS_DEV
    before = (row[None, :] // ROWS_DEV == row[:, None] // ROWS_DEV) & (row[None, :] < row[:, None])
    rank = jnp.sum(jnp.where(before & leaves[None, :], 1, 0), 1)
    before = (late_replica[None, :] == late_replica[:, None]) & (
        late_slot[None, :] < late_slot[:, None]
    )
    place = jnp.sum(jnp.where(before & leaves[None, :], 1, 0), 1)
    arrival = jnp.where(leaves, place * N_DP + late_replica, -1)
    chosen = arrival[None, :] == jnp.arange(N_DP * MOVES, dtype=jnp.int32)[:, None]
    route = jnp.sum(jnp.where(chosen, (row // ROWS_DEV * MOVES + rank)[None, :], 0), 1)[None, :]

    def attend(layer, received, specs="", *more):
        return call(
            lambda *refs: attend_kernel(layer, *refs),
            "attend",
            "ssvvvvvv" + specs,
            (shape(N_DP, USED, HEAD), shape(16, HEAD))
            + (() if layer else (shape(N_DP, 2 * TILE, HEAD),)),
            (ids, table, cosine, sine, received, keys, values, other, *more),
            [pltpu.VMEM((N_DP * TILE, HEAD), F32)]
            if layer
            else [
                pltpu.VMEM((N_DP * MOVES * PIECES, HEAD), F32),
                pltpu.VMEM((N_DP * TILES, HEAD), F32),
            ],
        )

    def output(layer, received):
        return call(
            lambda *refs: output_kernel(layer, *refs),
            "output",
            "svvv",
            shape(N_TENSOR, HALF_ROWS, WIDTH),
            (ids, received, w_out[0], out_other),
            [pltpu.VMEM((N_DP * USED, HEAD), F32), pltpu.VMEM((HALF_ROWS, GROUP * HEAD), BF16)],
        )

    payload, own_0, later = attend(0, first, "va", route, out_other)
    second = exchange(payload, "dp")
    sums = exchange(output(0, second), "tensor")
    payload, result_0 = call(
        second_kernel,
        "second",
        "svvvvv",
        (shape(N_DP, USED + TILE, HEAD), shape(HALF_ROWS, WIDTH)),
        (ids, sums, residual, weights, other, later),
        [pltpu.VMEM((USED * N_DP, HEAD), F32)],
    )
    third = exchange(payload, "dp")
    payload, own_1 = attend(1, third, "v", later)
    fourth = exchange(payload, "dp")
    sums = exchange(output(1, fourth), "tensor")
    result_1, mine, swapped = call(
        last_kernel,
        "last",
        "ssvvvvvv",
        (shape(HALF_ROWS, WIDTH), shape(16, HEAD), shape(HALF_ROWS + 16, WIDTH)),
        (ids, table, sums, result_0, second, fourth, own_0, own_1),
    )
    cache_shape = shape(ROWS_DEV, CONTEXT, HEAD)
    received = swap(swapped)
    part, key_rows, value_rows = call(
        arrive_kernel,
        "arrive",
        "ssvvvvvvvv",
        (jax.ShapeDtypeStruct((ROWS, WIDTH), F32), cache_shape, cache_shape),
        (ids, table, to_slots, result_0, result_1, keys, values, second, third, fourth),
        [pltpu.VMEM(((N_DP + 1) * TILES, HEAD), F32)],
    )
    layer_out, key_out, value_out = call(
        final_kernel,
        "final",
        "ssvvvvvv",
        (shape(ROWS, WIDTH), cache_shape, cache_shape),
        (ids, table, to_slots, part, key_rows, value_rows, received, mine),
    )
    return layer_out[None], key_out[None], value_out[None]


def solution(mesh):
    return jax.shard_map(
        on_device,
        mesh=mesh,
        in_specs=(
            P(None, "dp"),
            P("section", "dp"),
            P("section", "dp", "tensor"),
            P("section", "dp", "tensor"),
            P("section", "dp", "tensor"),
            P("section", "tensor", "dp"),
            P("section", "dp", None, "tensor"),
            P("section", "dp", None, "tensor"),
            P(),
            P(),
            P(),
        ),
        out_specs=(
            P("section", None, "dp"),
            P("section", "dp", None, "tensor"),
            P("section", "dp", None, "tensor"),
        ),
        check_vma=False,
    )
```
